32 devices in a mesh: rows: 4 (over z), cols: 8 (over y, x, core).
Axes of the slice: x: 2, y: 2, z: 4, core: 2. Of those that a mesh axis runs over, the one named last changes fastest.
Arguments:
- fields: float32 [5, 64, 256, 512], P(None, None, 'cols', 'rows'), may hold values from -6 to 6
- cotangent: float32 [5, 64, 256, 512], P(None, None, 'cols', 'rows'), may hold values from -6 to 6
- ocean_mask: int32 [256, 512], P('cols', 'rows'), may hold values from 0 to 1
- depth_levels: int32 [256, 512], P('cols', 'rows'), may hold values from 16 to 64
- in_weight: bfloat16 [256, 256], replicated, may hold values from -0.375 to 0.375
- in_bias: float32 [256], replicated, may hold values from -3 to 3
- out_weight: bfloat16 [256, 63], replicated, may hold values from -0.375 to 0.375
Outputs:
- new_fields: float32 [5, 64, 256, 512], P(None, None, 'cols', 'rows')
- pressure: float32 [64, 256, 512], P(None, 'cols', 'rows')
- grad_in_weight: float32 [256, 256], replicated
- grad_in_bias: float32 [256], replicated
- grad_out_weight: float32 [256, 63], replicated
The draws below stay inside these ranges and needn't reach their ends.
All inputs are finite; a program needn't handle non-finite values.
Results may differ from the reference program's by a relative error of at most 0.0059.
Values sent between devices are 32-bit elements; how exact they have to be, the bound alone decides.
No kernel may reach another device: no remote copies, remote signals or barrier semaphores. Data moves between devices by JAX's collectives and lax.ppermute only.
A program may use at most 192 MiB of HBM per device.

```python
import math
import jax
import jax.numpy as jnp
from jax import lax

NZ = 64
HID = 256
NX = 512
NY = 256


def draw_ocean_mask(key, part):
    walk_key, island_key = jax.random.split(jax.random.fold_in(key, 11))
    steps_taken = jax.random.randint(walk_key, (NY,), -3, 4)
    coast = jnp.clip(NX // 2 + jnp.cumsum(steps_taken), NX // 8, NX)
    east_ids = jnp.arange(NX)
    shore = east_ids[None, :] < coast[:, None]
    islands = jax.random.randint(island_key, (NY, NX), 0, 8) > 0
    return (shore & islands).astype(jnp.int32)


def draw_cotangent(key, part):
    field_key = jax.random.fold_in(key, 23)
    values = jnp.clip(jax.random.normal(field_key, (5, NZ, NY, NX), jnp.float32), -6.0, 6.0)
    factors = jnp.array([1.0, 1.0, 1.0, 0.01, 0.01], jnp.float32)[:, None, None, None]
    return (values * factors).astype(jnp.float32)


def touch_ends(result, key, least, high):
    place = [jax.random.randint(jax.random.fold_in(key, axis), (), 0, length) for axis, length in enumerate(result.shape)]
    widest = result.shape.index(max(result.shape))
    neighbour = place[:widest] + [(place[widest] + 1) % result.shape[widest]] + place[widest + 1:]
    return result.at[tuple(place)].set(least).at[tuple(neighbour)].set(high)


def level_of(rng, extent, pieces, smallest, top_value):
    def one(axis_at, shards_of):
        heights = jax.random.uniform(jax.random.fold_in(jax.random.fold_in(rng, 6), axis_at), (shards_of,), jnp.float32, smallest / len(pieces), top_value / len(pieces))
        return jnp.repeat(jnp.exp(heights), extent[axis_at] // shards_of).reshape((-1,) + (1,) * (len(extent) - axis_at - 1))

    factor_of = one(*pieces[0])
    for cut in pieces[1:]:
        factor_of = factor_of * one(*cut)
    return factor_of


def centred(own_key, shape, scale, bound, shards=(), kind=jnp.bfloat16):
    factor_of = level_of(own_key, shape, shards, -0.22, 0.18) if shards else 1.0
    values = jax.random.normal(own_key, shape, jnp.float32) * scale * factor_of
    return jnp.minimum(jnp.maximum(values, -bound), bound).astype(kind)


def setup_inputs(seed: int = 0) -> dict:
    key_of = jax.random.split(jax.random.key(seed), 8)
    return {
        "fields": centred(key_of[0], (5, NZ, NY, NX), 1.0, 6.0, ((2, 8), (3, 4)), jnp.float32),
        "cotangent": draw_cotangent(jax.random.fold_in(key_of[7], 71), 0),
        "ocean_mask": draw_ocean_mask(jax.random.fold_in(key_of[7], 71), 0),
        "depth_levels": touch_ends(jax.random.randint(key_of[3], (NY, NX), NZ // 4, NZ + 1), jax.random.fold_in(key_of[3], 1), NZ // 4, NZ).astype(jnp.int32),
        "in_weight": centred(key_of[4], (4 * NZ, HID), (4 * NZ) ** -0.5, 0.375),
        "in_bias": centred(key_of[5], (HID,), 0.5, 3.0, (), jnp.float32),
        "out_weight": centred(key_of[6], (HID, NZ - 1), HID ** -0.5, 0.375),
    }


TIME_STEP = 0.2
RATE_MAX = 2.0
THERMAL = 0.5
HALINE = 0.5
SPECTRAL_SHIFT = 0.001
WENO_EPS = 1e-06

def weno_face(first, second, third, fourth, fifth):
    cand_low = (2.0 * first - 7.0 * second + 11.0 * third) / 6.0
    cand_mid = (-second + 5.0 * third + 2.0 * fourth) / 6.0
    cand_high = (2.0 * third + 5.0 * fourth - fifth) / 6.0
    rough_low = 13.0 / 12.0 * jnp.square(first - 2.0 * second + third) + 0.25 * jnp.square(first - 4.0 * second + 3.0 * third)
    rough_mid = 13.0 / 12.0 * jnp.square(second - 2.0 * third + fourth) + 0.25 * jnp.square(second - fourth)
    rough_high = 13.0 / 12.0 * jnp.square(third - 2.0 * fourth + fifth) + 0.25 * jnp.square(3.0 * third - 4.0 * fourth + fifth)
    weight_low = 0.1 / jnp.square(WENO_EPS + rough_low)
    weight_mid = 0.6 / jnp.square(WENO_EPS + rough_mid)
    weight_high = 0.3 / jnp.square(WENO_EPS + rough_high)
    return (weight_low * cand_low + weight_mid * cand_mid + weight_high * cand_high) / (weight_low + weight_mid + weight_high)

def take_cells(array, start, length, along):
    return lax.slice_in_dim(array, start, start + length, axis=along)

def flux_tendency(tracer, velocity, wet_cells, along, length):
    shifted = [take_cells(tracer, offset, length + 1, along) for offset in range(6)]
    left_value = weno_face(shifted[0], shifted[1], shifted[2], shifted[3], shifted[4])
    right_value = weno_face(shifted[5], shifted[4], shifted[3], shifted[2], shifted[1])
    face_speed = 0.5 * (take_cells(velocity, 2, length + 1, along) + take_cells(velocity, 3, length + 1, along))
    face_speed = face_speed * take_cells(wet_cells, 2, length + 1, along) * take_cells(wet_cells, 3, length + 1, along)
    face_flux = jnp.maximum(face_speed, 0.0) * left_value + jnp.minimum(face_speed, 0.0) * right_value
    return take_cells(face_flux, 0, length, along) - take_cells(face_flux, 1, length, along)

def advect_one(tracer, east_speed, north_speed, wet_cells, north_count, east_count):
    inner_rows = slice(3, 3 + north_count)
    inner_cols = slice(3, 3 + east_count)
    along_east = flux_tendency(tracer[:, inner_rows, :], east_speed[:, inner_rows, :], wet_cells[:, inner_rows, :], 2, east_count)
    along_north = flux_tendency(tracer[:, :, inner_cols], north_speed[:, :, inner_cols], wet_cells[:, :, inner_cols], 1, north_count)
    inner = tracer[:, inner_rows, inner_cols]
    return wet_cells[:, inner_rows, inner_cols] * (inner + TIME_STEP * (along_east + along_north))

def advance(extended, north_count, east_count):
    advected = lax.map(lambda tracer: advect_one(tracer, extended[0], extended[1], extended[5], north_count, east_count), extended[:5])
    east_speed = extended[0]
    north_speed = extended[1]
    east_change = east_speed[:, 3:3 + north_count, 4:4 + east_count] - east_speed[:, 3:3 + north_count, 2:2 + east_count]
    north_change = north_speed[:, 4:4 + north_count, 3:3 + east_count] - north_speed[:, 2:2 + north_count, 3:3 + east_count]
    return (advected, 0.5 * (east_change + north_change))

def wet_mask(ocean_mask, depth_levels):
    level_ids = jnp.arange(NZ, dtype=jnp.int32)[:, None, None]
    wet_cells = (ocean_mask[None] == 1) & (level_ids < depth_levels[None])
    return wet_cells.astype(jnp.float32)

def vertical_diff(array):
    zero_layer = jnp.zeros_like(array[:1])
    upper = jnp.concatenate([array[1:], zero_layer], 0)
    lower = jnp.concatenate([zero_layer, array[:-1]], 0)
    return 0.5 * (upper - lower)

def mix_column(tracer, rates, wet_cells, bond):
    face_flux = rates * bond * (tracer[1:] - tracer[:-1])
    zero_layer = jnp.zeros_like(face_flux[:1])
    padded = jnp.concatenate([zero_layer, face_flux, zero_layer], 0)
    return wet_cells * (tracer + TIME_STEP * (padded[1:] - padded[:-1]))

def rate_gradient(tracer, grad_tracer, wet_cells, bond):
    weighted = wet_cells * grad_tracer
    return TIME_STEP * (weighted[:-1] - weighted[1:]) * bond * (tracer[1:] - tracer[:-1])

def closure_forward(advected, in_weight, in_bias, out_weight):
    levels = advected.shape[1]
    features = jnp.concatenate([advected[0], advected[1], advected[3], advected[4]], 0).reshape(4 * levels, -1).astype(jnp.bfloat16)
    hidden_pre = lax.dot_general(in_weight, features, (((0,), (0,)), ((), ())), preferred_element_type=jnp.float32) + in_bias[:, None]
    activity = jnp.tanh(hidden_pre)
    hidden = activity.astype(jnp.bfloat16)
    output = lax.dot_general(out_weight, hidden, (((0,), (0,)), ((), ())), preferred_element_type=jnp.float32)
    rates = RATE_MAX * jax.nn.sigmoid(output)
    return (features, activity, hidden, rates)

def closure_backward(features, activity, hidden, rates, grad_rates, out_weight):
    grad_output = (grad_rates * rates * (1.0 - rates / RATE_MAX)).astype(jnp.bfloat16)
    grad_w_out = lax.dot_general(hidden, grad_output, (((1,), (1,)), ((), ())), preferred_element_type=jnp.float32)
    grad_pre = jnp.dot(out_weight, grad_output, preferred_element_type=jnp.float32) * (1.0 - activity * activity)
    grad_b_in = lax.optimization_barrier(jnp.sum(grad_pre, axis=1))
    grad_w_in = lax.dot_general(features, grad_pre.astype(jnp.bfloat16), (((1,), (1,)), ((), ())), preferred_element_type=jnp.float32)
    return (grad_w_in, grad_b_in, grad_w_out)

def column_step(advected, masked, wet_cells, spread, cotangent, in_weight, in_bias, out_weight):
    features, activity, hidden, rates_flat = closure_forward(advected, in_weight, in_bias, out_weight)
    rates = rates_flat.reshape(wet_cells.shape[0] - 1, wet_cells.shape[1], wet_cells.shape[2])
    bond = wet_cells[:-1] * wet_cells[1:]
    heat = mix_column(advected[3], rates, wet_cells, bond)
    salt = mix_column(advected[4], rates, wet_cells, bond)
    density = THERMAL * heat - HALINE * salt
    forcing = wet_cells * (vertical_diff(density) - (spread + vertical_diff(masked[2])) / TIME_STEP)
    adjoint_source = TIME_STEP * vertical_diff(wet_cells * cotangent[2])
    saved = (features, activity, hidden, rates_flat, bond, heat, salt)
    return (saved, forcing, adjoint_source)

def finish_step(advected, wet_cells, pressure, back, cotangent, saved, out_weight):
    features, activity, hidden, rates_flat, bond, heat, salt = saved
    new_w = wet_cells * (advected[2] - TIME_STEP * vertical_diff(pressure))
    new_fields = jnp.stack([advected[0], advected[1], new_w, heat, salt])
    grad_density = -vertical_diff(wet_cells * back)
    grad_heat = cotangent[3] + THERMAL * grad_density
    grad_salt = cotangent[4] - HALINE * grad_density
    grad_rates = rate_gradient(advected[3], grad_heat, wet_cells, bond) + rate_gradient(advected[4], grad_salt, wet_cells, bond)
    grads = closure_backward(features, activity, hidden, rates_flat, grad_rates.reshape(rates_flat.shape), out_weight)
    return (new_fields, grads)

def dct_matrix(length):
    freq = jnp.arange(length, dtype=jnp.float32)[:, None]
    cells = jnp.arange(length, dtype=jnp.float32)[None, :]
    scale = jnp.where(freq == 0.0, jnp.sqrt(1.0 / length), jnp.sqrt(2.0 / length))
    return scale * jnp.cos(math.pi * (cells + 0.5) * freq / length)

def eigen_values(freq, length):
    return 2.0 - 2.0 * jnp.cos(math.pi * freq.astype(jnp.float32) / length)

def spectral_solve(source):
    high = lax.Precision.HIGHEST
    level_matrix = dct_matrix(NZ)
    north_matrix = dct_matrix(NY)
    east_matrix = dct_matrix(NX)
    spectrum = jnp.einsum('mz,zyx->myx', level_matrix, source, precision=high)
    spectrum = jnp.einsum('ky,myx->mkx', north_matrix, spectrum, precision=high)
    spectrum = jnp.einsum('myx,kx->myk', spectrum, east_matrix, precision=high)
    denominator = SPECTRAL_SHIFT + eigen_values(jnp.arange(NZ), NZ)[:, None, None] + eigen_values(jnp.arange(NY), NY)[None, :, None] + eigen_values(jnp.arange(NX), NX)[None, None, :]
    spectrum = spectrum / denominator
    spectrum = jnp.einsum('myk,kx->myx', spectrum, east_matrix, precision=high)
    spectrum = jnp.einsum('ky,mkx->myx', north_matrix, spectrum, precision=high)
    return jnp.einsum('mz,myx->zyx', level_matrix, spectrum, precision=high)

def reference(fields, cotangent, ocean_mask, depth_levels, in_weight, in_bias, out_weight):
    wet_cells = wet_mask(ocean_mask, depth_levels)
    masked = fields * wet_cells[None]
    stacked = jnp.concatenate([masked, wet_cells[None]], 0)
    extended = jnp.pad(stacked, ((0, 0), (0, 0), (3, 3), (3, 3)))
    advected, spread = advance(extended, NY, NX)
    saved, forcing, adjoint_source = column_step(advected, masked, wet_cells, spread, cotangent, in_weight, in_bias, out_weight)
    pressure = spectral_solve(forcing)
    back = spectral_solve(adjoint_source)
    new_fields, grads = finish_step(advected, wet_cells, pressure, back, cotangent, saved, out_weight)
    return (new_fields, pressure, grads[0], grads[1], grads[2])
```

```python
import math

import jax
import jax.numpy as jnp
from jax import lax
from jax.sharding import PartitionSpec as P

NZ = 64


TIME_STEP = 0.2
RATE_MAX = 2.0
THERMAL = 0.5
HALINE = 0.5
SPECTRAL_SHIFT = 0.001
WENO_EPS = 1e-06


def padded_2(block, sides, width):
    for axis, dim in sides:
        count = lax.axis_size(axis)
        forward = [(i, i + 1) for i in range(count - 1)]
        backward = [(target, source) for source, target in forward]
        low = lax.ppermute(
            lax.slice_in_dim(block, block.shape[dim] - width, None, axis=dim), axis, forward
        )
        high = lax.ppermute(lax.slice_in_dim(block, 0, width, axis=dim), axis, backward)
        block = jnp.concatenate([low, block, high], axis=dim)
    return block


def weno_face(first, second, third, fourth, fifth):
    cand_low = (2.0 * first - 7.0 * second + 11.0 * third) / 6.0
    cand_mid = (-second + 5.0 * third + 2.0 * fourth) / 6.0
    cand_high = (2.0 * third + 5.0 * fourth - fifth) / 6.0
    rough_low = 13.0 / 12.0 * jnp.square(first - 2.0 * second + third) + 0.25 * jnp.square(
        first - 4.0 * second + 3.0 * third
    )
    rough_mid = 13.0 / 12.0 * jnp.square(second - 2.0 * third + fourth) + 0.25 * jnp.square(
        second - fourth
    )
    rough_high = 13.0 / 12.0 * jnp.square(third - 2.0 * fourth + fifth) + 0.25 * jnp.square(
        3.0 * third - 4.0 * fourth + fifth
    )
    weight_low = 0.1 / jnp.square(WENO_EPS + rough_low)
    weight_mid = 0.6 / jnp.square(WENO_EPS + rough_mid)
    weight_high = 0.3 / jnp.square(WENO_EPS + rough_high)
    return (weight_low * cand_low + weight_mid * cand_mid + weight_high * cand_high) / (
        weight_low + weight_mid + weight_high
    )


def take_cells(array, start, length, along):
    return lax.slice_in_dim(array, start, start + length, axis=along)


def flux_tendency(tracer, velocity, wet_cells, along, length):
    shifted = [take_cells(tracer, offset, length + 1, along) for offset in range(6)]
    left_value = weno_face(shifted[0], shifted[1], shifted[2], shifted[3], shifted[4])
    right_value = weno_face(shifted[5], shifted[4], shifted[3], shifted[2], shifted[1])
    face_speed = 0.5 * (
        take_cells(velocity, 2, length + 1, along) + take_cells(velocity, 3, length + 1, along)
    )
    face_speed = (
        face_speed
        * take_cells(wet_cells, 2, length + 1, along)
        * take_cells(wet_cells, 3, length + 1, along)
    )
    face_flux = (
        jnp.maximum(face_speed, 0.0) * left_value + jnp.minimum(face_speed, 0.0) * right_value
    )
    return take_cells(face_flux, 0, length, along) - take_cells(face_flux, 1, length, along)


def advect_one(tracer, east_speed, north_speed, wet_cells, north_count, east_count):
    inner_rows = slice(3, 3 + north_count)
    inner_cols = slice(3, 3 + east_count)
    along_east = flux_tendency(
        tracer[:, inner_rows, :],
        east_speed[:, inner_rows, :],
        wet_cells[:, inner_rows, :],
        2,
        east_count,
    )
    along_north = flux_tendency(
        tracer[:, :, inner_cols],
        north_speed[:, :, inner_cols],
        wet_cells[:, :, inner_cols],
        1,
        north_count,
    )
    inner = tracer[:, inner_rows, inner_cols]
    return wet_cells[:, inner_rows, inner_cols] * (inner + TIME_STEP * (along_east + along_north))


def advance(extended, north_count, east_count):
    advected = lax.map(
        lambda tracer: advect_one(
            tracer, extended[0], extended[1], extended[5], north_count, east_count
        ),
        extended[:5],
    )
    east_speed = extended[0]
    north_speed = extended[1]
    east_change = (
        east_speed[:, 3 : 3 + north_count, 4 : 4 + east_count]
        - east_speed[:, 3 : 3 + north_count, 2 : 2 + east_count]
    )
    north_change = (
        north_speed[:, 4 : 4 + north_count, 3 : 3 + east_count]
        - north_speed[:, 2 : 2 + north_count, 3 : 3 + east_count]
    )
    return (advected, 0.5 * (east_change + north_change))


def wet_mask(ocean_mask, depth_levels):
    level_ids = jnp.arange(NZ, dtype=jnp.int32)[:, None, None]
    wet_cells = (ocean_mask[None] == 1) & (level_ids < depth_levels[None])
    return wet_cells.astype(jnp.float32)


def vertical_diff(array):
    zero_layer = jnp.zeros_like(array[:1])
    upper = jnp.concatenate([array[1:], zero_layer], 0)
    lower = jnp.concatenate([zero_layer, array[:-1]], 0)
    return 0.5 * (upper - lower)


def mix_column(tracer, rates, wet_cells, bond):
    face_flux = rates * bond * (tracer[1:] - tracer[:-1])
    zero_layer = jnp.zeros_like(face_flux[:1])
    padded = jnp.concatenate([zero_layer, face_flux, zero_layer], 0)
    return wet_cells * (tracer + TIME_STEP * (padded[1:] - padded[:-1]))


def rate_gradient(tracer, grad_tracer, wet_cells, bond):
    weighted = wet_cells * grad_tracer
    return TIME_STEP * (weighted[:-1] - weighted[1:]) * bond * (tracer[1:] - tracer[:-1])


def closure_forward(advected, in_weight, in_bias, out_weight):
    levels = advected.shape[1]
    features = (
        jnp.concatenate([advected[0], advected[1], advected[3], advected[4]], 0)
        .reshape(4 * levels, -1)
        .astype(jnp.bfloat16)
    )
    hidden_pre = (
        lax.dot_general(
            in_weight, features, (((0,), (0,)), ((), ())), preferred_element_type=jnp.float32
        )
        + in_bias[:, None]
    )
    activity = jnp.tanh(hidden_pre)
    hidden = activity.astype(jnp.bfloat16)
    output = lax.dot_general(
        out_weight, hidden, (((0,), (0,)), ((), ())), preferred_element_type=jnp.float32
    )
    rates = RATE_MAX * jax.nn.sigmoid(output)
    return (features, activity, hidden, rates)


def closure_backward(features, activity, hidden, rates, grad_rates, out_weight):
    grad_output = (grad_rates * rates * (1.0 - rates / RATE_MAX)).astype(jnp.bfloat16)
    grad_w_out = lax.dot_general(
        hidden, grad_output, (((1,), (1,)), ((), ())), preferred_element_type=jnp.float32
    )
    grad_pre = jnp.dot(out_weight, grad_output, preferred_element_type=jnp.float32) * (
        1.0 - activity * activity
    )
    grad_b_in = jnp.sum(grad_pre, axis=1)
    grad_w_in = lax.dot_general(
        features,
        grad_pre.astype(jnp.bfloat16),
        (((1,), (1,)), ((), ())),
        preferred_element_type=jnp.float32,
    )
    return (grad_w_in, grad_b_in, grad_w_out)


def column_step(advected, masked, wet_cells, spread, cotangent, in_weight, in_bias, out_weight):
    features, activity, hidden, rates_flat = closure_forward(
        advected, in_weight, in_bias, out_weight
    )
    rates = rates_flat.reshape(wet_cells.shape[0] - 1, wet_cells.shape[1], wet_cells.shape[2])
    bond = wet_cells[:-1] * wet_cells[1:]
    heat = mix_column(advected[3], rates, wet_cells, bond)
    salt = mix_column(advected[4], rates, wet_cells, bond)
    density = THERMAL * heat - HALINE * salt
    forcing = wet_cells * (vertical_diff(density) - (spread + vertical_diff(masked[2])) / TIME_STEP)
    adjoint_source = TIME_STEP * vertical_diff(wet_cells * cotangent[2])
    saved = (features, activity, hidden, rates_flat, bond, heat, salt)
    return (saved, forcing, adjoint_source)


def finish_step(advected, wet_cells, pressure, back, cotangent, saved, out_weight):
    features, activity, hidden, rates_flat, bond, heat, salt = saved
    new_w = wet_cells * (advected[2] - TIME_STEP * vertical_diff(pressure))
    new_fields = jnp.stack([advected[0], advected[1], new_w, heat, salt])
    grad_density = -vertical_diff(wet_cells * back)
    grad_heat = cotangent[3] + THERMAL * grad_density
    grad_salt = cotangent[4] - HALINE * grad_density
    grad_rates = rate_gradient(advected[3], grad_heat, wet_cells, bond) + rate_gradient(
        advected[4], grad_salt, wet_cells, bond
    )
    grads = closure_backward(
        features, activity, hidden, rates_flat, grad_rates.reshape(rates_flat.shape), out_weight
    )
    return (new_fields, grads)


def dct_matrix(length):
    freq = jnp.arange(length, dtype=jnp.float32)[:, None]
    cells = jnp.arange(length, dtype=jnp.float32)[None, :]
    scale = jnp.where(freq == 0.0, jnp.sqrt(1.0 / length), jnp.sqrt(2.0 / length))
    return scale * jnp.cos(math.pi * (cells + 0.5) * freq / length)


def eigen_values(freq, length):
    return 2.0 - 2.0 * jnp.cos(math.pi * freq.astype(jnp.float32) / length)


def spectral_denominator(plane_ids, north_ids, east_ids, north_total, east_total):
    level_part = eigen_values(plane_ids % NZ, NZ)[:, None, None]
    north_part = eigen_values(north_ids, north_total)[None, :, None]
    east_part = eigen_values(east_ids, east_total)[None, None, :]
    return SPECTRAL_SHIFT + level_part + north_part + east_part


AXES = ("rows", "cols")


def mesh_size():
    return lax.axis_size("rows") * lax.axis_size("cols")


def whole_planes(block):
    rows_total, cols_total = lax.axis_size("rows"), lax.axis_size("cols")
    levels, north, east = block.shape
    share = -(-levels // mesh_size())
    if share * mesh_size() != levels:
        block = jnp.pad(block, ((0, share * mesh_size() - levels), (0, 0), (0, 0)))
    swapped = lax.all_to_all(block, AXES, split_axis=0, concat_axis=0, tiled=True)
    return (
        swapped.reshape(rows_total, cols_total, share, north, east)
        .transpose(2, 1, 3, 0, 4)
        .reshape(share, cols_total * north, rows_total * east)
    )


def block_of_planes(planes, levels):
    rows_total, cols_total = lax.axis_size("rows"), lax.axis_size("cols")
    share, north_total, east_total = planes.shape
    north, east = north_total // cols_total, east_total // rows_total
    ordered = (
        planes.reshape(share, cols_total, north, rows_total, east)
        .transpose(3, 1, 0, 2, 4)
        .reshape(rows_total * cols_total * share, north, east)
    )
    return lax.all_to_all(ordered, AXES, split_axis=0, concat_axis=0, tiled=True)[:levels]


def spectral_solve(source):
    high = lax.Precision.HIGH
    level_matrix = dct_matrix(NZ)
    planes = whole_planes(jnp.einsum("mz,zyx->myx", level_matrix, source, precision=high))
    share, north_total, east_total = planes.shape
    north_matrix = dct_matrix(north_total)
    east_matrix = dct_matrix(east_total)
    device = lax.axis_index("rows") * lax.axis_size("cols") + lax.axis_index("cols")
    plane_ids = device * share + jnp.arange(share, dtype=jnp.int32)
    spectrum = jnp.einsum("ky,pyx->pkx", north_matrix, planes, precision=high)
    spectrum = jnp.einsum("pyx,kx->pyk", spectrum, east_matrix, precision=high)
    spectrum = spectrum / spectral_denominator(
        plane_ids, jnp.arange(north_total), jnp.arange(east_total), north_total, east_total
    )
    spectrum = jnp.einsum("pyk,kx->pyx", spectrum, east_matrix, precision=high)
    spectrum = jnp.einsum("ky,pkx->pyx", north_matrix, spectrum, precision=high)
    solved = block_of_planes(spectrum, NZ)
    return jnp.einsum("mz,myx->zyx", level_matrix, solved, precision=high)


def sum_over_mesh(parts):
    count = mesh_size()
    flat = jnp.concatenate([part.reshape(-1) for part in parts])
    total = flat.shape[0]
    chunk = -(-total // (count * 1024)) * 1024
    flat = jnp.pad(flat, (0, chunk * count - total)).reshape(count, chunk // 128, 128)
    pieces = lax.all_to_all(flat, AXES, split_axis=0, concat_axis=0, tiled=True)
    summed = jnp.broadcast_to(jnp.sum(pieces, 0, keepdims=True), flat.shape)
    flat = lax.all_to_all(summed, AXES, split_axis=0, concat_axis=0, tiled=True).reshape(-1)
    results = []
    start = 0
    for part in parts:
        results.append(flat[start : start + part.size].reshape(part.shape))
        start += part.size
    return results


def per_device(fields, cotangent, ocean_mask, depth_levels, in_weight, in_bias, out_weight):
    north_count = fields.shape[2]
    east_count = fields.shape[3]
    wet_cells = wet_mask(ocean_mask, depth_levels)
    masked = fields * wet_cells[None]
    stacked = jnp.concatenate([masked, wet_cells[None]], 0)
    extended = padded_2(stacked, (("rows", 3), ("cols", 2)), 3)
    advected, spread = advance(extended, north_count, east_count)
    saved, forcing, adjoint_source = column_step(
        advected, masked, wet_cells, spread, cotangent, in_weight, in_bias, out_weight
    )
    back = spectral_solve(adjoint_source)
    pressure = spectral_solve(forcing)
    new_fields, grads = finish_step(
        advected, wet_cells, pressure, back, cotangent, saved, out_weight
    )
    grad_w_in, grad_b_in, grad_w_out = sum_over_mesh(grads)
    return (new_fields, pressure, grad_w_in, grad_b_in, grad_w_out)


def solution(mesh):
    in_specs = (
        P(None, None, "cols", "rows"),
        P(None, None, "cols", "rows"),
        P("cols", "rows"),
        P("cols", "rows"),
        P(),
        P(),
        P(),
    )
    out_specs = (P(None, None, "cols", "rows"), P(None, "cols", "rows"), P(), P(), P())
    return jax.shard_map(
        per_device, mesh=mesh, in_specs=in_specs, out_specs=out_specs, check_vma=False
    )
```

```python
import math

import jax
import jax.numpy as jnp
from jax import lax
from jax.experimental import pallas as pl
from jax.experimental.pallas import tpu as pltpu
from jax.sharding import PartitionSpec as P

NZ = 64


TIME_STEP = 0.2
RATE_MAX = 2.0
THERMAL = 0.5
HALINE = 0.5
SPECTRAL_SHIFT = 0.001
WENO_EPS = 1e-06


HALO = 3
FIELDS = 5
SUB = 8


def pack_kernel(dep_ref, fields_ref, xfirst_ref, xlast_ref, yfirst_ref, ylast_ref):
    field = pl.program_id(0)
    north, east = dep_ref.shape
    levels = fields_ref.shape[1] // north
    per = east // north
    blocks = levels // per
    dep = dep_ref[...]
    tiled = jnp.concatenate([dep] * per, 0)
    level_in_block = lax.broadcasted_iota(jnp.int32, (east, east), 0) // north
    for t in range(blocks):
        block = fields_ref[0, t * east : (t + 1) * east, :]
        masked = jnp.where(level_in_block + t * per < tiled, block, 0.0)
        turned = masked.T
        row = field * blocks + t
        for s in range(HALO):
            xfirst_ref[s, pl.ds(row, 1), :] = turned[s : s + 1]
            xlast_ref[s, pl.ds(row, 1), :] = turned[east - HALO + s : east - HALO + s + 1]
    level = lax.broadcasted_iota(jnp.int32, (levels, east), 0)
    for s in range(HALO):
        at = pl.multiple_of((field * HALO + s) * levels, SUB)
        low, high = s, north - HALO + s
        first = fields_ref[0, pl.ds(low, levels, stride=north), :]
        last = fields_ref[0, pl.ds(high, levels, stride=north), :]
        yfirst_ref[pl.ds(at, levels), :] = jnp.where(level < dep[low : low + 1], first, 0.0)
        ylast_ref[pl.ds(at, levels), :] = jnp.where(level < dep[high : high + 1], last, 0.0)

    @pl.when(field == 0)
    def _():
        depths = dep.astype(jnp.float32)
        end = FIELDS * HALO * levels
        yfirst_ref[end:, :] = jnp.broadcast_to(depths[:1], (SUB, east))
        ylast_ref[end:, :] = jnp.broadcast_to(depths[north - 1 :], (SUB, east))
        turned = tiled.astype(jnp.float32).T
        for s in range(HALO):
            high = east - HALO + s
            xfirst_ref[s, FIELDS * blocks :, :] = jnp.broadcast_to(turned[s : s + 1], (SUB, east))
            xlast_ref[s, FIELDS * blocks :, :] = jnp.broadcast_to(
                turned[high : high + 1], (SUB, east)
            )


def pack_edges(fields, dep):
    _, levels, north, east = fields.shape
    rows = FIELDS * levels * north // east + SUB
    x_shape = jax.ShapeDtypeStruct((HALO, rows, east), jnp.float32)
    y_shape = jax.ShapeDtypeStruct((FIELDS * HALO * levels + SUB, east), jnp.float32)
    whole = lambda shape: pl.BlockSpec(shape.shape, lambda f: (0,) * len(shape.shape))
    return pl.pallas_call(
        pack_kernel,
        grid=(FIELDS,),
        in_specs=[
            pl.BlockSpec((north, east), lambda f: (0, 0)),
            pl.BlockSpec((1, levels * north, east), lambda f: (f, 0, 0)),
        ],
        out_specs=[whole(x_shape), whole(x_shape), whole(y_shape), whole(y_shape)],
        out_shape=[x_shape, x_shape, y_shape, y_shape],
        compiler_params=pltpu.CompilerParams(vmem_limit_bytes=32 << 20),
    )(dep, fields.reshape(FIELDS, levels * north, east))


def face_flux(slopes, left, right, speed, share):
    dm2, dm1, d0, dp1, dp2 = slopes
    ahead = speed > 0.0
    e1 = jnp.where(ahead, dm2, dp2)
    e2 = jnp.where(ahead, dm1, dp1)
    e4 = jnp.where(ahead, dp1, dm1)
    near = jnp.where(ahead, left, right)
    bend0, bend1, bend2 = e2 - e1, d0 - e2, e4 - d0
    twice2, twice3 = e2 + e2, d0 + d0
    tilt0, tilt1, tilt2 = bend0 + twice2, e2 + d0, bend2 - twice3
    rough0 = bend0 * bend0 * (13.0 / 3.0) + (tilt0 * tilt0 + 4.0 * WENO_EPS)
    rough1 = bend1 * bend1 * (13.0 / 3.0) + (tilt1 * tilt1 + 4.0 * WENO_EPS)
    rough2 = bend2 * bend2 * (13.0 / 3.0) + (tilt2 * tilt2 + 4.0 * WENO_EPS)
    pair0, pair1, pair2 = rough1 * rough2, rough0 * rough2, rough0 * rough1
    g0, g1, g2 = pair0 * pair0, 6.0 * (pair1 * pair1), 3.0 * (pair2 * pair2)
    total = g0 * (5.0 * e2 - (e1 + e1)) + g1 * (e2 + twice3) + g2 * (4.0 * d0 - e4)
    return speed * near + share * (total * pltpu.reciprocal(g0 + g1 + g2, approx=True))


def advect_kernel(
    dep_ref, fields_ref, xlo_ref, xhi_ref, ylo_ref, yhi_ref,
    adv_ref, spread_ref, wm_ref,
    deep, both, lines, slopes, fluxes, cells, wets, su, su6, sv, sv6, sides,
):
    step = pl.program_id(0)
    north, east = dep_ref.shape
    per = east // north
    blocks = SUB // per
    all_blocks = (xlo_ref.shape[1] - SUB) // FIELDS
    levels = all_blocks * per
    depth_row = FIELDS * all_blocks
    depth_end = FIELDS * HALO * levels
    faces = range(0, east + SUB, SUB)
    first_level = step * SUB

    @pl.when(step == 0)
    def _():
        depths = dep_ref[...].astype(jnp.float32)
        deep[SUB : SUB + east, :] = jnp.concatenate([depths] * per, 0).T
        deep[SUB - 1 : SUB, :] = xlo_ref[HALO - 1, depth_row : depth_row + 1, :]
        deep[SUB + east : SUB + east + 1, :] = xhi_ref[0, depth_row : depth_row + 1, :]
        both[:east, :] = jnp.minimum(deep[SUB - 1 : SUB - 1 + east, :], deep[SUB : SUB + east, :])
        both[east : east + 1, :] = jnp.minimum(
            deep[SUB + east - 1 : SUB + east, :], deep[SUB + east : SUB + east + 1, :]
        )

    level = (lax.broadcasted_iota(jnp.int32, (SUB, east), 0) + first_level).astype(jnp.float32)
    side_level = lax.broadcasted_iota(jnp.int32, (SUB, east), 1) // north + first_level
    depths = dep_ref[...].astype(jnp.float32)
    wets[0] = (level < ylo_ref[depth_end : depth_end + 1, :]).astype(jnp.float32)
    wets[north + 1] = (level < yhi_ref[depth_end : depth_end + 1, :]).astype(jnp.float32)
    for y in range(north):
        wets[y + 1] = (level < depths[y : y + 1]).astype(jnp.float32)

    def stage(f, carry):
        for s in range(HALO):
            at = pl.multiple_of((f * HALO + s) * levels + first_level, SUB)
            cells[f, s] = ylo_ref[pl.ds(at, SUB), :]
            cells[f, north + HALO + s] = yhi_ref[pl.ds(at, SUB), :]
        for y in range(north):
            cells[f, y + HALO] = fields_ref[f, pl.ds(y, SUB, stride=north), :] * wets[y + 1]
        for b in range(blocks):
            row = f * all_blocks + step * blocks + b
            for s in range(HALO):
                lines[f, b, SUB - HALO + s : SUB - HALO + s + 1, :] = xlo_ref[s, pl.ds(row, 1), :]
                lines[f, b, SUB + east + s : SUB + east + s + 1, :] = xhi_ref[s, pl.ds(row, 1), :]
            turned = fields_ref[f, b * east : (b + 1) * east, :].T
            height = (side_level + b * per).astype(jnp.float32)
            for r in range(0, east, SUB):
                wet = height < deep[SUB + r : 2 * SUB + r, :]
                lines[f, b, SUB + r : 2 * SUB + r, :] = jnp.where(wet, turned[r : r + SUB], 0.0)
        return carry

    lax.fori_loop(0, FIELDS, stage, 0)

    for b in range(blocks):
        height = (side_level + b * per).astype(jnp.float32)
        for r in faces:
            speed = (0.5 * TIME_STEP) * (
                lines[0, b, SUB + r - 1 : 2 * SUB + r - 1, :] + lines[0, b, SUB + r : 2 * SUB + r, :]
            )
            speed = jnp.where(height < both[r : r + SUB, :], speed, 0.0)
            su[b, r : r + SUB, :] = speed
            su6[b, r : r + SUB, :] = jnp.abs(speed) * (1.0 / 6.0)
        change = 0.5 * (
            lines[0, b, SUB + 1 : SUB + 1 + east, :] - lines[0, b, SUB - 1 : SUB - 1 + east, :]
        )
        sides[b * east : (b + 1) * east, :] = change.T
    for y in range(north):
        spread_ref[y] = sides[pl.ds(y, SUB, stride=north), :] + 0.5 * (
            cells[1, y + HALO + 1] - cells[1, y + HALO - 1]
        )
        wm_ref[y] = cells[2, y + HALO]
    for y in range(north + 1):
        speed = (0.5 * TIME_STEP) * (cells[1, y + HALO - 1] + cells[1, y + HALO])
        speed = speed * (wets[y] * wets[y + 1])
        sv[y] = speed
        sv6[y] = jnp.abs(speed) * (1.0 / 6.0)

    def advance_field(f, carry):
        for b in range(blocks):
            for r in range(0, east + 2 * SUB, SUB):
                ahead = lines[f, b, r + 1 : r + 1 + SUB, :]
                slopes[b, r : r + SUB, :] = ahead - lines[f, b, r : r + SUB, :]
            for r in faces:
                at = SUB + r
                near = [slopes[b, at + k : at + k + SUB, :] for k in (-3, -2, -1, 0, 1)]
                fluxes[b, r : r + SUB, :] = face_flux(
                    near,
                    lines[f, b, at - 1 : at - 1 + SUB, :],
                    lines[f, b, at : at + SUB, :],
                    su[b, r : r + SUB, :],
                    su6[b, r : r + SUB, :],
                )
            change = fluxes[b, 0:east, :] - fluxes[b, 1 : 1 + east, :]
            sides[b * east : (b + 1) * east, :] = change.T
        line = [cells[f, k] for k in range(5)]
        inclines = [line[k + 1] - line[k] for k in range(4)]
        south = None
        for y in range(north + 1):
            line.append(cells[f, y + 2 * HALO - 1])
            inclines.append(line[-1] - line[-2])
            north_face = face_flux(inclines[-5:], line[-4], line[-3], sv[y], sv6[y])
            if y > 0:
                change = sides[pl.ds(y - 1, SUB, stride=north), :] + (south - north_face)
                adv_ref[f, y - 1] = wets[y] * (line[-4] + change)
            south = north_face
        return carry

    lax.fori_loop(0, FIELDS, advance_field, 0)


def advect(fields, dep, xlo, xhi, ylo, yhi):
    _, levels, north, east = fields.shape
    whole = lambda a: pl.BlockSpec(a.shape, lambda k: (0,) * a.ndim)
    plane = pl.BlockSpec((north, SUB, east), lambda k: (0, k, 0))
    f32 = jnp.float32
    one = jax.ShapeDtypeStruct((north, levels, east), f32)
    blocks = SUB * north // east
    return pl.pallas_call(
        advect_kernel,
        grid=(levels // SUB,),
        in_specs=[
            whole(dep),
            pl.BlockSpec((FIELDS, SUB * north, east), lambda k: (0, k, 0)),
            whole(xlo), whole(xhi), whole(ylo), whole(yhi),
        ],
        out_specs=[
            pl.BlockSpec((FIELDS, north, SUB, east), lambda k: (0, 0, k, 0)), plane, plane,
        ],
        out_shape=[jax.ShapeDtypeStruct((FIELDS, north, levels, east), f32), one, one],
        scratch_shapes=[
            pltpu.VMEM((east + 2 * SUB, east), f32),
            pltpu.VMEM((east + SUB, east), f32),
            pltpu.VMEM((FIELDS, blocks, east + 3 * SUB, east), f32),
            pltpu.VMEM((blocks, east + 3 * SUB, east), f32),
            pltpu.VMEM((blocks, east + SUB, east), f32),
            pltpu.VMEM((FIELDS, north + 2 * HALO, SUB, east), f32),
            pltpu.VMEM((north + 2, SUB, east), f32),
            pltpu.VMEM((blocks, east + SUB, east), f32),
            pltpu.VMEM((blocks, east + SUB, east), f32),
            pltpu.VMEM((north + 1, SUB, east), f32),
            pltpu.VMEM((north + 1, SUB, east), f32),
            pltpu.VMEM((SUB * north, east), f32),
        ],
        compiler_params=pltpu.CompilerParams(vmem_limit_bytes=40 << 20),
        cost_estimate=pl.CostEstimate(
            flops=int(fields.size) * 130, bytes_accessed=2 * 4 * int(fields.size), transcendentals=0
        ),
    )(dep, fields.reshape(FIELDS, levels * north, east), xlo, xhi, ylo, yhi)


def shift_both(block, axis, first, last):
    count = lax.axis_size(axis)
    forward = [(i, i + 1) for i in range(count - 1)]
    backward = [(i + 1, i) for i in range(count - 1)]
    return lax.ppermute(last, axis, forward), lax.ppermute(first, axis, backward)


def advance_block(fields, dep):
    xfirst, xlast, yfirst, ylast = pack_edges(fields, dep)
    ylo, yhi = shift_both(None, "cols", yfirst, ylast)
    xlo, xhi = shift_both(None, "rows", xfirst, xlast)
    return advect(fields, dep, xlo, xhi, ylo, yhi)


def wet_mask(ocean_mask, depth_levels):
    level_ids = jnp.arange(NZ, dtype=jnp.int32)[:, None, None]
    wet_cells = (ocean_mask[None] == 1) & (level_ids < depth_levels[None])
    return wet_cells.astype(jnp.float32)


def vertical_diff(array):
    zero_layer = jnp.zeros_like(array[:1])
    upper = jnp.concatenate([array[1:], zero_layer], 0)
    lower = jnp.concatenate([zero_layer, array[:-1]], 0)
    return 0.5 * (upper - lower)


def mix_column(tracer, rates, wet_cells, bond):
    face_flux = rates * bond * (tracer[1:] - tracer[:-1])
    zero_layer = jnp.zeros_like(face_flux[:1])
    padded = jnp.concatenate([zero_layer, face_flux, zero_layer], 0)
    return wet_cells * (tracer + TIME_STEP * (padded[1:] - padded[:-1]))


def rate_gradient(tracer, grad_tracer, wet_cells, bond):
    weighted = wet_cells * grad_tracer
    return TIME_STEP * (weighted[:-1] - weighted[1:]) * bond * (tracer[1:] - tracer[:-1])


def closure_forward(advected, in_weight, in_bias, out_weight):
    levels = advected.shape[1]
    features = (
        jnp.concatenate([advected[0], advected[1], advected[3], advected[4]], 0)
        .reshape(4 * levels, -1)
        .astype(jnp.bfloat16)
    )
    hidden_pre = (
        lax.dot_general(
            in_weight, features, (((0,), (0,)), ((), ())), preferred_element_type=jnp.float32
        )
        + in_bias[:, None]
    )
    activity = jnp.tanh(hidden_pre)
    hidden = activity.astype(jnp.bfloat16)
    output = lax.dot_general(
        out_weight, hidden, (((0,), (0,)), ((), ())), preferred_element_type=jnp.float32
    )
    rates = RATE_MAX * jax.nn.sigmoid(output)
    return (features, activity, hidden, rates)


def closure_backward(features, activity, hidden, rates, grad_rates, out_weight):
    grad_output = (grad_rates * rates * (1.0 - rates / RATE_MAX)).astype(jnp.bfloat16)
    grad_w_out = lax.dot_general(
        hidden, grad_output, (((1,), (1,)), ((), ())), preferred_element_type=jnp.float32
    )
    grad_pre = jnp.dot(out_weight, grad_output, preferred_element_type=jnp.float32) * (
        1.0 - activity * activity
    )
    grad_b_in = jnp.sum(grad_pre, axis=1)
    grad_w_in = lax.dot_general(
        features,
        grad_pre.astype(jnp.bfloat16),
        (((1,), (1,)), ((), ())),
        preferred_element_type=jnp.float32,
    )
    return (grad_w_in, grad_b_in, grad_w_out)


def column_step(advected, masked, wet_cells, spread, cotangent, in_weight, in_bias, out_weight):
    features, activity, hidden, rates_flat = closure_forward(
        advected, in_weight, in_bias, out_weight
    )
    rates = rates_flat.reshape(wet_cells.shape[0] - 1, wet_cells.shape[1], wet_cells.shape[2])
    bond = wet_cells[:-1] * wet_cells[1:]
    heat = mix_column(advected[3], rates, wet_cells, bond)
    salt = mix_column(advected[4], rates, wet_cells, bond)
    density = THERMAL * heat - HALINE * salt
    forcing = wet_cells * (vertical_diff(density) - (spread + vertical_diff(masked[2])) / TIME_STEP)
    adjoint_source = TIME_STEP * vertical_diff(wet_cells * cotangent[2])
    saved = (features, activity, hidden, rates_flat, bond, heat, salt)
    return (saved, forcing, adjoint_source)


def finish_step(advected, wet_cells, pressure, back, cotangent, saved, out_weight):
    features, activity, hidden, rates_flat, bond, heat, salt = saved
    new_w = wet_cells * (advected[2] - TIME_STEP * vertical_diff(pressure))
    new_fields = jnp.stack([advected[0], advected[1], new_w, heat, salt])
    grad_density = -vertical_diff(wet_cells * back)
    grad_heat = cotangent[3] + THERMAL * grad_density
    grad_salt = cotangent[4] - HALINE * grad_density
    grad_rates = rate_gradient(advected[3], grad_heat, wet_cells, bond) + rate_gradient(
        advected[4], grad_salt, wet_cells, bond
    )
    grads = closure_backward(
        features, activity, hidden, rates_flat, grad_rates.reshape(rates_flat.shape), out_weight
    )
    return (new_fields, grads)


def dct_matrix(length):
    freq = jnp.arange(length, dtype=jnp.float32)[:, None]
    cells = jnp.arange(length, dtype=jnp.float32)[None, :]
    scale = jnp.where(freq == 0.0, jnp.sqrt(1.0 / length), jnp.sqrt(2.0 / length))
    return scale * jnp.cos(math.pi * (cells + 0.5) * freq / length)


def eigen_values(freq, length):
    return 2.0 - 2.0 * jnp.cos(math.pi * freq.astype(jnp.float32) / length)


def spectral_denominator(plane_ids, north_ids, east_ids, north_total, east_total):
    level_part = eigen_values(plane_ids % NZ, NZ)[:, None, None]
    north_part = eigen_values(north_ids, north_total)[None, :, None]
    east_part = eigen_values(east_ids, east_total)[None, None, :]
    return SPECTRAL_SHIFT + level_part + north_part + east_part


AXES = ("rows", "cols")


def mesh_size():
    return lax.axis_size("rows") * lax.axis_size("cols")


def whole_planes(block):
    rows_total, cols_total = lax.axis_size("rows"), lax.axis_size("cols")
    levels, north, east = block.shape
    share = -(-levels // mesh_size())
    if share * mesh_size() != levels:
        block = jnp.pad(block, ((0, share * mesh_size() - levels), (0, 0), (0, 0)))
    swapped = lax.all_to_all(block, AXES, split_axis=0, concat_axis=0, tiled=True)
    return (
        swapped.reshape(rows_total, cols_total, share, north, east)
        .transpose(2, 1, 3, 0, 4)
        .reshape(share, cols_total * north, rows_total * east)
    )


def block_of_planes(planes, levels):
    rows_total, cols_total = lax.axis_size("rows"), lax.axis_size("cols")
    share, north_total, east_total = planes.shape
    north, east = north_total // cols_total, east_total // rows_total
    ordered = (
        planes.reshape(share, cols_total, north, rows_total, east)
        .transpose(3, 1, 0, 2, 4)
        .reshape(rows_total * cols_total * share, north, east)
    )
    return lax.all_to_all(ordered, AXES, split_axis=0, concat_axis=0, tiled=True)[:levels]


def spectral_solve(source):
    high = lax.Precision.HIGH
    level_matrix = dct_matrix(NZ)
    planes = whole_planes(jnp.einsum("mz,zyx->myx", level_matrix, source, precision=high))
    share, north_total, east_total = planes.shape
    north_matrix = dct_matrix(north_total)
    east_matrix = dct_matrix(east_total)
    device = lax.axis_index("rows") * lax.axis_size("cols") + lax.axis_index("cols")
    plane_ids = device * share + jnp.arange(share, dtype=jnp.int32)
    spectrum = jnp.einsum("ky,pyx->pkx", north_matrix, planes, precision=high)
    spectrum = jnp.einsum("pyx,kx->pyk", spectrum, east_matrix, precision=high)
    spectrum = spectrum / spectral_denominator(
        plane_ids, jnp.arange(north_total), jnp.arange(east_total), north_total, east_total
    )
    spectrum = jnp.einsum("pyk,kx->pyx", spectrum, east_matrix, precision=high)
    spectrum = jnp.einsum("ky,pkx->pyx", north_matrix, spectrum, precision=high)
    solved = block_of_planes(spectrum, NZ)
    return jnp.einsum("mz,myx->zyx", level_matrix, solved, precision=high)


def sum_over_mesh(parts):
    count = mesh_size()
    flat = jnp.concatenate([part.reshape(-1) for part in parts])
    total = flat.shape[0]
    chunk = -(-total // (count * 1024)) * 1024
    flat = jnp.pad(flat, (0, chunk * count - total)).reshape(count, chunk // 128, 128)
    pieces = lax.all_to_all(flat, AXES, split_axis=0, concat_axis=0, tiled=True)
    summed = jnp.broadcast_to(jnp.sum(pieces, 0, keepdims=True), flat.shape)
    flat = lax.all_to_all(summed, AXES, split_axis=0, concat_axis=0, tiled=True).reshape(-1)
    results = []
    start = 0
    for part in parts:
        results.append(flat[start : start + part.size].reshape(part.shape))
        start += part.size
    return results


def per_device(fields, cotangent, ocean_mask, depth_levels, in_weight, in_bias, out_weight):
    wet_cells = wet_mask(ocean_mask, depth_levels)
    masked = fields * wet_cells[None]
    dep = jnp.where(ocean_mask == 1, depth_levels, 0)
    advected, spread, _ = advance_block(fields, dep)
    advected = advected.transpose(0, 2, 1, 3)
    spread = spread.transpose(1, 0, 2)
    saved, forcing, adjoint_source = column_step(
        advected, masked, wet_cells, spread, cotangent, in_weight, in_bias, out_weight
    )
    back = spectral_solve(adjoint_source)
    pressure = spectral_solve(forcing)
    new_fields, grads = finish_step(
        advected, wet_cells, pressure, back, cotangent, saved, out_weight
    )
    grad_w_in, grad_b_in, grad_w_out = sum_over_mesh(grads)
    return (new_fields, pressure, grad_w_in, grad_b_in, grad_w_out)


def solution(mesh):
    in_specs = (
        P(None, None, "cols", "rows"),
        P(None, None, "cols", "rows"),
        P("cols", "rows"),
        P("cols", "rows"),
        P(),
        P(),
        P(),
    )
    out_specs = (P(None, None, "cols", "rows"), P(None, "cols", "rows"), P(), P(), P())
    return jax.shard_map(
        per_device, mesh=mesh, in_specs=in_specs, out_specs=out_specs, check_vma=False
    )
```

```python
import functools

import jax
import jax.numpy as jnp
import numpy as np
from jax import lax
from jax.experimental import pallas as pl
from jax.experimental.pallas import tpu as pltpu
from jax.sharding import PartitionSpec as P

TIME_STEP = 0.2
RATE_MAX = 2.0
THERMAL = 0.5
HALINE = 0.5
SPECTRAL_SHIFT = 0.001
WENO_EPS = 1e-06
HALO = 3
FIELDS = 5
SUB = 8


def pack_kernel(dep_ref, fields_ref, xfirst_ref, xlast_ref, yfirst_ref, ylast_ref):
    field = pl.program_id(0)
    north, east = dep_ref.shape
    levels = fields_ref.shape[1] // north
    per = east // north
    blocks = levels // per
    dep = dep_ref[...]
    tiled = jnp.concatenate([dep] * per, 0)
    level_in_block = lax.broadcasted_iota(jnp.int32, (east, east), 0) // north
    for t in range(blocks):
        block = fields_ref[0, t * east : (t + 1) * east, :]
        masked = jnp.where(level_in_block + t * per < tiled, block, 0.0)
        turned = masked.T
        row = field * blocks + t
        for s in range(HALO):
            xfirst_ref[s, pl.ds(row, 1), :] = turned[s : s + 1]
            xlast_ref[s, pl.ds(row, 1), :] = turned[east - HALO + s : east - HALO + s + 1]
    level = lax.broadcasted_iota(jnp.int32, (levels, east), 0)
    for s in range(HALO):
        at = pl.multiple_of((field * HALO + s) * levels, SUB)
        low, high = s, north - HALO + s
        first = fields_ref[0, pl.ds(low, levels, stride=north), :]
        last = fields_ref[0, pl.ds(high, levels, stride=north), :]
        yfirst_ref[pl.ds(at, levels), :] = jnp.where(level < dep[low : low + 1], first, 0.0)
        ylast_ref[pl.ds(at, levels), :] = jnp.where(level < dep[high : high + 1], last, 0.0)

    @pl.when(field == 0)
    def _():
        depths = dep.astype(jnp.float32)
        end = FIELDS * HALO * levels
        yfirst_ref[end:, :] = jnp.broadcast_to(depths[:1], (SUB, east))
        ylast_ref[end:, :] = jnp.broadcast_to(depths[north - 1 :], (SUB, east))
        turned = tiled.astype(jnp.float32).T
        for s in range(HALO):
            high = east - HALO + s
            xfirst_ref[s, FIELDS * blocks :, :] = jnp.broadcast_to(turned[s : s + 1], (SUB, east))
            xlast_ref[s, FIELDS * blocks :, :] = jnp.broadcast_to(
                turned[high : high + 1], (SUB, east)
            )


def pack_edges(fields, dep):
    _, levels, north, east = fields.shape
    rows = FIELDS * levels * north // east + SUB
    x_shape = jax.ShapeDtypeStruct((HALO, rows, east), jnp.float32)
    y_shape = jax.ShapeDtypeStruct((FIELDS * HALO * levels + SUB, east), jnp.float32)
    whole = lambda shape: pl.BlockSpec(shape.shape, lambda f: (0,) * len(shape.shape))
    return pl.pallas_call(
        pack_kernel,
        grid=(FIELDS,),
        in_specs=[
            pl.BlockSpec((north, east), lambda f: (0, 0)),
            pl.BlockSpec((1, levels * north, east), lambda f: (f, 0, 0)),
        ],
        out_specs=[whole(x_shape), whole(x_shape), whole(y_shape), whole(y_shape)],
        out_shape=[x_shape, x_shape, y_shape, y_shape],
        compiler_params=pltpu.CompilerParams(vmem_limit_bytes=32 << 20),
    )(dep, fields.reshape(FIELDS, levels * north, east))


def face_flux(slopes, left, right, speed, share):
    dm2, dm1, d0, dp1, dp2 = slopes
    ahead = speed > 0.0
    e1 = jnp.where(ahead, dm2, dp2)
    e2 = jnp.where(ahead, dm1, dp1)
    e4 = jnp.where(ahead, dp1, dm1)
    near = jnp.where(ahead, left, right)
    bend0, bend1, bend2 = e2 - e1, d0 - e2, e4 - d0
    twice2, twice3 = e2 + e2, d0 + d0
    tilt0, tilt1, tilt2 = bend0 + twice2, e2 + d0, bend2 - twice3
    rough0 = bend0 * bend0 * (13.0 / 3.0) + (tilt0 * tilt0 + 4.0 * WENO_EPS)
    rough1 = bend1 * bend1 * (13.0 / 3.0) + (tilt1 * tilt1 + 4.0 * WENO_EPS)
    rough2 = bend2 * bend2 * (13.0 / 3.0) + (tilt2 * tilt2 + 4.0 * WENO_EPS)
    pair0, pair1, pair2 = rough1 * rough2, rough0 * rough2, rough0 * rough1
    g0, g1, g2 = pair0 * pair0, 6.0 * (pair1 * pair1), 3.0 * (pair2 * pair2)
    total = g0 * (5.0 * e2 - (e1 + e1)) + g1 * (e2 + twice3) + g2 * (4.0 * d0 - e4)
    return speed * near + share * (total * pltpu.reciprocal(g0 + g1 + g2, approx=True))


def advect_kernel(
    dep_ref, fields_ref, xlo_ref, xhi_ref, ylo_ref, yhi_ref,
    adv_ref, spread_ref, wm_ref,
    deep, both, lines, slopes, fluxes, cells, wets, su, su6, sv, sv6, sides,
):
    step = pl.program_id(0)
    north, east = dep_ref.shape
    per = east // north
    blocks = SUB // per
    all_blocks = (xlo_ref.shape[1] - SUB) // FIELDS
    levels = all_blocks * per
    depth_row = FIELDS * all_blocks
    depth_end = FIELDS * HALO * levels
    faces = range(0, east + SUB, SUB)
    first_level = step * SUB

    @pl.when(step == 0)
    def _():
        depths = dep_ref[...].astype(jnp.float32)
        deep[SUB : SUB + east, :] = jnp.concatenate([depths] * per, 0).T
        deep[SUB - 1 : SUB, :] = xlo_ref[HALO - 1, depth_row : depth_row + 1, :]
        deep[SUB + east : SUB + east + 1, :] = xhi_ref[0, depth_row : depth_row + 1, :]
        both[:east, :] = jnp.minimum(deep[SUB - 1 : SUB - 1 + east, :], deep[SUB : SUB + east, :])
        both[east : east + 1, :] = jnp.minimum(
            deep[SUB + east - 1 : SUB + east, :], deep[SUB + east : SUB + east + 1, :]
        )

    level = (lax.broadcasted_iota(jnp.int32, (SUB, east), 0) + first_level).astype(jnp.float32)
    side_level = lax.broadcasted_iota(jnp.int32, (SUB, east), 1) // north + first_level
    depths = dep_ref[...].astype(jnp.float32)
    wets[0] = (level < ylo_ref[depth_end : depth_end + 1, :]).astype(jnp.float32)
    wets[north + 1] = (level < yhi_ref[depth_end : depth_end + 1, :]).astype(jnp.float32)
    for y in range(north):
        wets[y + 1] = (level < depths[y : y + 1]).astype(jnp.float32)

    def stage(f, carry):
        for s in range(HALO):
            at = pl.multiple_of((f * HALO + s) * levels + first_level, SUB)
            cells[f, s] = ylo_ref[pl.ds(at, SUB), :]
            cells[f, north + HALO + s] = yhi_ref[pl.ds(at, SUB), :]
        for y in range(north):
            cells[f, y + HALO] = fields_ref[f, pl.ds(y, SUB, stride=north), :] * wets[y + 1]
        for b in range(blocks):
            row = f * all_blocks + step * blocks + b
            for s in range(HALO):
                lines[f, b, SUB - HALO + s : SUB - HALO + s + 1, :] = xlo_ref[s, pl.ds(row, 1), :]
                lines[f, b, SUB + east + s : SUB + east + s + 1, :] = xhi_ref[s, pl.ds(row, 1), :]
            turned = fields_ref[f, b * east : (b + 1) * east, :].T
            height = (side_level + b * per).astype(jnp.float32)
            for r in range(0, east, SUB):
                wet = height < deep[SUB + r : 2 * SUB + r, :]
                lines[f, b, SUB + r : 2 * SUB + r, :] = jnp.where(wet, turned[r : r + SUB], 0.0)
        return carry

    lax.fori_loop(0, FIELDS, stage, 0)

    for b in range(blocks):
        height = (side_level + b * per).astype(jnp.float32)
        for r in faces:
            speed = (0.5 * TIME_STEP) * (
                lines[0, b, SUB + r - 1 : 2 * SUB + r - 1, :] + lines[0, b, SUB + r : 2 * SUB + r, :]
            )
            speed = jnp.where(height < both[r : r + SUB, :], speed, 0.0)
            su[b, r : r + SUB, :] = speed
            su6[b, r : r + SUB, :] = jnp.abs(speed) * (1.0 / 6.0)
        change = 0.5 * (
            lines[0, b, SUB + 1 : SUB + 1 + east, :] - lines[0, b, SUB - 1 : SUB - 1 + east, :]
        )
        sides[b * east : (b + 1) * east, :] = change.T
    for y in range(north):
        spread_ref[y] = sides[pl.ds(y, SUB, stride=north), :] + 0.5 * (
            cells[1, y + HALO + 1] - cells[1, y + HALO - 1]
        )
        wm_ref[y] = cells[2, y + HALO]
    for y in range(north + 1):
        speed = (0.5 * TIME_STEP) * (cells[1, y + HALO - 1] + cells[1, y + HALO])
        speed = speed * (wets[y] * wets[y + 1])
        sv[y] = speed
        sv6[y] = jnp.abs(speed) * (1.0 / 6.0)

    def advance_field(f, carry):
        for b in range(blocks):
            for r in range(0, east + 2 * SUB, SUB):
                ahead = lines[f, b, r + 1 : r + 1 + SUB, :]
                slopes[b, r : r + SUB, :] = ahead - lines[f, b, r : r + SUB, :]
            for r in faces:
                at = SUB + r
                near = [slopes[b, at + k : at + k + SUB, :] for k in (-3, -2, -1, 0, 1)]
                fluxes[b, r : r + SUB, :] = face_flux(
                    near,
                    lines[f, b, at - 1 : at - 1 + SUB, :],
                    lines[f, b, at : at + SUB, :],
                    su[b, r : r + SUB, :],
                    su6[b, r : r + SUB, :],
                )
            change = fluxes[b, 0:east, :] - fluxes[b, 1 : 1 + east, :]
            sides[b * east : (b + 1) * east, :] = change.T
        line = [cells[f, k] for k in range(5)]
        inclines = [line[k + 1] - line[k] for k in range(4)]
        south = None
        for y in range(north + 1):
            line.append(cells[f, y + 2 * HALO - 1])
            inclines.append(line[-1] - line[-2])
            north_face = face_flux(inclines[-5:], line[-4], line[-3], sv[y], sv6[y])
            if y > 0:
                change = sides[pl.ds(y - 1, SUB, stride=north), :] + (south - north_face)
                adv_ref[f, y - 1] = wets[y] * (line[-4] + change)
            south = north_face
        return carry

    lax.fori_loop(0, FIELDS, advance_field, 0)


def advect(fields, dep, xlo, xhi, ylo, yhi):
    _, levels, north, east = fields.shape
    whole = lambda a: pl.BlockSpec(a.shape, lambda k: (0,) * a.ndim)
    plane = pl.BlockSpec((north, SUB, east), lambda k: (0, k, 0))
    f32 = jnp.float32
    one = jax.ShapeDtypeStruct((north, levels, east), f32)
    blocks = SUB * north // east
    return pl.pallas_call(
        advect_kernel,
        grid=(levels // SUB,),
        in_specs=[
            whole(dep),
            pl.BlockSpec((FIELDS, SUB * north, east), lambda k: (0, k, 0)),
            whole(xlo), whole(xhi), whole(ylo), whole(yhi),
        ],
        out_specs=[
            pl.BlockSpec((FIELDS, north, SUB, east), lambda k: (0, 0, k, 0)), plane, plane,
        ],
        out_shape=[jax.ShapeDtypeStruct((FIELDS, north, levels, east), f32), one, one],
        scratch_shapes=[
            pltpu.VMEM((east + 2 * SUB, east), f32),
            pltpu.VMEM((east + SUB, east), f32),
            pltpu.VMEM((FIELDS, blocks, east + 3 * SUB, east), f32),
            pltpu.VMEM((blocks, east + 3 * SUB, east), f32),
            pltpu.VMEM((blocks, east + SUB, east), f32),
            pltpu.VMEM((FIELDS, north + 2 * HALO, SUB, east), f32),
            pltpu.VMEM((north + 2, SUB, east), f32),
            pltpu.VMEM((blocks, east + SUB, east), f32),
            pltpu.VMEM((blocks, east + SUB, east), f32),
            pltpu.VMEM((north + 1, SUB, east), f32),
            pltpu.VMEM((north + 1, SUB, east), f32),
            pltpu.VMEM((SUB * north, east), f32),
        ],
        compiler_params=pltpu.CompilerParams(vmem_limit_bytes=40 << 20),
        cost_estimate=pl.CostEstimate(
            flops=int(fields.size) * 130, bytes_accessed=2 * 4 * int(fields.size), transcendentals=0
        ),
    )(dep, fields.reshape(FIELDS, levels * north, east), xlo, xhi, ylo, yhi)


def shift_both(block, axis, first, last):
    count = lax.axis_size(axis)
    forward = [(i, i + 1) for i in range(count - 1)]
    backward = [(i + 1, i) for i in range(count - 1)]
    return lax.ppermute(last, axis, forward), lax.ppermute(first, axis, backward)


def advance_block(fields, dep):
    xfirst, xlast, yfirst, ylast = pack_edges(fields, dep)
    ylo, yhi = shift_both(None, "cols", yfirst, ylast)
    xlo, xhi = shift_both(None, "rows", xfirst, xlast)
    return advect(fields, dep, xlo, xhi, ylo, yhi)


AXES = ("rows", "cols")
VMEM_LIMIT = 48 << 20
TRACERS = (0, 1, 3, 4)
PARTS = 4


def dct_table(length):
    freq = np.arange(length)[:, None]
    cells = np.arange(length)[None, :]
    scale = np.where(freq == 0, np.sqrt(1.0 / length), np.sqrt(2.0 / length))
    return scale * np.cos(np.pi * (cells + 0.5) * freq / length)


def eigen_table(length):
    return 2.0 - 2.0 * np.cos(np.pi * np.arange(length) / length)


def halves(table):
    high = table.astype(jnp.bfloat16)
    low = (table - high.astype(np.float64)).astype(jnp.bfloat16)
    return high, low


def right_factor(table):
    high, low = halves(table)
    return np.block([[high, low], [high, np.zeros_like(low)]])


def left_factor(table):
    high, low = halves(table)
    return np.concatenate([high, low], 0)


class Tables:
    def __init__(self, levels, north, east, rows, cols):
        self.levels, self.north, self.east, self.rows, self.cols = levels, north, east, rows, cols
        self.count = rows * cols
        self.share = -(-levels // self.count)
        padded = self.share * self.count
        cz, cy, cx = dct_table(levels), dct_table(north), dct_table(east)
        lz, ly, lx = eigen_table(levels), eigen_table(north), eigen_table(east)
        shift = SPECTRAL_SHIFT + lz
        f32 = np.float32
        eye = np.eye(SUB)
        self.ly = [float(v) for v in ly]
        self.south = [float(v) for v in cy[:, 0]]
        self.north_edge = [float(v) for v in cy[:, -1]]
        self.base = (shift[:, None] + lx[None]).astype(f32)
        self.z_forward, self.z_back = left_factor(cz), left_factor(cz.T)
        self.y_forward = left_factor(np.kron(cy, eye))
        self.y_back = left_factor(np.kron(cy.T, eye))
        self.x_forward, self.x_back = right_factor(cx.T), right_factor(cx)
        take = np.zeros((north, east, 2 * north))
        give = np.zeros((2 * north, north, east))
        for k in range(north):
            take[k, :, k], take[k, :, north + k] = cx[:, 0], cx[:, -1]
            give[k, k], give[north + k, k] = -cx[:, -1], cx[:, 0]
        self.take = np.concatenate(halves(take.reshape(north * east, 2 * north)), 1)
        self.give = np.concatenate(halves(give.reshape(2 * north, north * east)), 0)
        lanes = max(east, 2 * north)
        assert lanes == east and cols % SUB == 0
        grid = 1.0 / (shift[:, None, None] + ly[None, :, None] + lx[None, None, :])
        alpha = np.einsum("k,myk->my", cx[:, -1] ** 2, grid)
        beta = np.einsum("k,myk->my", cx[:, -1] * cx[:, 0], grid)
        inner = rows - 1
        near = np.eye(inner, k=1) + np.eye(inner, k=-1)
        system = (1.0 + 2.0 * alpha)[..., None, None] * np.eye(inner) - beta[
            ..., None, None
        ] * near
        inverse = np.linalg.inv(system).transpose(0, 2, 3, 1).reshape(levels, inner**2, north)
        cross = np.zeros((padded, inner**2 + 1, east), f32)
        cross[:levels, : inner**2, :north] = inverse
        cross[:, inner**2] = 1.0
        cross[:levels, inner**2] = shift[:, None]
        self.cross = cross
        all_east = eigen_table(rows * east)
        grid = 1.0 / (shift[:, None, None] + ly[None, :, None] + all_east[None, None, :])
        alpha = np.einsum("y,myk->mk", cy[:, -1] ** 2, grid)
        beta = np.einsum("y,myk->mk", cy[:, -1] * cy[:, 0], grid)
        waves = np.cos(np.pi * np.arange(1, cols) / cols)
        along = np.zeros((padded, cols, rows * east), f32)
        along[:levels, : cols - 1] = 1.0 / (
            1.0 + 2.0 * alpha[:, None] - 2.0 * beta[:, None] * waves[None, :, None]
        )
        self.along = along
        order = np.arange(1, cols)
        sines = np.zeros((cols, cols))
        sines[: cols - 1, : cols - 1] = np.sqrt(2.0 / cols) * np.sin(
            np.pi * np.outer(order, order) / cols
        )
        self.sines = np.kron(np.eye(self.share), sines).astype(f32)
        wide = dct_table(rows * east).reshape(rows * east, rows, east)
        turn = np.einsum("gax,kx->gak", wide, cx).reshape(rows * east, rows * east)
        self.wide_forward = np.stack(halves(turn.T))
        self.wide_back = np.stack(halves(turn))
        both = (ly[:, None] + lx[None]).astype(f32)
        self.strip = np.stack(
            [both, np.broadcast_to(cy[:, -1:], both.shape), np.broadcast_to(cy[:, :1], both.shape)]
        ).astype(f32)
        back = np.full((east, east), 1.0)
        gain = np.zeros((east, east))
        back[:, :north] = back[:, north : 2 * north] = both.T
        gain[:, :north], gain[:, north : 2 * north] = cx[:, -1:], cx[:, :1]
        self.column = np.stack([back, gain]).astype(f32)
        lines = np.zeros((SUB, east), f32)
        lines[0], lines[1] = cx[:, -1], cx[:, 0]
        lines[2, :north] = lines[2, north : 2 * north] = cy[:, -1]
        lines[3, :north] = lines[3, north : 2 * north] = cy[:, 0]
        self.lines = lines


def parts(value):
    high = value.astype(jnp.bfloat16)
    return high, (value - high.astype(jnp.float32)).astype(jnp.bfloat16)


def mul(a, b):
    return jnp.dot(a, b, preferred_element_type=jnp.float32)


def from_left(factor, value):
    rows = factor.shape[0] // 2
    high, low = parts(value)
    both = mul(factor, high)
    return both[:rows] + (both[rows:] + mul(factor[:rows], low))


def from_right(value, factor):
    columns = factor.shape[1] // 2
    both = mul(jnp.concatenate(parts(value), 1), factor)
    return both[:, :columns] + both[:, columns:]


def times(value, high, low):
    first, second = parts(value)
    return mul(first, high) + (mul(second, high) + mul(first, low))


def vertical_change(value):
    levels = value.shape[0]
    level = lax.broadcasted_iota(jnp.int32, value.shape, 0)
    above = jnp.where(level == levels - 1, 0.0, pltpu.roll(value, levels - 1, 0))
    below = jnp.where(level == 0, 0.0, pltpu.roll(value, 1, 0))
    return 0.5 * (above - below)


def local_solve(tables, spec, base_ref, x_ref, y_ref, take_ref, coef_ref, edge_ref):
    north, east, levels = tables.north, tables.east, tables.levels
    for y in range(0, north, 4):
        tile = spec[y : y + 4].reshape(4 * levels, east)
        spec[y : y + 4] = from_right(tile, x_ref[...]).reshape(4, levels, east)
    for m in range(0, levels, SUB):
        tile = from_left(y_ref[...], spec[:, m : m + SUB, :].reshape(north * SUB, east))
        base = base_ref[m : m + SUB, :]
        even = odd = jnp.zeros((SUB, east), jnp.float32)
        for k in range(north):
            value = tile[k * SUB : (k + 1) * SUB] / (base + tables.ly[k])
            coef_ref[k, m : m + SUB, :] = value
            if k % 2:
                odd = odd + tables.south[k] * value
            else:
                even = even + tables.south[k] * value
        edge_ref[pl.ds(PARTS * m + 1, SUB, stride=PARTS), :] = even + odd
        edge_ref[pl.ds(PARTS * m + 2, SUB, stride=PARTS), :] = even - odd
    total = jnp.zeros((levels, east), jnp.float32)
    rest = total
    for k in range(north):
        high, low = parts(coef_ref[k])
        factor = take_ref[k * east : (k + 1) * east, :]
        total = total + mul(high, factor)
        rest = rest + mul(low, factor)
    lane = lax.broadcasted_iota(jnp.int32, total.shape, 1)
    total = total + pltpu.roll(total, east // 2, 1) + rest
    edge_ref[pl.ds(0, levels, stride=PARTS), :] = jnp.where(lane < 2 * north, total, 0.0)
    edge_ref[pl.ds(PARTS - 1, levels, stride=PARTS), :] = jnp.zeros_like(total)
    if edge_ref.shape[0] > levels * PARTS:
        edge_ref[levels * PARTS :, :] = jnp.zeros_like(edge_ref[levels * PARTS :, :])


def finish_solve(tables, spec, coef_ref, jump_ref, base_ref, y_ref, x_ref, z_ref, give_ref, use):
    north, east, levels = tables.north, tables.east, tables.levels
    side, ahead, behind = (
        jump_ref[pl.ds(part, levels, stride=PARTS), :] for part in range(PARTS - 1)
    )
    both = side + pltpu.roll(side, east // 2, 1)
    side_high, side_low = parts(side)
    both = both.astype(jnp.bfloat16)
    half = 2 * north
    for k in range(north):
        lanes = slice(k * east, (k + 1) * east)
        change = mul(both, give_ref[:, lanes]) + mul(side_low[:, :half], give_ref[:half, lanes])
        change = change + (tables.south[k] * behind - tables.north_edge[k] * ahead)
        spec[k] = coef_ref[k] + change / (base_ref[...] + tables.ly[k])
    for m in range(0, levels, SUB):
        tile = from_left(y_ref[...], spec[:, m : m + SUB, :].reshape(north * SUB, east))
        spec[:, m : m + SUB, :] = tile.reshape(north, SUB, east)
    for y in range(0, north, 4):
        tile = from_right(spec[y : y + 4].reshape(4 * levels, east), x_ref[...])
        tile = jnp.concatenate([tile[k * levels : (k + 1) * levels] for k in range(4)], 1)
        tile = from_left(z_ref[...], tile)
        for k in range(4):
            use(y + k, tile[:, k * east : (k + 1) * east])


def interface_kernel(
    tables, edge_ref, cross_ref, along_ref, sines_ref, forward_ref, back_ref,
    strip_ref, column_ref, lines_ref, jump_ref,
):
    rows, cols, east, north = tables.rows, tables.cols, tables.east, tables.north
    share, inner = tables.share, tables.rows - 1
    f32 = jnp.float32
    east_last, east_first = lines_ref[0:1, :], lines_ref[1:2, :]
    north_last, north_first = lines_ref[2:3, :], lines_ref[3:4, :]
    every = lax.Precision.HIGHEST

    def across(m, changes):
        result = []
        for i in range(inner):
            total = jnp.zeros((cols, east), f32)
            for j in range(inner):
                at = i * inner + j
                total = total + cross_ref[m, at : at + 1, :] * changes[j]
            result.append(total)
        return result

    gaps, steps = [], []
    for m in range(share):
        west, south, top = (
            [
                edge_ref[pl.ds((a * cols * share + m) * PARTS + part, cols, stride=share * PARTS), :]
                for a in range(rows)
            ]
            for part in range(PARTS - 1)
        )
        right = [pltpu.roll(tile, east - north, 1) for tile in west]
        gap = [right[i] - west[i + 1] for i in range(inner)]
        gaps.append(gap)
        jumps = jnp.concatenate(across(m, gap), 0)
        shift = cross_ref[m, inner**2 : inner**2 + 1, :]
        inverse = 1.0 / (strip_ref[0] + shift)
        weights = jnp.concatenate([strip_ref[1] * inverse, strip_ref[2] * inverse], 1)
        weights = jnp.concatenate([weights, jnp.zeros((east - north, 2 * east), f32)], 0)
        moved = times(jumps, *parts(weights))
        for a in range(rows):
            for side, at in ((top, 0), (south, east)):
                if a < inner:
                    side[a] = side[a] - east_last * moved[a * cols : (a + 1) * cols, at : at + east]
                if a > 0:
                    side[a] = side[a] + east_first * moved[
                        (a - 1) * cols : a * cols, at : at + east
                    ]
        steps.append(
            jnp.concatenate([top[a] - pltpu.roll(south[a], cols - 1, 0) for a in range(rows)], 1)
        )
    step = jnp.concatenate(steps, 0)
    waves = times(step, forward_ref[0], forward_ref[1])
    waves = jnp.dot(sines_ref[...], waves, precision=every, preferred_element_type=f32)
    waves = waves * jnp.concatenate([along_ref[m] for m in range(share)], 0)
    waves = jnp.dot(sines_ref[...], waves, precision=every, preferred_element_type=f32)
    step = times(waves, back_ref[0], back_ref[1])
    for m in range(share):
        shift = cross_ref[m, inner**2 : inner**2 + 1, :]
        here = step[m * cols : (m + 1) * cols]
        tall = [here[:, a * east : (a + 1) * east] for a in range(rows)]
        weights = column_ref[1] / (column_ref[0] + shift)
        moved = times(jnp.concatenate(tall, 0), *parts(weights))
        sides = []
        for a in range(rows):
            tile = moved[a * cols : (a + 1) * cols]
            sides.append(north_last * tile - north_first * pltpu.roll(tile, 1, 0))
        gap = [
            gaps[m][i] - (sides[i] - pltpu.roll(sides[i + 1], east - north, 1))
            for i in range(inner)
        ]
        jumps = across(m, gap)
        for a in range(rows):
            tile = jnp.zeros((cols, east), f32)
            if a < inner:
                tile = tile + jumps[a]
            if a > 0:
                tile = tile + pltpu.roll(jumps[a - 1], north, 1)
            out = (tile, tall[a], pltpu.roll(tall[a], 1, 0), jnp.zeros_like(tile))
            for part in range(PARTS):
                at = (a * cols * share + m) * PARTS + part
                jump_ref[pl.ds(at, cols, stride=share * PARTS), :] = out[part]


def whole_spec(array):
    shape = tuple(array.shape)
    return pl.BlockSpec(shape, lambda *_: (0,) * len(shape))


def call_params():
    return pltpu.CompilerParams(vmem_limit_bytes=VMEM_LIMIT)


def exchange(block):
    return lax.all_to_all(block, AXES, split_axis=0, concat_axis=0, tiled=True)


def interface(tables, edges):
    received = exchange(edges)
    device = lax.axis_index("rows") * lax.axis_size("cols") + lax.axis_index("cols")
    cross = lax.dynamic_slice_in_dim(tables.cross, device * tables.share, tables.share, 0)
    along = lax.dynamic_slice_in_dim(tables.along, device * tables.share, tables.share, 0)
    operands = (
        received, cross, along, tables.sines, tables.wide_forward, tables.wide_back,
        tables.strip, tables.column, tables.lines,
    )
    jumps = pl.pallas_call(
        functools.partial(interface_kernel, tables),
        in_specs=[whole_spec(a) for a in operands],
        out_specs=whole_spec(received),
        out_shape=jax.ShapeDtypeStruct(received.shape, jnp.float32),
        grid=(1,),
        compiler_params=call_params(),
    )(*operands)
    return exchange(jumps)


def adjoint_kernel(
    tables, dep_ref, cot_ref, z_ref, base_ref, x_ref, y_ref, take_ref, coef_ref, edge_ref, spec
):
    north, east, levels = tables.north, tables.east, tables.levels
    level = lax.broadcasted_iota(jnp.int32, (levels, east), 0)
    for y in range(0, north, 4):
        tiles = []
        for k in range(y, y + 4):
            value = cot_ref[0, pl.ds(k, levels, stride=north), :]
            value = jnp.where(level < dep_ref[k : k + 1, :], value, 0.0)
            tiles.append(TIME_STEP * vertical_change(value))
        tile = from_left(z_ref[...], jnp.concatenate(tiles, 1))
        for k in range(4):
            spec[y + k] = tile[:, k * east : (k + 1) * east]
    local_solve(tables, spec, base_ref, x_ref, y_ref, take_ref, coef_ref, edge_ref)


def solve_shapes(tables):
    coef = jax.ShapeDtypeStruct((tables.north, tables.levels, tables.east), jnp.float32)
    edge = jax.ShapeDtypeStruct((tables.share * tables.count * PARTS, tables.east), jnp.float32)
    return [coef, edge]


def adjoint_local(tables, cotangent, dep):
    levels, north, east = tables.levels, tables.north, tables.east
    consts = (tables.z_forward, tables.base, tables.x_forward, tables.y_forward, tables.take)
    shapes = solve_shapes(tables)
    return pl.pallas_call(
        functools.partial(adjoint_kernel, tables),
        grid=(1,),
        in_specs=[
            whole_spec(dep),
            pl.BlockSpec((1, levels * north, east), lambda k: (2, 0, 0)),
            *(whole_spec(a) for a in consts),
        ],
        out_specs=[whole_spec(a) for a in shapes],
        out_shape=shapes,
        scratch_shapes=[pltpu.VMEM(shapes[0].shape, jnp.float32)],
        compiler_params=call_params(),
    )(dep, cotangent.reshape(FIELDS, levels * north, east), *consts)


def closure(feats, w_in, bias, w_out):
    activity = jnp.tanh(mul(w_in, feats) + bias)
    hidden = activity.astype(jnp.bfloat16)
    return activity, hidden, RATE_MAX * jax.nn.sigmoid(mul(w_out, hidden))


def column_kernel(
    tables, dep_ref, adv_ref, spread_ref, wm_ref, w_in_ref, bias_ref, w_out_ref,
    z_ref, base_ref, x_ref, y_ref, take_ref,
    new_ref, coef_ref, edge_ref, spec, feats, flat,
):
    step = pl.program_id(0)
    north, east, levels = tables.north, tables.east, tables.levels
    for k in range(SUB):
        for i, f in enumerate(TRACERS):
            feats[i * levels : (i + 1) * levels, k * east : (k + 1) * east] = adv_ref[f, k].astype(
                jnp.bfloat16
            )
    _, _, rates = closure(feats[...], w_in_ref[...], bias_ref[...], w_out_ref[...])
    level = lax.broadcasted_iota(jnp.int32, (levels, east), 0)
    depths = dep_ref[pl.ds(pl.multiple_of(step * SUB, SUB), SUB), :]
    sources = []
    for k in range(SUB):
        depth = depths[k : k + 1]
        wet = level < depth
        bond = jnp.where(level + 1 < depth, TIME_STEP, 0.0)
        flow = bond * rates[:, k * east : (k + 1) * east]
        mixed = []
        for f in (3, 4):
            value = adv_ref[f, k]
            flux = flow * (pltpu.roll(value, levels - 1, 0) - value)
            value = jnp.where(wet, value + (flux - pltpu.roll(flux, 1, 0)), 0.0)
            mixed.append(value)
            flat[f, pl.ds(k, levels, stride=SUB), :] = value
        for f in (0, 1):
            flat[f, pl.ds(k, levels, stride=SUB), :] = adv_ref[f, k]
        density = THERMAL * mixed[0] - HALINE * mixed[1] - wm_ref[k] * (1.0 / TIME_STEP)
        source = vertical_change(density) - spread_ref[k] * (1.0 / TIME_STEP)
        sources.append(jnp.where(wet, source, 0.0))
    tile = from_left(z_ref[...], jnp.concatenate(sources, 1))
    for k in range(SUB):
        spec[step * SUB + k] = tile[:, k * east : (k + 1) * east]
    for f in TRACERS:
        new_ref[f] = flat[f].reshape(levels, SUB, east)

    @pl.when(step == north // SUB - 1)
    def _():
        local_solve(tables, spec, base_ref, x_ref, y_ref, take_ref, coef_ref, edge_ref)


def column(tables, dep, adv, spread, wm, w_in, bias, w_out):
    levels, north, east = tables.levels, tables.north, tables.east
    tall = lambda n: pl.BlockSpec((n, SUB, levels, east), lambda k: (0, k, 0, 0))
    plane = pl.BlockSpec((SUB, levels, east), lambda k: (k, 0, 0))
    consts = (
        w_in, bias, w_out,
        tables.z_forward, tables.base, tables.x_forward, tables.y_forward, tables.take,
    )
    shapes = solve_shapes(tables)
    return pl.pallas_call(
        functools.partial(column_kernel, tables),
        grid=(north // SUB,),
        in_specs=[whole_spec(dep), tall(FIELDS), plane, plane, *(whole_spec(a) for a in consts)],
        out_specs=[
            pl.BlockSpec((FIELDS, levels, SUB, east), lambda k: (0, 0, k, 0)),
            *(whole_spec(a) for a in shapes),
        ],
        out_shape=[jax.ShapeDtypeStruct((FIELDS, levels, north, east), jnp.float32), *shapes],
        scratch_shapes=[
            pltpu.VMEM(shapes[0].shape, jnp.float32),
            pltpu.VMEM((len(TRACERS) * levels, SUB * east), jnp.bfloat16),
            pltpu.VMEM((FIELDS, levels * SUB, east), jnp.float32),
        ],
        compiler_params=call_params(),
    )(dep, adv, spread, wm, *consts)


def back_kernel(
    tables, coef_ref, jump_ref, base_ref, y_ref, x_ref, z_ref, give_ref, back_ref, spec
):
    def use(y, tile):
        back_ref[y] = tile

    finish_solve(
        tables, spec, coef_ref, jump_ref, base_ref, y_ref, x_ref, z_ref, give_ref, use
    )


def solve_consts(tables):
    return (tables.base, tables.y_back, tables.x_back, tables.z_back, tables.give)


def back_finish(tables, coef, jumps):
    operands = (coef, jumps, *solve_consts(tables))
    return pl.pallas_call(
        functools.partial(back_kernel, tables),
        grid=(1,),
        in_specs=[whole_spec(a) for a in operands],
        out_specs=whole_spec(coef),
        out_shape=jax.ShapeDtypeStruct(coef.shape, jnp.float32),
        scratch_shapes=[pltpu.VMEM(coef.shape, jnp.float32)],
        compiler_params=call_params(),
    )(*operands)


def pressure_kernel(
    tables, dep_ref, adv_ref, new_ref, coef_ref, jump_ref, base_ref, y_ref, x_ref, z_ref, give_ref,
    pressure_ref, out_ref, spec,
):
    north, east, levels = tables.north, tables.east, tables.levels
    level = lax.broadcasted_iota(jnp.int32, (levels, east), 0)

    def use(y, tile):
        pressure_ref[pl.ds(y, levels, stride=north), :] = tile
        value = adv_ref[0, y] - TIME_STEP * vertical_change(tile)
        value = jnp.where(level < dep_ref[y : y + 1, :], value, 0.0)
        out_ref[0, pl.ds(y, levels, stride=north), :] = value

    finish_solve(
        tables, spec, coef_ref, jump_ref, base_ref, y_ref, x_ref, z_ref, give_ref, use
    )


def pressure_finish(tables, dep, adv, new, coef, jumps):
    levels, north, east = tables.levels, tables.north, tables.east
    consts = solve_consts(tables)
    flat = jax.ShapeDtypeStruct((levels * north, east), jnp.float32)
    pressure, new = pl.pallas_call(
        functools.partial(pressure_kernel, tables),
        grid=(1,),
        in_specs=[
            whole_spec(dep),
            pl.BlockSpec((1, north, levels, east), lambda k: (2, 0, 0, 0)),
            pl.BlockSpec(memory_space=pl.ANY),
            whole_spec(coef),
            whole_spec(jumps),
            *(whole_spec(a) for a in consts),
        ],
        out_specs=[
            whole_spec(flat),
            pl.BlockSpec((1, levels * north, east), lambda k: (2, 0, 0)),
        ],
        out_shape=[flat, jax.ShapeDtypeStruct((FIELDS, levels * north, east), jnp.float32)],
        input_output_aliases={2: 1},
        scratch_shapes=[pltpu.VMEM(coef.shape, jnp.float32)],
        compiler_params=call_params(),
    )(dep, adv, new.reshape(FIELDS, levels * north, east), coef, jumps, *consts)
    return pressure.reshape(levels, north, east), new.reshape(FIELDS, levels, north, east)


def gradient_kernel(
    tables, dep_ref, adv_ref, back_ref, heat_ref, salt_ref, w_in_ref, bias_ref, w_out_ref, w_ref,
    g_in_ref, g_bias_ref, g_out_ref, feats, grads, flat,
):
    step = pl.program_id(0)
    east, levels = tables.east, tables.levels
    for k in range(SUB):
        for i, f in enumerate(TRACERS):
            feats[i * levels : (i + 1) * levels, k * east : (k + 1) * east] = adv_ref[f, k].astype(
                jnp.bfloat16
            )
    activity, hidden, rates = closure(feats[...], w_in_ref[...], bias_ref[...], w_out_ref[...])
    flat[0] = heat_ref[0].reshape(levels * SUB, east)
    flat[1] = salt_ref[0].reshape(levels * SUB, east)
    level = lax.broadcasted_iota(jnp.int32, (levels, east), 0)
    depths = dep_ref[pl.ds(pl.multiple_of(step * SUB, SUB), SUB), :]
    for k in range(SUB):
        depth = depths[k : k + 1]
        wet = level < depth
        density = -vertical_change(jnp.where(wet, back_ref[k], 0.0))
        total = jnp.zeros((levels, east), jnp.float32)
        for i, f, share in ((0, 3, THERMAL), (1, 4, -HALINE)):
            value = adv_ref[f, k]
            grad = flat[i, pl.ds(k, levels, stride=SUB), :] + share * density
            grad = jnp.where(wet, grad, 0.0)
            total = total + (grad - pltpu.roll(grad, levels - 1, 0)) * (
                pltpu.roll(value, levels - 1, 0) - value
            )
        total = jnp.where(level + 1 < depth, TIME_STEP * total, 0.0)
        rate = rates[:, k * east : (k + 1) * east]
        grads[:, k * east : (k + 1) * east] = (
            total * rate * (1.0 - rate * (1.0 / RATE_MAX))
        ).astype(jnp.bfloat16)
    over = (((1,), (1,)), ((), ()))
    grad = grads[...]
    g_out = lax.dot_general(hidden, grad, over, preferred_element_type=jnp.float32)
    pre = mul(w_ref[...], grad) * (1.0 - activity * activity)
    g_in = lax.dot_general(
        feats[...], pre.astype(jnp.bfloat16), over, preferred_element_type=jnp.float32
    )
    g_bias = pre[:, :east]
    for k in range(1, SUB):
        g_bias = g_bias + pre[:, k * east : (k + 1) * east]

    @pl.when(step == 0)
    def _():
        g_in_ref[...] = g_in
        g_out_ref[...] = g_out
        g_bias_ref[...] = g_bias

    @pl.when(step > 0)
    def _():
        g_in_ref[...] += g_in
        g_out_ref[...] += g_out
        g_bias_ref[...] += g_bias


def gradients(tables, dep, adv, back, cotangent, w_in, bias, w_out, w):
    levels, north, east = tables.levels, tables.north, tables.east
    hidden, inputs = w_in.shape
    f32 = jnp.float32
    shapes = [
        jax.ShapeDtypeStruct((inputs, hidden), f32),
        jax.ShapeDtypeStruct((hidden, east), f32),
        jax.ShapeDtypeStruct((hidden, levels), f32),
    ]
    field = lambda f: pl.BlockSpec((1, levels, SUB, east), lambda k: (f, 0, k, 0))
    consts = (w_in, bias, w_out, w)
    g_in, g_bias, g_out = pl.pallas_call(
        functools.partial(gradient_kernel, tables),
        grid=(north // SUB,),
        in_specs=[
            whole_spec(dep),
            pl.BlockSpec((FIELDS, SUB, levels, east), lambda k: (0, k, 0, 0)),
            pl.BlockSpec((SUB, levels, east), lambda k: (k, 0, 0)),
            field(3),
            field(4),
            *(whole_spec(a) for a in consts),
        ],
        out_specs=[whole_spec(a) for a in shapes],
        out_shape=shapes,
        scratch_shapes=[
            pltpu.VMEM((len(TRACERS) * levels, SUB * east), jnp.bfloat16),
            pltpu.VMEM((levels, SUB * east), jnp.bfloat16),
            pltpu.VMEM((2, levels * SUB, east), f32),
        ],
        compiler_params=call_params(),
    )(dep, adv, back, cotangent, cotangent, *consts)
    return g_in, jnp.sum(g_bias, 1), g_out[:, : levels - 1]


def sum_over_mesh(parts):
    count = lax.axis_size("rows") * lax.axis_size("cols")
    flat = jnp.concatenate([part.reshape(-1) for part in parts])
    total = flat.shape[0]
    chunk = -(-total // (count * 1024)) * 1024
    flat = jnp.pad(flat, (0, chunk * count - total)).reshape(count, chunk // 128, 128)
    pieces = exchange(flat)
    summed = jnp.broadcast_to(jnp.sum(pieces, 0, keepdims=True), flat.shape)
    flat = exchange(summed).reshape(-1)
    results = []
    start = 0
    for part in parts:
        results.append(flat[start : start + part.size].reshape(part.shape))
        start += part.size
    return results


def per_device(fields, cotangent, ocean_mask, depth_levels, in_weight, in_bias, out_weight):
    _, levels, north, east = fields.shape
    tables = Tables(levels, north, east, lax.axis_size("rows"), lax.axis_size("cols"))
    dep = jnp.where(ocean_mask == 1, depth_levels, 0)
    w_in = in_weight.T
    bias = in_bias[:, None]
    w = jnp.pad(out_weight, ((0, 0), (0, levels - out_weight.shape[1])))
    w_out = w.T
    back_coef, back_edges = adjoint_local(tables, cotangent, dep)
    back_jumps = interface(tables, back_edges)
    adv, spread, wm = advance_block(fields, dep)
    new, coef, edges = column(tables, dep, adv, spread, wm, w_in, bias, w_out)
    back = back_finish(tables, back_coef, back_jumps)
    jumps = interface(tables, edges)
    grads = gradients(tables, dep, adv, back, cotangent, w_in, bias, w_out, w)
    grad_w_in, grad_b_in, grad_w_out = sum_over_mesh(grads)
    pressure, new_fields = pressure_finish(tables, dep, adv, new, coef, jumps)
    return (new_fields, pressure, grad_w_in, grad_b_in, grad_w_out)


def solution(mesh):
    in_specs = (
        P(None, None, "cols", "rows"),
        P(None, None, "cols", "rows"),
        P("cols", "rows"),
        P("cols", "rows"),
        P(),
        P(),
        P(),
    )
    out_specs = (P(None, None, "cols", "rows"), P(None, "cols", "rows"), P(), P(), P())
    return jax.shard_map(
        per_device, mesh=mesh, in_specs=in_specs, out_specs=out_specs, check_vma=False
    )
```

```python
import functools

import jax
import jax.numpy as jnp
import numpy as np
from jax import lax
from jax.experimental import pallas as pl
from jax.experimental.pallas import tpu as pltpu
from jax.sharding import PartitionSpec as P

TIME_STEP = 0.2
RATE_MAX = 2.0
THERMAL = 0.5
HALINE = 0.5
SPECTRAL_SHIFT = 0.001
WENO_EPS = 1e-06
HALO = 3
FIELDS = 5
SUB = 8


def pack_kernel(dep_ref, fields_ref, xfirst_ref, xlast_ref, yfirst_ref, ylast_ref):
    field = pl.program_id(0)
    north, east = dep_ref.shape
    levels = fields_ref.shape[1] // north
    per = east // north
    blocks = levels // per
    dep = dep_ref[...]
    tiled = jnp.concatenate([dep] * per, 0)
    level_in_block = lax.broadcasted_iota(jnp.int32, (east, east), 0) // north
    for t in range(blocks):
        block = fields_ref[0, t * east : (t + 1) * east, :]
        masked = jnp.where(level_in_block + t * per < tiled, block, 0.0)
        turned = masked.T
        row = field * blocks + t
        for s in range(HALO):
            xfirst_ref[s, pl.ds(row, 1), :] = turned[s : s + 1]
            xlast_ref[s, pl.ds(row, 1), :] = turned[east - HALO + s : east - HALO + s + 1]
    level = lax.broadcasted_iota(jnp.int32, (levels, east), 0)
    for s in range(HALO):
        at = pl.multiple_of((field * HALO + s) * levels, SUB)
        low, high = s, north - HALO + s
        first = fields_ref[0, pl.ds(low, levels, stride=north), :]
        last = fields_ref[0, pl.ds(high, levels, stride=north), :]
        yfirst_ref[pl.ds(at, levels), :] = jnp.where(level < dep[low : low + 1], first, 0.0)
        ylast_ref[pl.ds(at, levels), :] = jnp.where(level < dep[high : high + 1], last, 0.0)

    @pl.when(field == 0)
    def _():
        depths = dep.astype(jnp.float32)
        end = FIELDS * HALO * levels
        yfirst_ref[end:, :] = jnp.broadcast_to(depths[:1], (SUB, east))
        ylast_ref[end:, :] = jnp.broadcast_to(depths[north - 1 :], (SUB, east))
        turned = tiled.astype(jnp.float32).T
        for s in range(HALO):
            high = east - HALO + s
            xfirst_ref[s, FIELDS * blocks :, :] = jnp.broadcast_to(turned[s : s + 1], (SUB, east))
            xlast_ref[s, FIELDS * blocks :, :] = jnp.broadcast_to(
                turned[high : high + 1], (SUB, east)
            )


def pack_edges(fields, dep):
    _, levels, north, east = fields.shape
    rows = FIELDS * levels * north // east + SUB
    x_shape = jax.ShapeDtypeStruct((HALO, rows, east), jnp.float32)
    y_shape = jax.ShapeDtypeStruct((FIELDS * HALO * levels + SUB, east), jnp.float32)
    whole = lambda shape: pl.BlockSpec(shape.shape, lambda f: (0,) * len(shape.shape))
    return pl.pallas_call(
        pack_kernel,
        grid=(FIELDS,),
        in_specs=[
            pl.BlockSpec((north, east), lambda f: (0, 0)),
            pl.BlockSpec((1, levels * north, east), lambda f: (f, 0, 0)),
        ],
        out_specs=[whole(x_shape), whole(x_shape), whole(y_shape), whole(y_shape)],
        out_shape=[x_shape, x_shape, y_shape, y_shape],
        compiler_params=pltpu.CompilerParams(vmem_limit_bytes=VMEM_LIMIT),
    )(dep, fields.reshape(FIELDS, levels * north, east))


def face_flux(slopes, left, right, speed, share):
    dm2, dm1, d0, dp1, dp2 = slopes
    ahead = speed > 0.0
    e1 = jnp.where(ahead, dm2, dp2)
    e2 = jnp.where(ahead, dm1, dp1)
    e4 = jnp.where(ahead, dp1, dm1)
    near = jnp.where(ahead, left, right)
    bend0, bend1, bend2 = e2 - e1, d0 - e2, e4 - d0
    twice2, twice3 = e2 + e2, d0 + d0
    tilt0, tilt1, tilt2 = bend0 + twice2, e2 + d0, bend2 - twice3
    rough0 = bend0 * bend0 * (13.0 / 3.0) + (tilt0 * tilt0 + 4.0 * WENO_EPS)
    rough1 = bend1 * bend1 * (13.0 / 3.0) + (tilt1 * tilt1 + 4.0 * WENO_EPS)
    rough2 = bend2 * bend2 * (13.0 / 3.0) + (tilt2 * tilt2 + 4.0 * WENO_EPS)
    pair0, pair1, pair2 = rough1 * rough2, rough0 * rough2, rough0 * rough1
    g0, g1, g2 = pair0 * pair0, 6.0 * (pair1 * pair1), 3.0 * (pair2 * pair2)
    total = g0 * (5.0 * e2 - (e1 + e1)) + g1 * (e2 + twice3) + g2 * (4.0 * d0 - e4)
    return speed * near + share * (total * pltpu.reciprocal(g0 + g1 + g2, approx=True))


def advect_kernel(
    tracers, staged, dep_ref, *refs,
):
    field_refs, refs = refs[: len(staged)], refs[len(staged) :]
    xlo_ref, xhi_ref, ylo_ref, yhi_ref, _, adv_ref = refs[:6]
    spread_ref = refs[6] if len(tracers) > 1 else None
    (
        deep, both, lines, slopes, fluxes, cells, wets, su, su6, sv, sv6, sides,
    ) = refs[-12:]
    step = pl.program_id(0)
    north, east = dep_ref.shape
    per = east // north
    blocks = SUB // per
    all_blocks = (xlo_ref.shape[1] - SUB) // FIELDS
    levels = all_blocks * per
    depth_row = FIELDS * all_blocks
    depth_end = FIELDS * HALO * levels
    faces = range(0, east + SUB, SUB)
    first_level = step * SUB

    @pl.when(step == 0)
    def _():
        depths = dep_ref[...].astype(jnp.float32)
        deep[SUB : SUB + east, :] = jnp.concatenate([depths] * per, 0).T
        deep[SUB - 1 : SUB, :] = xlo_ref[HALO - 1, depth_row : depth_row + 1, :]
        deep[SUB + east : SUB + east + 1, :] = xhi_ref[0, depth_row : depth_row + 1, :]
        both[:east, :] = jnp.minimum(deep[SUB - 1 : SUB - 1 + east, :], deep[SUB : SUB + east, :])
        both[east : east + 1, :] = jnp.minimum(
            deep[SUB + east - 1 : SUB + east, :], deep[SUB + east : SUB + east + 1, :]
        )

    level = (lax.broadcasted_iota(jnp.int32, (SUB, east), 0) + first_level).astype(jnp.float32)
    side_level = lax.broadcasted_iota(jnp.int32, (SUB, east), 1) // north + first_level
    depths = dep_ref[...].astype(jnp.float32)
    wets[0] = (level < ylo_ref[depth_end : depth_end + 1, :]).astype(jnp.float32)
    wets[north + 1] = (level < yhi_ref[depth_end : depth_end + 1, :]).astype(jnp.float32)
    for y in range(north):
        wets[y + 1] = (level < depths[y : y + 1]).astype(jnp.float32)

    for slot, f in enumerate(staged):
        field = field_refs[slot]
        for s in range(HALO):
            at = pl.multiple_of((f * HALO + s) * levels + first_level, SUB)
            cells[slot, s] = ylo_ref[pl.ds(at, SUB), :]
            cells[slot, north + HALO + s] = yhi_ref[pl.ds(at, SUB), :]
        for y in range(north):
            cells[slot, y + HALO] = field[0, pl.ds(y, SUB, stride=north), :] * wets[y + 1]
        for b in range(blocks):
            row = f * all_blocks + step * blocks + b
            for s in range(HALO):
                lines[slot, b, SUB - HALO + s : SUB - HALO + s + 1, :] = xlo_ref[
                    s, pl.ds(row, 1), :
                ]
                lines[slot, b, SUB + east + s : SUB + east + s + 1, :] = xhi_ref[
                    s, pl.ds(row, 1), :
                ]
            turned = field[0, b * east : (b + 1) * east, :].T
            height = (side_level + b * per).astype(jnp.float32)
            for r in range(0, east, SUB):
                wet = height < deep[SUB + r : 2 * SUB + r, :]
                lines[slot, b, SUB + r : 2 * SUB + r, :] = jnp.where(
                    wet, turned[r : r + SUB], 0.0
                )

    for b in range(blocks):
        height = (side_level + b * per).astype(jnp.float32)
        for r in faces:
            speed = (0.5 * TIME_STEP) * (
                lines[0, b, SUB + r - 1 : 2 * SUB + r - 1, :] + lines[0, b, SUB + r : 2 * SUB + r, :]
            )
            speed = jnp.where(height < both[r : r + SUB, :], speed, 0.0)
            su[b, r : r + SUB, :] = speed
            su6[b, r : r + SUB, :] = jnp.abs(speed) * (1.0 / 6.0)
        if spread_ref is not None:
            change = 0.5 * (
                lines[0, b, SUB + 1 : SUB + 1 + east, :] - lines[0, b, SUB - 1 : SUB - 1 + east, :]
            )
            sides[b * east : (b + 1) * east, :] = change.T
    if spread_ref is not None:
        for y in range(north):
            spread_ref[y] = sides[pl.ds(y, SUB, stride=north), :] + 0.5 * (
                cells[1, y + HALO + 1] - cells[1, y + HALO - 1]
            )
    for y in range(north + 1):
        speed = (0.5 * TIME_STEP) * (cells[1, y + HALO - 1] + cells[1, y + HALO])
        speed = speed * (wets[y] * wets[y + 1])
        sv[y] = speed
        sv6[y] = jnp.abs(speed) * (1.0 / 6.0)

    first = len(staged) - len(tracers)

    def advance_field(f, carry):
        for b in range(blocks):
            for r in range(0, east + 2 * SUB, SUB):
                ahead = lines[f, b, r + 1 : r + 1 + SUB, :]
                slopes[b, r : r + SUB, :] = ahead - lines[f, b, r : r + SUB, :]
            for r in faces:
                at = SUB + r
                near = [slopes[b, at + k : at + k + SUB, :] for k in (-3, -2, -1, 0, 1)]
                fluxes[b, r : r + SUB, :] = face_flux(
                    near,
                    lines[f, b, at - 1 : at - 1 + SUB, :],
                    lines[f, b, at : at + SUB, :],
                    su[b, r : r + SUB, :],
                    su6[b, r : r + SUB, :],
                )
            change = fluxes[b, 0:east, :] - fluxes[b, 1 : 1 + east, :]
            sides[b * east : (b + 1) * east, :] = change.T
        line = [cells[f, k] for k in range(5)]
        inclines = [line[k + 1] - line[k] for k in range(4)]
        south = None
        for y in range(north + 1):
            line.append(cells[f, y + 2 * HALO - 1])
            inclines.append(line[-1] - line[-2])
            north_face = face_flux(inclines[-5:], line[-4], line[-3], sv[y], sv6[y])
            if y > 0:
                change = sides[pl.ds(y - 1, SUB, stride=north), :] + (south - north_face)
                adv_ref[f - first, y - 1] = wets[y] * (line[-4] + change)
            south = north_face
        return carry

    lax.fori_loop(first, len(staged), advance_field, 0)


def advect(fields, dep, tracers, edges, after):
    _, levels, north, east = fields.shape
    whole = lambda a: pl.BlockSpec(a.shape, lambda k: (0,) * a.ndim)
    staged = tracers if tracers[0] == 0 else (0, 1, *tracers)
    one = lambda f: pl.BlockSpec((1, SUB * north, east), lambda k: (f, k, 0))
    f32 = jnp.float32
    blocks = SUB * north // east
    flat = fields.reshape(FIELDS, levels * north, east)
    out_specs = [pl.BlockSpec((len(tracers), north, SUB, east), lambda k: (0, 0, k, 0))]
    out_shape = [jax.ShapeDtypeStruct((len(tracers), north, levels, east), f32)]
    if tracers[0] == 0:
        out_specs.append(pl.BlockSpec((north, SUB, east), lambda k: (0, k, 0)))
        out_shape.append(jax.ShapeDtypeStruct((north, levels, east), f32))
    return pl.pallas_call(
        functools.partial(advect_kernel, tracers, staged),
        grid=(levels // SUB,),
        in_specs=[
            whole(dep),
            *(one(f) for f in staged),
            *(whole(a) for a in edges),
            pl.BlockSpec(memory_space=pl.ANY),
        ],
        out_specs=out_specs,
        out_shape=out_shape,
        scratch_shapes=[
            pltpu.VMEM((east + 2 * SUB, east), f32),
            pltpu.VMEM((east + SUB, east), f32),
            pltpu.VMEM((len(staged), blocks, east + 3 * SUB, east), f32),
            pltpu.VMEM((blocks, east + 3 * SUB, east), f32),
            pltpu.VMEM((blocks, east + SUB, east), f32),
            pltpu.VMEM((len(staged), north + 2 * HALO, SUB, east), f32),
            pltpu.VMEM((north + 2, SUB, east), f32),
            pltpu.VMEM((blocks, east + SUB, east), f32),
            pltpu.VMEM((blocks, east + SUB, east), f32),
            pltpu.VMEM((north + 1, SUB, east), f32),
            pltpu.VMEM((north + 1, SUB, east), f32),
            pltpu.VMEM((SUB * north, east), f32),
        ],
        compiler_params=pltpu.CompilerParams(vmem_limit_bytes=VMEM_LIMIT),
    )(dep, *(flat for _ in staged), *edges, after)


def shift_both(axis, first, last):
    count = lax.axis_size(axis)
    forward = [(i, i + 1) for i in range(count - 1)]
    backward = [(i + 1, i) for i in range(count - 1)]
    return lax.ppermute(last, axis, forward), lax.ppermute(first, axis, backward)


def advance_edges(fields, dep):
    xfirst, xlast, yfirst, ylast = pack_edges(fields, dep)
    return (*shift_both("rows", xfirst, xlast), *shift_both("cols", yfirst, ylast))


AXES = ("rows", "cols")
VMEM_LIMIT = 60 << 20
TRACERS = (0, 1, 3, 4)
PARTS = 4


def dct_table(length):
    freq = np.arange(length)[:, None]
    cells = np.arange(length)[None, :]
    scale = np.where(freq == 0, np.sqrt(1.0 / length), np.sqrt(2.0 / length))
    return scale * np.cos(np.pi * (cells + 0.5) * freq / length)


def eigen_table(length):
    return 2.0 - 2.0 * np.cos(np.pi * np.arange(length) / length)


def halves(table):
    high = table.astype(jnp.bfloat16)
    low = (table - high.astype(np.float64)).astype(jnp.bfloat16)
    return high, low


def right_factor(table):
    high, low = halves(table)
    return np.block([[high, low], [high, np.zeros_like(low)]])


def left_factor(table):
    high, low = halves(table)
    return np.concatenate([high, low], 0)


class Tables:
    def __init__(self, levels, north, east, rows, cols):
        self.levels, self.north, self.east, self.rows, self.cols = levels, north, east, rows, cols
        self.count = rows * cols
        self.share = -(-levels // self.count)
        padded = self.share * self.count
        cz, cy, cx = dct_table(levels), dct_table(north), dct_table(east)
        lz, ly, lx = eigen_table(levels), eigen_table(north), eigen_table(east)
        shift = SPECTRAL_SHIFT + lz
        f32 = np.float32
        eye = np.eye(SUB)
        self.ly = [float(v) for v in ly]
        self.south = [float(v) for v in cy[:, 0]]
        self.north_edge = [float(v) for v in cy[:, -1]]
        self.base = (shift[:, None] + lx[None]).astype(f32)
        self.z_forward, self.z_back = left_factor(cz), left_factor(cz.T)
        self.y_forward = left_factor(np.kron(cy, eye))
        self.y_back = left_factor(np.kron(cy.T, eye))
        self.x_forward, self.x_back = right_factor(cx.T), right_factor(cx)
        take = np.zeros((north, east, 2 * north))
        give = np.zeros((2 * north, north, east))
        for k in range(north):
            take[k, :, k], take[k, :, north + k] = cx[:, 0], cx[:, -1]
            give[k, k], give[north + k, k] = -cx[:, -1], cx[:, 0]
        self.take = np.concatenate(halves(take.reshape(north * east, 2 * north)), 1)
        self.give = np.concatenate(halves(give.reshape(2 * north, north * east)), 0)
        lanes = max(east, 2 * north)
        assert lanes == east and cols % SUB == 0
        grid = 1.0 / (shift[:, None, None] + ly[None, :, None] + lx[None, None, :])
        alpha = np.einsum("k,myk->my", cx[:, -1] ** 2, grid)
        beta = np.einsum("k,myk->my", cx[:, -1] * cx[:, 0], grid)
        inner = rows - 1
        near = np.eye(inner, k=1) + np.eye(inner, k=-1)
        system = (1.0 + 2.0 * alpha)[..., None, None] * np.eye(inner) - beta[
            ..., None, None
        ] * near
        inverse = np.linalg.inv(system).transpose(0, 2, 3, 1).reshape(levels, inner**2, north)
        cross = np.zeros((padded, inner**2 + 1, east), f32)
        cross[:levels, : inner**2, :north] = inverse
        cross[:, inner**2] = 1.0
        cross[:levels, inner**2] = shift[:, None]
        self.cross = cross
        all_east = eigen_table(rows * east)
        grid = 1.0 / (shift[:, None, None] + ly[None, :, None] + all_east[None, None, :])
        alpha = np.einsum("y,myk->mk", cy[:, -1] ** 2, grid)
        beta = np.einsum("y,myk->mk", cy[:, -1] * cy[:, 0], grid)
        waves = np.cos(np.pi * np.arange(1, cols) / cols)
        along = np.zeros((padded, cols, rows * east), f32)
        along[:levels, : cols - 1] = 1.0 / (
            1.0 + 2.0 * alpha[:, None] - 2.0 * beta[:, None] * waves[None, :, None]
        )
        self.along = along
        order = np.arange(1, cols)
        sines = np.zeros((cols, cols))
        sines[: cols - 1, : cols - 1] = np.sqrt(2.0 / cols) * np.sin(
            np.pi * np.outer(order, order) / cols
        )
        self.sines = np.kron(np.eye(self.share), sines).astype(f32)
        wide = dct_table(rows * east).reshape(rows * east, rows, east)
        turn = np.einsum("gax,kx->gak", wide, cx).reshape(rows * east, rows * east)
        self.wide_forward = np.stack(halves(turn.T))
        self.wide_back = np.stack(halves(turn))
        both = (ly[:, None] + lx[None]).astype(f32)
        self.strip = np.stack(
            [both, np.broadcast_to(cy[:, -1:], both.shape), np.broadcast_to(cy[:, :1], both.shape)]
        ).astype(f32)
        back = np.full((east, east), 1.0)
        gain = np.zeros((east, east))
        back[:, :north] = back[:, north : 2 * north] = both.T
        gain[:, :north], gain[:, north : 2 * north] = cx[:, -1:], cx[:, :1]
        self.column = np.stack([back, gain]).astype(f32)
        lines = np.zeros((SUB, east), f32)
        lines[0], lines[1] = cx[:, -1], cx[:, 0]
        lines[2, :north] = lines[2, north : 2 * north] = cy[:, -1]
        lines[3, :north] = lines[3, north : 2 * north] = cy[:, 0]
        self.lines = lines


def parts(value):
    high = value.astype(jnp.bfloat16)
    return high, (value - high.astype(jnp.float32)).astype(jnp.bfloat16)


def mul(a, b):
    return jnp.dot(a, b, preferred_element_type=jnp.float32)


def from_left(factor, value):
    rows = factor.shape[0] // 2
    high, low = parts(value)
    both = mul(factor, high)
    return both[:rows] + (both[rows:] + mul(factor[:rows], low))


def from_right(value, factor):
    columns = factor.shape[1] // 2
    both = mul(jnp.concatenate(parts(value), 1), factor)
    return both[:, :columns] + both[:, columns:]


def times(value, high, low):
    first, second = parts(value)
    return mul(first, high) + (mul(second, high) + mul(first, low))


def vertical_change(value):
    levels = value.shape[0]
    level = lax.broadcasted_iota(jnp.int32, value.shape, 0)
    above = jnp.where(level == levels - 1, 0.0, pltpu.roll(value, levels - 1, 0))
    below = jnp.where(level == 0, 0.0, pltpu.roll(value, 1, 0))
    return 0.5 * (above - below)


def local_solve(tables, spec, base_ref, x_ref, y_ref, take_ref, coef_ref, edge_ref):
    north, east, levels = tables.north, tables.east, tables.levels
    for y in range(0, north, 4):
        tile = spec[y : y + 4].reshape(4 * levels, east)
        spec[y : y + 4] = from_right(tile, x_ref[...]).reshape(4, levels, east)
    for m in range(0, levels, SUB):
        tile = from_left(y_ref[...], spec[:, m : m + SUB, :].reshape(north * SUB, east))
        base = base_ref[m : m + SUB, :]
        even = odd = jnp.zeros((SUB, east), jnp.float32)
        for k in range(north):
            value = tile[k * SUB : (k + 1) * SUB] / (base + tables.ly[k])
            coef_ref[k, m : m + SUB, :] = value
            if k % 2:
                odd = odd + tables.south[k] * value
            else:
                even = even + tables.south[k] * value
        edge_ref[pl.ds(PARTS * m + 1, SUB, stride=PARTS), :] = even + odd
        edge_ref[pl.ds(PARTS * m + 2, SUB, stride=PARTS), :] = even - odd
    total = jnp.zeros((levels, east), jnp.float32)
    rest = total
    for k in range(north):
        high, low = parts(coef_ref[k])
        factor = take_ref[k * east : (k + 1) * east, :]
        total = total + mul(high, factor)
        rest = rest + mul(low, factor)
    lane = lax.broadcasted_iota(jnp.int32, total.shape, 1)
    total = total + pltpu.roll(total, east // 2, 1) + rest
    edge_ref[pl.ds(0, levels, stride=PARTS), :] = jnp.where(lane < 2 * north, total, 0.0)
    edge_ref[pl.ds(PARTS - 1, levels, stride=PARTS), :] = jnp.zeros_like(total)
    if edge_ref.shape[0] > levels * PARTS:
        edge_ref[levels * PARTS :, :] = jnp.zeros_like(edge_ref[levels * PARTS :, :])


def finish_solve(tables, spec, coef_ref, jump_ref, base_ref, y_ref, x_ref, z_ref, give_ref, use):
    north, east, levels = tables.north, tables.east, tables.levels
    side, ahead, behind = (
        jump_ref[pl.ds(part, levels, stride=PARTS), :] for part in range(PARTS - 1)
    )
    both = side + pltpu.roll(side, east // 2, 1)
    side_high, side_low = parts(side)
    both = both.astype(jnp.bfloat16)
    half = 2 * north
    for k in range(north):
        lanes = slice(k * east, (k + 1) * east)
        change = mul(both, give_ref[:, lanes]) + mul(side_low[:, :half], give_ref[:half, lanes])
        change = change + (tables.south[k] * behind - tables.north_edge[k] * ahead)
        spec[k] = coef_ref[k] + change / (base_ref[...] + tables.ly[k])
    for m in range(0, levels, SUB):
        tile = from_left(y_ref[...], spec[:, m : m + SUB, :].reshape(north * SUB, east))
        spec[:, m : m + SUB, :] = tile.reshape(north, SUB, east)
    for y in range(0, north, 4):
        tile = from_right(spec[y : y + 4].reshape(4 * levels, east), x_ref[...])
        tile = jnp.concatenate([tile[k * levels : (k + 1) * levels] for k in range(4)], 1)
        tile = from_left(z_ref[...], tile)
        for k in range(4):
            use(y + k, tile[:, k * east : (k + 1) * east])


def interface_kernel(
    tables, device_ref, edge_ref, cross_ref, along_ref, sines_ref, forward_ref, back_ref,
    strip_ref, column_ref, lines_ref, *rest,
):
    del device_ref
    extra_ref, jump_ref = rest
    rows, cols, east, north = tables.rows, tables.cols, tables.east, tables.north
    each = jump_ref.shape[0] // tables.count
    if each > tables.share * PARTS:
        more = extra_ref.shape[0] // tables.count
        for d in range(tables.count):
            at = d * each + tables.share * PARTS
            jump_ref[at : at + more, :] = extra_ref[d * more : (d + 1) * more, :]
    share, inner = tables.share, tables.rows - 1
    f32 = jnp.float32
    east_last, east_first = lines_ref[0:1, :], lines_ref[1:2, :]
    north_last, north_first = lines_ref[2:3, :], lines_ref[3:4, :]
    every = lax.Precision.HIGHEST

    def across(m, changes):
        result = []
        for i in range(inner):
            total = jnp.zeros((cols, east), f32)
            for j in range(inner):
                at = i * inner + j
                total = total + cross_ref[m, at : at + 1, :] * changes[j]
            result.append(total)
        return result

    gaps, steps = [], []
    for m in range(share):
        west, south, top = (
            [
                edge_ref[pl.ds((a * cols * share + m) * PARTS + part, cols, stride=share * PARTS), :]
                for a in range(rows)
            ]
            for part in range(PARTS - 1)
        )
        right = [pltpu.roll(tile, east - north, 1) for tile in west]
        gap = [right[i] - west[i + 1] for i in range(inner)]
        gaps.append(gap)
        jumps = jnp.concatenate(across(m, gap), 0)
        shift = cross_ref[m, inner**2 : inner**2 + 1, :]
        inverse = 1.0 / (strip_ref[0] + shift)
        weights = jnp.concatenate([strip_ref[1] * inverse, strip_ref[2] * inverse], 1)
        weights = jnp.concatenate([weights, jnp.zeros((east - north, 2 * east), f32)], 0)
        moved = times(jumps, *parts(weights))
        for a in range(rows):
            for side, at in ((top, 0), (south, east)):
                if a < inner:
                    side[a] = side[a] - east_last * moved[a * cols : (a + 1) * cols, at : at + east]
                if a > 0:
                    side[a] = side[a] + east_first * moved[
                        (a - 1) * cols : a * cols, at : at + east
                    ]
        steps.append(
            jnp.concatenate([top[a] - pltpu.roll(south[a], cols - 1, 0) for a in range(rows)], 1)
        )
    step = jnp.concatenate(steps, 0)
    waves = times(step, forward_ref[0], forward_ref[1])
    waves = jnp.dot(sines_ref[...], waves, precision=every, preferred_element_type=f32)
    waves = waves * jnp.concatenate([along_ref[m] for m in range(share)], 0)
    waves = jnp.dot(sines_ref[...], waves, precision=every, preferred_element_type=f32)
    step = times(waves, back_ref[0], back_ref[1])
    for m in range(share):
        shift = cross_ref[m, inner**2 : inner**2 + 1, :]
        here = step[m * cols : (m + 1) * cols]
        tall = [here[:, a * east : (a + 1) * east] for a in range(rows)]
        weights = column_ref[1] / (column_ref[0] + shift)
        moved = times(jnp.concatenate(tall, 0), *parts(weights))
        sides = []
        for a in range(rows):
            tile = moved[a * cols : (a + 1) * cols]
            sides.append(north_last * tile - north_first * pltpu.roll(tile, 1, 0))
        gap = [
            gaps[m][i] - (sides[i] - pltpu.roll(sides[i + 1], east - north, 1))
            for i in range(inner)
        ]
        jumps = across(m, gap)
        for a in range(rows):
            tile = jnp.zeros((cols, east), f32)
            if a < inner:
                tile = tile + jumps[a]
            if a > 0:
                tile = tile + pltpu.roll(jumps[a - 1], north, 1)
            out = (tile, tall[a], pltpu.roll(tall[a], 1, 0), jnp.zeros_like(tile))
            for part in range(PARTS):
                at = a * cols * each + m * PARTS + part
                jump_ref[pl.ds(at, cols, stride=each), :] = out[part]


def whole_spec(array):
    shape = tuple(array.shape)
    return pl.BlockSpec(shape, lambda *_: (0,) * len(shape))


def call_params():
    return pltpu.CompilerParams(vmem_limit_bytes=VMEM_LIMIT)


def exchange(block):
    return lax.all_to_all(block, AXES, split_axis=0, concat_axis=0, tiled=True)


def interface(tables, received, extra, travels):
    device = lax.axis_index("rows") * lax.axis_size("cols") + lax.axis_index("cols")
    operands = (
        received, tables.cross, tables.along, tables.sines, tables.wide_forward, tables.wide_back,
        tables.strip, tables.column, tables.lines,
    )
    specs = [whole_spec(a) for a in operands]
    for at in (1, 2):
        shape = (tables.share, *operands[at].shape[1:])
        specs[at] = pl.BlockSpec(shape, lambda k, mine: (mine[0], 0, 0))
    rows = received.shape[0] + (extra.shape[0] if travels else 0)
    shape = jax.ShapeDtypeStruct((rows, tables.east), jnp.float32)
    return pl.pallas_call(
        functools.partial(interface_kernel, tables),
        grid_spec=pltpu.PrefetchScalarGridSpec(
            num_scalar_prefetch=1,
            grid=(1,),
            in_specs=[
                *specs,
                whole_spec(extra) if travels else pl.BlockSpec(memory_space=pl.ANY),
            ],
            out_specs=whole_spec(shape),
        ),
        out_shape=shape,
        compiler_params=call_params(),
    )(device.astype(jnp.int32).reshape(1), *operands, extra)


def adjoint_kernel(
    tables, dep_ref, cot_ref, z_ref, base_ref, x_ref, y_ref, take_ref, *rest,
):
    coef_ref, edge_ref, spec = rest[-3:]
    north, east, levels = tables.north, tables.east, tables.levels
    level = lax.broadcasted_iota(jnp.int32, (levels, east), 0)
    for y in range(0, north, 4):
        tiles = []
        for k in range(y, y + 4):
            value = cot_ref[0, pl.ds(k, levels, stride=north), :]
            value = jnp.where(level < dep_ref[k : k + 1, :], value, 0.0)
            tiles.append(TIME_STEP * vertical_change(value))
        tile = from_left(z_ref[...], jnp.concatenate(tiles, 1))
        for k in range(4):
            spec[y + k] = tile[:, k * east : (k + 1) * east]
    local_solve(tables, spec, base_ref, x_ref, y_ref, take_ref, coef_ref, edge_ref)


def solve_shapes(tables):
    coef = jax.ShapeDtypeStruct((tables.north, tables.levels, tables.east), jnp.float32)
    edge = jax.ShapeDtypeStruct((tables.share * tables.count * PARTS, tables.east), jnp.float32)
    return [coef, edge]


def adjoint_local(tables, cotangent, dep, *after):
    levels, north, east = tables.levels, tables.north, tables.east
    consts = (tables.z_forward, tables.base, tables.x_forward, tables.y_forward, tables.take)
    shapes = solve_shapes(tables)
    return pl.pallas_call(
        functools.partial(adjoint_kernel, tables),
        grid=(1,),
        in_specs=[
            whole_spec(dep),
            pl.BlockSpec((1, levels * north, east), lambda k: (2, 0, 0)),
            *(whole_spec(a) for a in consts),
            *(pl.BlockSpec(memory_space=pl.ANY) for _ in after),
        ],
        out_specs=[whole_spec(a) for a in shapes],
        out_shape=shapes,
        scratch_shapes=[pltpu.VMEM(shapes[0].shape, jnp.float32)],
        compiler_params=call_params(),
    )(dep, cotangent.reshape(FIELDS, levels * north, east), *consts, *after)


def set_weights(w_in_ref, bias_ref, w_ref, w_in, bias, w, w_out, levels):
    inputs, width = w_in_ref.shape
    east = bias.shape[1]
    w_in[...] = w_in_ref[...].astype(jnp.float32).T.astype(jnp.bfloat16)
    bias[...] = jnp.broadcast_to(bias_ref[...], (east, width)).T
    for k in range(0, width, east):
        w[k : k + east, :] = jnp.zeros((east, east), jnp.float32)
        w[k : k + levels - 1, :] = w_ref[:, k : k + east].astype(jnp.float32)
        tile = w[k : k + east, :]
        w_out[:, k : k + east] = tile[:levels].astype(jnp.bfloat16)
        w[k : k + east, :] = tile.T


def closure(adv_ref, w_in, bias, w_out, feats, activity, hidden):
    levels, east = adv_ref.shape[2:]
    for k in range(SUB):
        for f in range(len(TRACERS)):
            feats[f * levels : (f + 1) * levels, k * east : (k + 1) * east] = adv_ref[f, k].astype(
                jnp.bfloat16
            )
    before = mul(w_in[...], feats[...])
    for k in range(SUB):
        lanes = slice(k * east, (k + 1) * east)
        value = jnp.tanh(before[:, lanes] + bias[...])
        if activity is not None:
            activity[:, lanes] = value
        hidden[:, lanes] = value.astype(jnp.bfloat16)
    return RATE_MAX * jax.nn.sigmoid(mul(w_out[...], hidden[...]))


def column_kernel(
    tables, dep_ref, adv_ref, spread_ref, w_field_ref, w_in_ref, bias_ref, w_ref,
    z_ref, base_ref, x_ref, y_ref, take_ref,
    mixed_ref, coef_ref, edge_ref,
    spec, feats, hidden, flat, w_in, bias, w, w_out,
):
    step = pl.program_id(0)
    north, east, levels = tables.north, tables.east, tables.levels

    @pl.when(step == 0)
    def _():
        set_weights(w_in_ref, bias_ref, w_ref, w_in, bias, w, w_out, levels)

    rates = closure(adv_ref, w_in, bias, w_out, feats, None, hidden)
    flat[...] = w_field_ref[0].reshape(levels * SUB, east)
    level = lax.broadcasted_iota(jnp.int32, (levels, east), 0)
    depths = dep_ref[pl.ds(pl.multiple_of(step * SUB, SUB), SUB), :]
    sources = []
    for k in range(SUB):
        lanes = slice(k * east, (k + 1) * east)
        depth = depths[k : k + 1]
        wet = level < depth
        flow = jnp.where(level + 1 < depth, TIME_STEP, 0.0) * rates[:, lanes]
        mixed = []
        for i in range(2):
            value = adv_ref[2 + i, k]
            flux = flow * (pltpu.roll(value, levels - 1, 0) - value)
            value = jnp.where(wet, value + (flux - pltpu.roll(flux, 1, 0)), 0.0)
            mixed.append(value)
            mixed_ref[i, k] = value
        rise = jnp.where(wet, flat[pl.ds(k, levels, stride=SUB), :], 0.0)
        density = THERMAL * mixed[0] - HALINE * mixed[1] - rise * (1.0 / TIME_STEP)
        source = vertical_change(density) - spread_ref[k] * (1.0 / TIME_STEP)
        sources.append(jnp.where(wet, source, 0.0))
    tile = from_left(z_ref[...], jnp.concatenate(sources, 1))
    for k in range(SUB):
        spec[step * SUB + k] = tile[:, k * east : (k + 1) * east]

    @pl.when(step == north // SUB - 1)
    def _():
        local_solve(tables, spec, base_ref, x_ref, y_ref, take_ref, coef_ref, edge_ref)


def closure_scratch(levels, east, inputs, hidden):
    f32, bf16 = jnp.float32, jnp.bfloat16
    return [
        pltpu.VMEM((hidden, inputs), bf16),
        pltpu.VMEM((hidden, east), f32),
        pltpu.VMEM((hidden, east), f32),
        pltpu.VMEM((levels, hidden), bf16),
    ]


def column(tables, dep, adv, spread, fields, in_weight, in_bias, out_weight):
    levels, north, east = tables.levels, tables.north, tables.east
    inputs, hidden = in_weight.shape
    f32, bf16 = jnp.float32, jnp.bfloat16
    consts = (
        in_weight, in_bias, out_weight,
        tables.z_forward, tables.base, tables.x_forward, tables.y_forward, tables.take,
    )
    mixed = jax.ShapeDtypeStruct((2, north, levels, east), f32)
    shapes = solve_shapes(tables)
    lanes = SUB * east
    return pl.pallas_call(
        functools.partial(column_kernel, tables),
        grid=(north // SUB,),
        in_specs=[
            whole_spec(dep),
            pl.BlockSpec((len(TRACERS), SUB, levels, east), lambda k: (0, k, 0, 0)),
            pl.BlockSpec((SUB, levels, east), lambda k: (k, 0, 0)),
            pl.BlockSpec((1, levels, SUB, east), lambda k: (2, 0, k, 0)),
            *(whole_spec(a) for a in consts),
        ],
        out_specs=[
            pl.BlockSpec((2, SUB, levels, east), lambda k: (0, k, 0, 0)),
            *(whole_spec(a) for a in shapes),
        ],
        out_shape=[mixed, *shapes],
        scratch_shapes=[
            pltpu.VMEM(shapes[0].shape, f32),
            pltpu.VMEM((inputs, lanes), bf16),
            pltpu.VMEM((hidden, lanes), bf16),
            pltpu.VMEM((levels * SUB, east), f32),
            *closure_scratch(levels, east, inputs, hidden),
        ],
        compiler_params=call_params(),
    )(dep, adv, spread, fields, *consts)


def gradient_kernel(
    tables, dep_ref, adv_ref, heat_ref, salt_ref, w_in_ref, bias_ref, w_ref,
    coef_ref, jump_ref, base_ref, y_ref, x_ref, z_ref, give_ref, after_ref,
    total_ref,
    spec, back, feats, activity, hidden, grads, cots, w_in, bias, w, w_out,
    g_in_ref, g_bias_ref, g_out_ref,
):
    del after_ref
    step = pl.program_id(0)
    north, east, levels = tables.north, tables.east, tables.levels
    f32, bf16 = jnp.float32, jnp.bfloat16

    @pl.when(step == 0)
    def _():
        set_weights(w_in_ref, bias_ref, w_ref, w_in, bias, w, w_out, levels)
        g_in_ref[...] = jnp.zeros_like(g_in_ref)
        g_out_ref[...] = jnp.zeros_like(g_out_ref)
        g_bias_ref[...] = jnp.zeros_like(g_bias_ref)

        def use(y, tile):
            back[y] = tile

        finish_solve(
            tables, spec, coef_ref, jump_ref, base_ref, y_ref, x_ref, z_ref, give_ref, use
        )

    rates = closure(adv_ref, w_in, bias, w_out, feats, activity, hidden)
    cots[0] = heat_ref[0].reshape(levels * SUB, east)
    cots[1] = salt_ref[0].reshape(levels * SUB, east)
    level = lax.broadcasted_iota(jnp.int32, (levels, east), 0)
    depths = dep_ref[pl.ds(pl.multiple_of(step * SUB, SUB), SUB), :]
    for k in range(SUB):
        lanes = slice(k * east, (k + 1) * east)
        depth = depths[k : k + 1]
        wet = level < depth
        rate = rates[:, lanes]
        flow = jnp.where(level + 1 < depth, TIME_STEP, 0.0) * rate
        slope = -vertical_change(jnp.where(wet, back[step * SUB + k], 0.0))
        total = jnp.zeros((levels, east), f32)
        for i, share in ((0, THERMAL), (1, -HALINE)):
            value = adv_ref[2 + i, k]
            drop = pltpu.roll(value, levels - 1, 0) - value
            grad = cots[i, pl.ds(k, levels, stride=SUB), :] + share * slope
            grad = jnp.where(wet, grad, 0.0)
            total = total + (grad - pltpu.roll(grad, levels - 1, 0)) * drop
        grads[:, lanes] = (total * flow * (1.0 - rate * (1.0 / RATE_MAX))).astype(bf16)
    over = (((1,), (1,)), ((), ()))
    grad = grads[...]
    g_out_ref[...] += lax.dot_general(hidden[...], grad, over, preferred_element_type=f32)
    pre = mul(w[:, :levels].astype(bf16), grad)
    for k in range(SUB):
        lanes = slice(k * east, (k + 1) * east)
        value = activity[:, lanes]
        value = pre[:, lanes] * (1.0 - value * value)
        g_bias_ref[...] += value
        hidden[:, lanes] = value.astype(bf16)
    g_in_ref[...] += lax.dot_general(feats[...], hidden[...], over, preferred_element_type=f32)

    @pl.when(step == north // SUB - 1)
    def _():
        inputs, width = g_in_ref.shape
        for k in range(width // east):
            total_ref[k * inputs : (k + 1) * inputs, :] = g_in_ref[:, k * east : (k + 1) * east]
        sums = jnp.sum(g_bias_ref[...], 1, keepdims=True)
        last = jnp.concatenate([g_out_ref[...], jnp.broadcast_to(sums, g_out_ref.shape)], 1)
        at = inputs * width // east
        for k in range(0, width, east):
            total_ref[at + k : at + k + east, :] = last[k : k + east].T


def gradients(tables, dep, adv, cotangent, in_weight, in_bias, out_weight, coef, jumps, after):
    levels, north, east = tables.levels, tables.north, tables.east
    inputs, hidden = in_weight.shape
    f32, bf16 = jnp.float32, jnp.bfloat16
    field = lambda f: pl.BlockSpec((1, levels, SUB, east), lambda k: (f, 0, k, 0))
    consts = (in_weight, in_bias, out_weight, coef, jumps, *solve_consts(tables))
    rows = inputs * hidden // east + hidden
    assert 2 * levels == east
    total = jax.ShapeDtypeStruct((-(-rows // tables.count) * tables.count, east), f32)
    lanes = SUB * east
    return pl.pallas_call(
        functools.partial(gradient_kernel, tables),
        grid=(north // SUB,),
        in_specs=[
            whole_spec(dep),
            pl.BlockSpec((len(TRACERS), SUB, levels, east), lambda k: (0, k, 0, 0)),
            field(3),
            field(4),
            *(whole_spec(a) for a in consts),
            pl.BlockSpec(memory_space=pl.ANY),
        ],
        out_specs=whole_spec(total),
        out_shape=total,
        scratch_shapes=[
            pltpu.VMEM(coef.shape, f32),
            pltpu.VMEM(coef.shape, f32),
            pltpu.VMEM((inputs, lanes), bf16),
            pltpu.VMEM((hidden, lanes), f32),
            pltpu.VMEM((hidden, lanes), bf16),
            pltpu.VMEM((levels, lanes), bf16),
            pltpu.VMEM((2, levels * SUB, east), f32),
            *closure_scratch(levels, east, inputs, hidden),
            pltpu.VMEM((inputs, hidden), f32),
            pltpu.VMEM((hidden, east), f32),
            pltpu.VMEM((hidden, levels), f32),
        ],
        compiler_params=call_params(),
    )(dep, adv, cotangent, cotangent, *consts, after)


def gather_kernel(adv_ref, mixed_ref, after_ref, new_ref, flat):
    del after_ref
    levels, east = adv_ref.shape[2:]
    for f, (ref, i) in zip(TRACERS, ((adv_ref, 0), (adv_ref, 1), (mixed_ref, 0), (mixed_ref, 1))):
        for k in range(SUB):
            flat[f, pl.ds(k, levels, stride=SUB), :] = ref[i, k]
        new_ref[f] = flat[f].reshape(levels, SUB, east)


def gather_fields(adv, mixed, after):
    _, north, levels, east = adv.shape
    block = pl.BlockSpec((2, SUB, levels, east), lambda k: (0, k, 0, 0))
    return pl.pallas_call(
        gather_kernel,
        grid=(north // SUB,),
        in_specs=[block, block, pl.BlockSpec(memory_space=pl.ANY)],
        out_specs=pl.BlockSpec((FIELDS, levels, SUB, east), lambda k: (0, 0, k, 0)),
        out_shape=jax.ShapeDtypeStruct((FIELDS, levels, north, east), jnp.float32),
        scratch_shapes=[pltpu.VMEM((FIELDS, levels * SUB, east), jnp.float32)],
        compiler_params=call_params(),
    )(adv, mixed, after)


def solve_consts(tables):
    return (tables.base, tables.y_back, tables.x_back, tables.z_back, tables.give)


def pressure_kernel(
    tables, dep_ref, w_ref, new_ref, coef_ref, jump_ref, base_ref, y_ref, x_ref, z_ref, give_ref,
    pressure_ref, out_ref, spec, jumps,
):
    north, east, levels = tables.north, tables.east, tables.levels
    mine = tables.share * PARTS
    each = jump_ref.shape[0] // tables.count
    for part in range(mine):
        jumps[pl.ds(part, tables.count, stride=mine), :] = jump_ref[
            pl.ds(part, tables.count, stride=each), :
        ]
    level = lax.broadcasted_iota(jnp.int32, (levels, east), 0)

    def use(y, tile):
        pressure_ref[pl.ds(y, levels, stride=north), :] = tile
        value = w_ref[0, y] - TIME_STEP * vertical_change(tile)
        value = jnp.where(level < dep_ref[y : y + 1, :], value, 0.0)
        out_ref[0, pl.ds(y, levels, stride=north), :] = value

    finish_solve(
        tables, spec, coef_ref, jumps, base_ref, y_ref, x_ref, z_ref, give_ref, use
    )


def pressure_finish(tables, dep, w, new, coef, jumps):
    levels, north, east = tables.levels, tables.north, tables.east
    consts = solve_consts(tables)
    flat = jax.ShapeDtypeStruct((levels * north, east), jnp.float32)
    pressure, new = pl.pallas_call(
        functools.partial(pressure_kernel, tables),
        grid=(1,),
        in_specs=[
            whole_spec(dep),
            whole_spec(w),
            pl.BlockSpec(memory_space=pl.ANY),
            whole_spec(coef),
            whole_spec(jumps),
            *(whole_spec(a) for a in consts),
        ],
        out_specs=[
            whole_spec(flat),
            pl.BlockSpec((1, levels * north, east), lambda k: (2, 0, 0)),
        ],
        out_shape=[flat, jax.ShapeDtypeStruct((FIELDS, levels * north, east), jnp.float32)],
        input_output_aliases={2: 1},
        scratch_shapes=[
            pltpu.VMEM(coef.shape, jnp.float32),
            pltpu.VMEM((tables.share * tables.count * PARTS, east), jnp.float32),
        ],
        compiler_params=call_params(),
    )(dep, w, new.reshape(FIELDS, levels * north, east), coef, jumps, *consts)
    return pressure.reshape(levels, north, east), new.reshape(FIELDS, levels, north, east)


def sum_kernel(count, skip, pieces_ref, *rest):
    out_ref = rest[-1]
    each = pieces_ref.shape[0] // count
    more = each - skip
    total = pieces_ref[skip:each, :]
    for d in range(1, count):
        total = total + pieces_ref[d * each + skip : (d + 1) * each, :]
    for d in range(count):
        out_ref[d * more : (d + 1) * more, :] = total


def sum_pieces(tables, received, *after):
    skip = tables.share * PARTS
    rows = received.shape[0] - skip * tables.count
    shape = jax.ShapeDtypeStruct((rows, tables.east), jnp.float32)
    return pl.pallas_call(
        functools.partial(sum_kernel, tables.count, skip),
        grid=(1,),
        in_specs=[whole_spec(received), *(pl.BlockSpec(memory_space=pl.ANY) for _ in after)],
        out_specs=whole_spec(shape),
        out_shape=shape,
        compiler_params=call_params(),
    )(received, *after)


def split_kernel(sums_ref, in_ref, bias_ref, out_ref):
    inputs, width = in_ref.shape
    east = sums_ref.shape[1]
    wide = inputs * width // east
    for k in range(width // east):
        lanes = slice(k * east, (k + 1) * east)
        in_ref[:, lanes] = sums_ref[k * inputs : (k + 1) * inputs, :]
        at = wide + k * east
        out_ref[:, lanes] = sums_ref[at : at + out_ref.shape[0], :]
        bias_ref[:, lanes] = sums_ref[at + east // 2 : at + east // 2 + 1, :]


def split_sums(sums, inputs, hidden, outputs):
    shapes = [
        jax.ShapeDtypeStruct(shape, jnp.float32)
        for shape in ((inputs, hidden), (1, hidden), (outputs, hidden))
    ]
    g_in, g_bias, g_out = pl.pallas_call(
        split_kernel,
        grid=(1,),
        in_specs=[whole_spec(sums)],
        out_specs=[whole_spec(a) for a in shapes],
        out_shape=shapes,
        compiler_params=call_params(),
    )(sums)
    return g_in, g_bias.reshape(hidden), g_out.T


def per_device(fields, cotangent, ocean_mask, depth_levels, in_weight, in_bias, out_weight):
    _, levels, north, east = fields.shape
    tables = Tables(levels, north, east, lax.axis_size("rows"), lax.axis_size("cols"))
    dep = jnp.where(ocean_mask == 1, depth_levels, 0)
    inputs, hidden = in_weight.shape
    outputs = out_weight.shape[1]
    in_bias = in_bias.reshape(1, hidden)
    out_weight = out_weight.T
    edges = advance_edges(fields, dep)
    back_coef, back_edges = adjoint_local(tables, cotangent, dep, edges[0], edges[1])
    adv, spread = advect(fields, dep, TRACERS, edges, edges[0])
    back_jumps = exchange(interface(tables, exchange(back_edges), adv, False))
    mixed, coef, sides = column(tables, dep, adv, spread, fields, in_weight, in_bias, out_weight)
    received = exchange(sides)
    grads = gradients(
        tables, dep, adv, cotangent, in_weight, in_bias, out_weight, back_coef, back_jumps, coef
    )
    jumps_out = interface(tables, received, grads, True)
    jumps = exchange(jumps_out)
    w = advect(fields, dep, (2,), edges, jumps_out)[0]
    new = gather_fields(adv, mixed, jumps_out)
    sums = exchange(sum_pieces(tables, jumps, w, new))
    pressure, new_fields = pressure_finish(tables, dep, w, new, coef, jumps)
    return (new_fields, pressure, *split_sums(sums, inputs, hidden, outputs))


def solution(mesh):
    in_specs = (
        P(None, None, "cols", "rows"),
        P(None, None, "cols", "rows"),
        P("cols", "rows"),
        P("cols", "rows"),
        P(),
        P(),
        P(),
    )
    out_specs = (P(None, None, "cols", "rows"), P(None, "cols", "rows"), P(), P(), P())
    return jax.shard_map(
        per_device, mesh=mesh, in_specs=in_specs, out_specs=out_specs, check_vma=False
    )
```

```python
import functools

import jax
import jax.numpy as jnp
import numpy as np
from jax import lax
from jax.experimental import pallas as pl
from jax.experimental.pallas import tpu as pltpu
from jax.sharding import PartitionSpec as P

TIME_STEP = 0.2
RATE_MAX = 2.0
THERMAL = 0.5
HALINE = 0.5
SPECTRAL_SHIFT = 0.001
WENO_EPS = 1e-06
HALO = 3
FIELDS = 5
SUB = 8


def pack_kernel(mask_ref, depth_ref, fields_ref, dep_ref, xfirst_ref, xlast_ref, yfirst_ref, ylast_ref):
    field = pl.program_id(0)
    north, east = dep_ref.shape
    levels = fields_ref.shape[1] // north
    per = east // north
    blocks = levels // per
    dep = jnp.where(mask_ref[...] == 1, depth_ref[...], 0)
    dep_ref[...] = dep
    tiled = jnp.concatenate([dep] * per, 0)
    level_in_block = lax.broadcasted_iota(jnp.int32, (east, east), 0) // north
    for t in range(blocks):
        block = fields_ref[0, t * east : (t + 1) * east, :]
        masked = jnp.where(level_in_block + t * per < tiled, block, 0.0)
        turned = masked.T
        row = field * blocks + t
        for s in range(HALO):
            xfirst_ref[s, pl.ds(row, 1), :] = turned[s : s + 1]
            xlast_ref[s, pl.ds(row, 1), :] = turned[east - HALO + s : east - HALO + s + 1]
    level = lax.broadcasted_iota(jnp.int32, (levels, east), 0)
    for s in range(HALO):
        at = pl.multiple_of((field * HALO + s) * levels, SUB)
        low, high = s, north - HALO + s
        first = fields_ref[0, pl.ds(low, levels, stride=north), :]
        last = fields_ref[0, pl.ds(high, levels, stride=north), :]
        yfirst_ref[pl.ds(at, levels), :] = jnp.where(level < dep[low : low + 1], first, 0.0)
        ylast_ref[pl.ds(at, levels), :] = jnp.where(level < dep[high : high + 1], last, 0.0)

    @pl.when(field == 0)
    def _():
        depths = dep.astype(jnp.float32)
        end = FIELDS * HALO * levels
        yfirst_ref[end:, :] = jnp.broadcast_to(depths[:1], (SUB, east))
        ylast_ref[end:, :] = jnp.broadcast_to(depths[north - 1 :], (SUB, east))
        turned = tiled.astype(jnp.float32).T
        for s in range(HALO):
            high = east - HALO + s
            xfirst_ref[s, FIELDS * blocks :, :] = jnp.broadcast_to(turned[s : s + 1], (SUB, east))
            xlast_ref[s, FIELDS * blocks :, :] = jnp.broadcast_to(
                turned[high : high + 1], (SUB, east)
            )


def pack_edges(fields, mask, depth):
    _, levels, north, east = fields.shape
    rows = FIELDS * levels * north // east + SUB
    x_shape = jax.ShapeDtypeStruct((HALO, rows, east), jnp.float32)
    y_shape = jax.ShapeDtypeStruct((FIELDS * HALO * levels + SUB, east), jnp.float32)
    whole = lambda shape: pl.BlockSpec(shape.shape, lambda f: (0,) * len(shape.shape))
    return pl.pallas_call(
        pack_kernel,
        grid=(FIELDS,),
        in_specs=[
            whole(mask),
            whole(depth),
            pl.BlockSpec((1, levels * north, east), lambda f: (f, 0, 0)),
        ],
        out_specs=[whole(mask), whole(x_shape), whole(x_shape), whole(y_shape), whole(y_shape)],
        out_shape=[jax.ShapeDtypeStruct(mask.shape, jnp.int32), x_shape, x_shape, y_shape, y_shape],
        compiler_params=pltpu.CompilerParams(vmem_limit_bytes=52 << 20),
    )(mask, depth, fields.reshape(FIELDS, levels * north, east))


def face_flux(slopes, left, right, speed, share):
    dm2, dm1, d0, dp1, dp2 = slopes
    ahead = speed > 0.0
    e1 = jnp.where(ahead, dm2, dp2)
    e2 = jnp.where(ahead, dm1, dp1)
    e4 = jnp.where(ahead, dp1, dm1)
    near = jnp.where(ahead, left, right)
    bend0, bend1, bend2 = e2 - e1, d0 - e2, e4 - d0
    tilt0, tilt1, tilt2 = bend0 + (e2 + e2), e2 + d0, bend2 - (d0 + d0)
    rough0 = bend0 * bend0 * (13.0 / 3.0) + (tilt0 * tilt0 + 4.0 * WENO_EPS)
    rough1 = bend1 * bend1 * (13.0 / 3.0) + (tilt1 * tilt1 + 4.0 * WENO_EPS)
    rough2 = bend2 * bend2 * (13.0 / 3.0) + (tilt2 * tilt2 + 4.0 * WENO_EPS)
    pair0, pair1, pair2 = rough1 * rough2, rough0 * rough2, rough0 * rough1
    g0, g1, g2 = pair0 * pair0, 6.0 * (pair1 * pair1), 3.0 * (pair2 * pair2)
    total = g0 * (tilt0 + (bend0 + e2)) + g1 * (tilt1 + d0) + g2 * (d0 - tilt2)
    return speed * near + share * (total * pltpu.reciprocal(g0 + g1 + g2, approx=True))


def advect_kernel(
    tracers, staged, begin, filled, dep_ref, *refs,
):
    field_refs, refs = refs[: len(staged)], refs[len(staged) :]
    xlo_ref, xhi_ref, ylo_ref, yhi_ref = refs[:4]
    refs = refs[5 + filled :]
    adv_ref = refs[0]
    spread_ref = refs[1] if len(tracers) > 1 else None
    (
        deep, both, lines, slopes, fluxes, cells, wets, su, su6, sv, sv6, sides,
    ) = refs[-12:]
    step = pl.program_id(0) + begin
    north, east = dep_ref.shape
    per = east // north
    blocks = SUB // per
    all_blocks = (xlo_ref.shape[1] - SUB) // FIELDS
    levels = all_blocks * per
    depth_row = FIELDS * all_blocks
    depth_end = FIELDS * HALO * levels
    faces = range(0, east + SUB, SUB)
    first_level = step * SUB

    @pl.when(step == begin)
    def _():
        depths = dep_ref[...].astype(jnp.float32)
        deep[SUB : SUB + east, :] = jnp.concatenate([depths] * per, 0).T
        deep[SUB - 1 : SUB, :] = xlo_ref[HALO - 1, depth_row : depth_row + 1, :]
        deep[SUB + east : SUB + east + 1, :] = xhi_ref[0, depth_row : depth_row + 1, :]
        both[:east, :] = jnp.minimum(deep[SUB - 1 : SUB - 1 + east, :], deep[SUB : SUB + east, :])
        both[east : east + 1, :] = jnp.minimum(
            deep[SUB + east - 1 : SUB + east, :], deep[SUB + east : SUB + east + 1, :]
        )

    level = (lax.broadcasted_iota(jnp.int32, (SUB, east), 0) + first_level).astype(jnp.float32)
    side_level = lax.broadcasted_iota(jnp.int32, (SUB, east), 1) // north + first_level
    depths = dep_ref[...].astype(jnp.float32)
    wets[0] = (level < ylo_ref[depth_end : depth_end + 1, :]).astype(jnp.float32)
    wets[north + 1] = (level < yhi_ref[depth_end : depth_end + 1, :]).astype(jnp.float32)
    for y in range(north):
        wets[y + 1] = (level < depths[y : y + 1]).astype(jnp.float32)

    for slot, f in enumerate(staged):
        field = field_refs[slot]
        for s in range(HALO):
            at = pl.multiple_of((f * HALO + s) * levels + first_level, SUB)
            cells[slot, s] = ylo_ref[pl.ds(at, SUB), :]
            cells[slot, north + HALO + s] = yhi_ref[pl.ds(at, SUB), :]
        for y in range(north):
            cells[slot, y + HALO] = field[0, pl.ds(y, SUB, stride=north), :] * wets[y + 1]
        for b in range(blocks):
            row = f * all_blocks + step * blocks + b
            for s in range(HALO):
                lines[slot, b, SUB - HALO + s : SUB - HALO + s + 1, :] = xlo_ref[
                    s, pl.ds(row, 1), :
                ]
                lines[slot, b, SUB + east + s : SUB + east + s + 1, :] = xhi_ref[
                    s, pl.ds(row, 1), :
                ]
            turned = field[0, b * east : (b + 1) * east, :].T
            height = (side_level + b * per).astype(jnp.float32)
            for r in range(0, east, SUB):
                wet = height < deep[SUB + r : 2 * SUB + r, :]
                lines[slot, b, SUB + r : 2 * SUB + r, :] = jnp.where(
                    wet, turned[r : r + SUB], 0.0
                )

    for b in range(blocks):
        height = (side_level + b * per).astype(jnp.float32)
        for r in faces:
            speed = (0.5 * TIME_STEP) * (
                lines[0, b, SUB + r - 1 : 2 * SUB + r - 1, :] + lines[0, b, SUB + r : 2 * SUB + r, :]
            )
            speed = jnp.where(height < both[r : r + SUB, :], speed, 0.0)
            su[b, r : r + SUB, :] = speed
            su6[b, r : r + SUB, :] = jnp.abs(speed) * (1.0 / 6.0)
        if spread_ref is not None:
            change = 0.5 * (
                lines[0, b, SUB + 1 : SUB + 1 + east, :] - lines[0, b, SUB - 1 : SUB - 1 + east, :]
            )
            sides[b * east : (b + 1) * east, :] = change.T
    if spread_ref is not None:
        for y in range(north):
            spread_ref[y] = sides[pl.ds(y, SUB, stride=north), :] + 0.5 * (
                cells[1, y + HALO + 1] - cells[1, y + HALO - 1]
            )
    for y in range(north + 1):
        speed = (0.5 * TIME_STEP) * (cells[1, y + HALO - 1] + cells[1, y + HALO])
        speed = speed * (wets[y] * wets[y + 1])
        sv[y] = speed
        sv6[y] = jnp.abs(speed) * (1.0 / 6.0)

    first = len(staged) - len(tracers)

    def advance_field(f, carry):
        for b in range(blocks):
            for r in range(0, east + 2 * SUB, SUB):
                ahead = lines[f, b, r + 1 : r + 1 + SUB, :]
                slopes[b, r : r + SUB, :] = ahead - lines[f, b, r : r + SUB, :]
            for r in faces:
                at = SUB + r
                near = [slopes[b, at + k : at + k + SUB, :] for k in (-3, -2, -1, 0, 1)]
                fluxes[b, r : r + SUB, :] = face_flux(
                    near,
                    lines[f, b, at - 1 : at - 1 + SUB, :],
                    lines[f, b, at : at + SUB, :],
                    su[b, r : r + SUB, :],
                    su6[b, r : r + SUB, :],
                )
            change = fluxes[b, 0:east, :] - fluxes[b, 1 : 1 + east, :]
            sides[b * east : (b + 1) * east, :] = change.T
        line = [cells[f, k] for k in range(5)]
        inclines = [line[k + 1] - line[k] for k in range(4)]
        south = None
        for y in range(north + 1):
            line.append(cells[f, y + 2 * HALO - 1])
            inclines.append(line[-1] - line[-2])
            north_face = face_flux(inclines[-5:], line[-4], line[-3], sv[y], sv6[y])
            if y > 0:
                change = sides[pl.ds(y - 1, SUB, stride=north), :] + (south - north_face)
                adv_ref[f - first, y - 1] = wets[y] * (line[-4] + change)
            south = north_face
        return carry

    lax.fori_loop(first, len(staged), advance_field, 0)


def advect(fields, dep, tracers, edges, span, after, filled=()):
    _, levels, north, east = fields.shape
    whole = lambda a: pl.BlockSpec(a.shape, lambda k: (0,) * a.ndim)
    staged = tracers if tracers[0] == 0 else (0, 1, *tracers)
    one = lambda f: pl.BlockSpec((1, SUB * north, east), lambda k: (f, k + span[0], 0))
    f32 = jnp.float32
    blocks = SUB * north // east
    flat = fields.reshape(FIELDS, levels * north, east)
    out_specs = [pl.BlockSpec((len(tracers), north, SUB, east), lambda k: (0, 0, k + span[0], 0))]
    out_shape = [jax.ShapeDtypeStruct((len(tracers), north, levels, east), f32)]
    if tracers[0] == 0:
        out_specs.append(pl.BlockSpec((north, SUB, east), lambda k: (0, k + span[0], 0)))
        out_shape.append(jax.ShapeDtypeStruct((north, levels, east), f32))
    return pl.pallas_call(
        functools.partial(advect_kernel, tracers, staged, span[0], len(filled)),
        grid=(span[1] - span[0],),
        in_specs=[
            whole(dep),
            *(one(f) for f in staged),
            *(whole(a) for a in edges),
            pl.BlockSpec(memory_space=pl.ANY),
            *(pl.BlockSpec(memory_space=pl.ANY) for _ in filled),
        ],
        out_specs=out_specs,
        out_shape=out_shape,
        input_output_aliases={len(staged) + 6 + i: i for i in range(len(filled))},
        scratch_shapes=[
            pltpu.VMEM((east + 2 * SUB, east), f32),
            pltpu.VMEM((east + SUB, east), f32),
            pltpu.VMEM((len(staged), blocks, east + 3 * SUB, east), f32),
            pltpu.VMEM((blocks, east + 3 * SUB, east), f32),
            pltpu.VMEM((blocks, east + SUB, east), f32),
            pltpu.VMEM((len(staged), north + 2 * HALO, SUB, east), f32),
            pltpu.VMEM((north + 2, SUB, east), f32),
            pltpu.VMEM((blocks, east + SUB, east), f32),
            pltpu.VMEM((blocks, east + SUB, east), f32),
            pltpu.VMEM((north + 1, SUB, east), f32),
            pltpu.VMEM((north + 1, SUB, east), f32),
            pltpu.VMEM((SUB * north, east), f32),
        ],
        compiler_params=pltpu.CompilerParams(vmem_limit_bytes=VMEM_LIMIT),
    )(dep, *(flat for _ in staged), *edges, after, *filled)


def shift_both(axis, first, last):
    count = lax.axis_size(axis)
    forward = [(i, i + 1) for i in range(count - 1)]
    backward = [(i + 1, i) for i in range(count - 1)]
    return lax.ppermute(last, axis, forward), lax.ppermute(first, axis, backward)


def advance_edges(fields, mask, depth):
    dep, xfirst, xlast, yfirst, ylast = pack_edges(fields, mask, depth)
    south_north = shift_both("cols", yfirst, ylast)
    return (dep, *shift_both("rows", xfirst, xlast), *south_north)


AXES = ("rows", "cols")
VMEM_LIMIT = 52 << 20
TRACERS = (0, 1, 3, 4)
PARTS = 4


def dct_table(length):
    freq = np.arange(length)[:, None]
    cells = np.arange(length)[None, :]
    scale = np.where(freq == 0, np.sqrt(1.0 / length), np.sqrt(2.0 / length))
    return scale * np.cos(np.pi * (cells + 0.5) * freq / length)


def eigen_table(length):
    return 2.0 - 2.0 * np.cos(np.pi * np.arange(length) / length)


def halves(table):
    high = table.astype(jnp.bfloat16)
    low = (table - high.astype(np.float64)).astype(jnp.bfloat16)
    return high, low


def right_factor(table):
    high, low = halves(table)
    return np.block([[high, low], [high, np.zeros_like(low)]])


def left_factor(table):
    high, low = halves(table)
    return np.concatenate([high, low], 0)


class Tables:
    def __init__(self, levels, north, east, rows, cols):
        self.levels, self.north, self.east, self.rows, self.cols = levels, north, east, rows, cols
        self.count = rows * cols
        self.share = -(-levels // self.count)
        padded = self.share * self.count
        cz, cy, cx = dct_table(levels), dct_table(north), dct_table(east)
        lz, ly, lx = eigen_table(levels), eigen_table(north), eigen_table(east)
        shift = SPECTRAL_SHIFT + lz
        f32 = np.float32
        eye = np.eye(SUB)
        self.ly = [float(v) for v in ly]
        self.south = [float(v) for v in cy[:, 0]]
        self.north_edge = [float(v) for v in cy[:, -1]]
        self.base = (shift[:, None] + lx[None]).astype(f32)
        self.z_forward, self.z_back = left_factor(cz), left_factor(cz.T)
        self.y_forward = left_factor(np.kron(cy, eye))
        self.y_back = left_factor(np.kron(cy.T, eye))
        self.x_forward, self.x_back = right_factor(cx.T), right_factor(cx)
        edges = np.zeros((2 * north, east))
        edges[:north], edges[north:] = cx[:, 0], cx[:, -1]
        self.take = np.concatenate(halves(edges.T), 1)
        edges[:north], edges[north:] = -cx[:, -1], cx[:, 0]
        give = np.concatenate(halves(edges), 0)
        self.give = np.concatenate([give, give], 0)
        assert 4 * north == east
        lanes = max(east, 2 * north)
        assert lanes == east and cols % SUB == 0
        grid = 1.0 / (shift[:, None, None] + ly[None, :, None] + lx[None, None, :])
        alpha = np.einsum("k,myk->my", cx[:, -1] ** 2, grid)
        beta = np.einsum("k,myk->my", cx[:, -1] * cx[:, 0], grid)
        inner = rows - 1
        near = np.eye(inner, k=1) + np.eye(inner, k=-1)
        system = (1.0 + 2.0 * alpha)[..., None, None] * np.eye(inner) - beta[
            ..., None, None
        ] * near
        inverse = np.linalg.inv(system).transpose(0, 2, 3, 1).reshape(levels, inner**2, north)
        cross = np.zeros((padded, inner**2 + 1, east), f32)
        cross[:levels, : inner**2, :north] = inverse
        cross[:, inner**2] = 1.0
        cross[:levels, inner**2] = shift[:, None]
        self.cross = cross
        all_east = eigen_table(rows * east)
        grid = 1.0 / (shift[:, None, None] + ly[None, :, None] + all_east[None, None, :])
        alpha = np.einsum("y,myk->mk", cy[:, -1] ** 2, grid)
        beta = np.einsum("y,myk->mk", cy[:, -1] * cy[:, 0], grid)
        waves = np.cos(np.pi * np.arange(1, cols) / cols)
        along = np.zeros((padded, cols, rows * east), f32)
        along[:levels, : cols - 1] = 1.0 / (
            1.0 + 2.0 * alpha[:, None] - 2.0 * beta[:, None] * waves[None, :, None]
        )
        self.along = along
        order = np.arange(1, cols)
        sines = np.zeros((cols, cols))
        sines[: cols - 1, : cols - 1] = np.sqrt(2.0 / cols) * np.sin(
            np.pi * np.outer(order, order) / cols
        )
        self.sines = np.kron(np.eye(self.share), sines).astype(f32)
        wide = dct_table(rows * east).reshape(rows * east, rows, east)
        turn = np.einsum("gax,kx->gak", wide, cx).reshape(rows * east, rows * east)
        self.wide_forward = np.stack(halves(turn.T))
        self.wide_back = np.stack(halves(turn))
        both = (ly[:, None] + lx[None]).astype(f32)
        self.strip = np.stack(
            [both, np.broadcast_to(cy[:, -1:], both.shape), np.broadcast_to(cy[:, :1], both.shape)]
        ).astype(f32)
        back = np.full((east, east), 1.0)
        gain = np.zeros((east, east))
        back[:, :north] = back[:, north : 2 * north] = both.T
        gain[:, :north], gain[:, north : 2 * north] = cx[:, -1:], cx[:, :1]
        self.column = np.stack([back, gain]).astype(f32)
        lines = np.zeros((SUB, east), f32)
        lines[0], lines[1] = cx[:, -1], cx[:, 0]
        lines[2, :north] = lines[2, north : 2 * north] = cy[:, -1]
        lines[3, :north] = lines[3, north : 2 * north] = cy[:, 0]
        self.lines = lines


def parts(value):
    high = value.astype(jnp.bfloat16)
    return high, (value - high.astype(jnp.float32)).astype(jnp.bfloat16)


def mul(a, b):
    return jnp.dot(a, b, preferred_element_type=jnp.float32)


def from_left(factor, value):
    rows = factor.shape[0] // 2
    high, low = parts(value)
    both = mul(factor, high)
    return both[:rows] + (both[rows:] + mul(factor[:rows], low))


def from_right(value, factor):
    columns = factor.shape[1] // 2
    both = mul(jnp.concatenate(parts(value), 1), factor)
    return both[:, :columns] + both[:, columns:]


def times(value, high, low):
    first, second = parts(value)
    return mul(first, high) + (mul(second, high) + mul(first, low))


def vertical_change(value):
    levels = value.shape[0]
    level = lax.broadcasted_iota(jnp.int32, value.shape, 0)
    above = jnp.where(level == levels - 1, 0.0, pltpu.roll(value, levels - 1, 0))
    below = jnp.where(level == 0, 0.0, pltpu.roll(value, 1, 0))
    return 0.5 * (above - below)


def pair_of(spec, m, rows):
    return jnp.concatenate(
        [spec[:, at : at + SUB, :].reshape(rows, -1) for at in (m, m + SUB)], 1
    )


def block_solve(tables, spec, base_ref, x_ref, y_ref, coef_ref):
    north, east, levels = tables.north, tables.east, tables.levels
    for y in range(0, north, 4):
        tile = spec[y : y + 4].reshape(4 * levels, east)
        spec[y : y + 4] = from_right(tile, x_ref[...]).reshape(4, levels, east)
    for m in range(0, levels, 2 * SUB):
        both = from_left(y_ref[...], pair_of(spec, m, north * SUB))
        for i in range(2):
            at = m + i * SUB
            base = base_ref[at : at + SUB, :]
            tile = both[:, i * east : (i + 1) * east]
            for k in range(north):
                coef_ref[k, at : at + SUB, :] = tile[k * SUB : (k + 1) * SUB] / (
                    base + tables.ly[k]
                )


def block_edges(tables, coef_ref, take_ref, edge_ref):
    north, east, levels = tables.north, tables.east, tables.levels
    zero = jnp.zeros((levels, east), jnp.float32)
    even = odd = total = rest = zero
    lane = lax.broadcasted_iota(jnp.int32, (levels, east), 1)
    place = lane % north
    for k in range(0, north, 4):
        group = coef_ref[k : k + 4]
        high, low = parts(group.reshape(4 * levels, east))
        high, low = mul(high, take_ref[...]), mul(low, take_ref[...])
        for i in range(4):
            value = tables.south[k + i] * group[i]
            if i % 2:
                odd = odd + value
            else:
                even = even + value
            mine = place == k + i
            total = total + jnp.where(mine, high[i * levels : (i + 1) * levels], 0.0)
            rest = rest + jnp.where(mine, low[i * levels : (i + 1) * levels], 0.0)
    total = total + pltpu.roll(total, east // 2, 1) + rest
    sides = (jnp.where(lane < 2 * north, total, 0.0), even + odd, even - odd, zero)
    for part in range(PARTS):
        edge_ref[pl.ds(part, levels, stride=PARTS), :] = sides[part]
    if edge_ref.shape[0] > levels * PARTS:
        edge_ref[levels * PARTS :, :] = jnp.zeros_like(edge_ref[levels * PARTS :, :])


def finish_solve(tables, spec, coef_ref, jump_ref, base_ref, y_ref, x_ref, z_ref, give_ref, use):
    north, east, levels = tables.north, tables.east, tables.levels
    side, ahead, behind = (
        jump_ref[pl.ds(part, levels, stride=PARTS), :] for part in range(PARTS - 1)
    )
    high, low = (half.astype(jnp.float32) for half in parts(side))
    sides = jnp.concatenate([high + pltpu.roll(high, east // 2, 1), low], 1)
    place = lax.broadcasted_iota(jnp.int32, sides.shape, 1) % north
    for k in range(0, north, 4):
        picked = [jnp.where(place == k + i, sides, 0.0).astype(jnp.bfloat16) for i in range(4)]
        change = mul(jnp.concatenate(picked, 0), give_ref[...])
        for i in range(4):
            value = change[i * levels : (i + 1) * levels] + (
                tables.south[k + i] * behind - tables.north_edge[k + i] * ahead
            )
            spec[k + i] = coef_ref[k + i] + value / (base_ref[...] + tables.ly[k + i])
    for m in range(0, levels, 2 * SUB):
        both = from_left(y_ref[...], pair_of(spec, m, north * SUB))
        for i in range(2):
            at = m + i * SUB
            tile = both[:, i * east : (i + 1) * east]
            spec[:, at : at + SUB, :] = tile.reshape(north, SUB, east)
    for y in range(0, north, 4):
        tile = from_right(spec[y : y + 4].reshape(4 * levels, east), x_ref[...])
        tile = jnp.concatenate([tile[k * levels : (k + 1) * levels] for k in range(4)], 1)
        tile = from_left(z_ref[...], tile)
        for k in range(4):
            use(y + k, tile[:, k * east : (k + 1) * east])


def interface_kernel(
    tables, device_ref, edge_ref, cross_ref, along_ref, sines_ref, forward_ref, back_ref,
    strip_ref, column_ref, lines_ref, *rest,
):
    del device_ref
    extra_ref, jump_ref = rest[0], rest[-1]
    rows, cols, east, north = tables.rows, tables.cols, tables.east, tables.north
    each = jump_ref.shape[0] // tables.count
    every_in = edge_ref.shape[0] // tables.count
    if each > tables.share * PARTS:
        more = extra_ref.shape[0] // tables.count
        for d in range(tables.count):
            at = d * each + tables.share * PARTS
            jump_ref[at : at + more, :] = extra_ref[d * more : (d + 1) * more, :]
    share, inner = tables.share, tables.rows - 1
    f32 = jnp.float32
    east_last, east_first = lines_ref[0:1, :], lines_ref[1:2, :]
    north_last, north_first = lines_ref[2:3, :], lines_ref[3:4, :]
    every = lax.Precision.HIGHEST

    def across(m, changes):
        result = []
        for i in range(inner):
            total = jnp.zeros((cols, east), f32)
            for j in range(inner):
                at = i * inner + j
                total = total + cross_ref[m, at : at + 1, :] * changes[j]
            result.append(total)
        return result

    gaps, steps = [], []
    for m in range(share):
        west, south, top = (
            [
                edge_ref[pl.ds(a * cols * every_in + m * PARTS + part, cols, stride=every_in), :]
                for a in range(rows)
            ]
            for part in range(PARTS - 1)
        )
        right = [pltpu.roll(tile, east - north, 1) for tile in west]
        gap = [right[i] - west[i + 1] for i in range(inner)]
        gaps.append(gap)
        jumps = jnp.concatenate(across(m, gap), 0)
        shift = cross_ref[m, inner**2 : inner**2 + 1, :]
        inverse = 1.0 / (strip_ref[0] + shift)
        weights = jnp.concatenate([strip_ref[1] * inverse, strip_ref[2] * inverse], 1)
        weights = jnp.concatenate([weights, jnp.zeros((east - north, 2 * east), f32)], 0)
        moved = times(jumps, *parts(weights))
        for a in range(rows):
            for side, at in ((top, 0), (south, east)):
                if a < inner:
                    side[a] = side[a] - east_last * moved[a * cols : (a + 1) * cols, at : at + east]
                if a > 0:
                    side[a] = side[a] + east_first * moved[
                        (a - 1) * cols : a * cols, at : at + east
                    ]
        steps.append(
            jnp.concatenate([top[a] - pltpu.roll(south[a], cols - 1, 0) for a in range(rows)], 1)
        )
    step = jnp.concatenate(steps, 0)
    waves = times(step, forward_ref[0], forward_ref[1])
    waves = jnp.dot(sines_ref[...], waves, precision=every, preferred_element_type=f32)
    waves = waves * jnp.concatenate([along_ref[m] for m in range(share)], 0)
    waves = jnp.dot(sines_ref[...], waves, precision=every, preferred_element_type=f32)
    step = times(waves, back_ref[0], back_ref[1])
    for m in range(share):
        shift = cross_ref[m, inner**2 : inner**2 + 1, :]
        here = step[m * cols : (m + 1) * cols]
        tall = [here[:, a * east : (a + 1) * east] for a in range(rows)]
        weights = column_ref[1] / (column_ref[0] + shift)
        moved = times(jnp.concatenate(tall, 0), *parts(weights))
        sides = []
        for a in range(rows):
            tile = moved[a * cols : (a + 1) * cols]
            sides.append(north_last * tile - north_first * pltpu.roll(tile, 1, 0))
        gap = [
            gaps[m][i] - (sides[i] - pltpu.roll(sides[i + 1], east - north, 1))
            for i in range(inner)
        ]
        jumps = across(m, gap)
        for a in range(rows):
            tile = jnp.zeros((cols, east), f32)
            if a < inner:
                tile = tile + jumps[a]
            if a > 0:
                tile = tile + pltpu.roll(jumps[a - 1], north, 1)
            out = (tile, tall[a], pltpu.roll(tall[a], 1, 0), jnp.zeros_like(tile))
            for part in range(PARTS):
                at = a * cols * each + m * PARTS + part
                jump_ref[pl.ds(at, cols, stride=each), :] = out[part]


def whole_spec(array):
    shape = tuple(array.shape)
    return pl.BlockSpec(shape, lambda *_: (0,) * len(shape))


def call_params(limit=VMEM_LIMIT):
    return pltpu.CompilerParams(vmem_limit_bytes=limit)


def exchange(block):
    return lax.all_to_all(block, AXES, split_axis=0, concat_axis=0, tiled=True)


def interface(tables, received, extra, travels, limit, *after):
    device = lax.axis_index("rows") * lax.axis_size("cols") + lax.axis_index("cols")
    operands = (
        received, tables.cross, tables.along, tables.sines, tables.wide_forward, tables.wide_back,
        tables.strip, tables.column, tables.lines,
    )
    specs = [whole_spec(a) for a in operands]
    for at in (1, 2):
        shape = (tables.share, *operands[at].shape[1:])
        specs[at] = pl.BlockSpec(shape, lambda k, mine: (mine[0], 0, 0))
    rows = received.shape[0] + (extra.shape[0] if travels else 0)
    shape = jax.ShapeDtypeStruct((rows, tables.east), jnp.float32)
    return pl.pallas_call(
        functools.partial(interface_kernel, tables),
        grid_spec=pltpu.PrefetchScalarGridSpec(
            num_scalar_prefetch=1,
            grid=(1,),
            in_specs=[
                *specs,
                whole_spec(extra) if travels else pl.BlockSpec(memory_space=pl.ANY),
                *(pl.BlockSpec(memory_space=pl.ANY) for _ in after),
            ],
            out_specs=whole_spec(shape),
        ),
        out_shape=shape,
        compiler_params=call_params(limit),
    )(device.astype(jnp.int32).reshape(1), *operands, extra, *after)


def adjoint_kernel(
    tables, dep_ref, cot_ref, z_ref, base_ref, x_ref, y_ref, coef_ref, spec
):
    north, east, levels = tables.north, tables.east, tables.levels
    level = lax.broadcasted_iota(jnp.int32, (levels, east), 0)
    for y in range(0, north, 4):
        tiles = []
        for k in range(y, y + 4):
            value = cot_ref[0, pl.ds(k, levels, stride=north), :]
            value = jnp.where(level < dep_ref[k : k + 1, :], value, 0.0)
            tiles.append(TIME_STEP * vertical_change(value))
        tile = from_left(z_ref[...], jnp.concatenate(tiles, 1))
        for k in range(4):
            spec[y + k] = tile[:, k * east : (k + 1) * east]
    block_solve(tables, spec, base_ref, x_ref, y_ref, coef_ref)


def solve_shapes(tables):
    coef = jax.ShapeDtypeStruct((tables.north, tables.levels, tables.east), jnp.float32)
    edge = jax.ShapeDtypeStruct((tables.share * tables.count * PARTS, tables.east), jnp.float32)
    return [coef, edge]


def adjoint_local(tables, cotangent, dep):
    levels, north, east = tables.levels, tables.north, tables.east
    consts = (tables.z_forward, tables.base, tables.x_forward, tables.y_forward)
    coef = solve_shapes(tables)[0]
    return pl.pallas_call(
        functools.partial(adjoint_kernel, tables),
        grid=(1,),
        in_specs=[
            whole_spec(dep),
            pl.BlockSpec((1, levels * north, east), lambda k: (2, 0, 0)),
            *(whole_spec(a) for a in consts),
        ],
        out_specs=whole_spec(coef),
        out_shape=coef,
        scratch_shapes=[pltpu.VMEM(coef.shape, jnp.float32)],
        compiler_params=call_params(52 << 20),
    )(dep, cotangent.reshape(FIELDS, levels * north, east), *consts)


def edges_kernel(tables, coef_ref, take_ref, *rest):
    block_edges(tables, coef_ref, take_ref, rest[-1])


def adjoint_edges(tables, coef, *after):
    edge = solve_shapes(tables)[1]
    return pl.pallas_call(
        functools.partial(edges_kernel, tables),
        grid=(1,),
        in_specs=[
            whole_spec(coef),
            whole_spec(tables.take),
            *(pl.BlockSpec(memory_space=pl.ANY) for _ in after),
        ],
        out_specs=whole_spec(edge),
        out_shape=edge,
        compiler_params=call_params(),
    )(coef, tables.take, *after)


def set_weights(w_in_ref, bias_ref, w_ref, w_in, bias, w, w_out, levels):
    inputs, width = w_in_ref.shape
    east = bias.shape[1]
    w_in[...] = w_in_ref[...].astype(jnp.float32).T.astype(jnp.bfloat16)
    bias[...] = jnp.broadcast_to(bias_ref[...], (east, width)).T
    for k in range(0, width, east):
        w[k : k + east, :] = jnp.zeros((east, east), jnp.float32)
        w[k : k + levels - 1, :] = w_ref[:, k : k + east].astype(jnp.float32)
        tile = w[k : k + east, :]
        w_out[:, k : k + east] = tile[:levels].astype(jnp.bfloat16)
        w[k : k + east, :] = tile.T


def closure(adv_ref, w_in, bias, w_out, feats, activity, hidden):
    levels, east = adv_ref.shape[2:]
    for k in range(SUB):
        for f in range(len(TRACERS)):
            feats[f * levels : (f + 1) * levels, k * east : (k + 1) * east] = adv_ref[f, k].astype(
                jnp.bfloat16
            )
    before = mul(w_in[...], feats[...])
    for k in range(SUB):
        lanes = slice(k * east, (k + 1) * east)
        value = jnp.tanh(before[:, lanes] + bias[...])
        if activity is not None:
            activity[:, lanes] = value
        hidden[:, lanes] = value.astype(jnp.bfloat16)
    return RATE_MAX * jax.nn.sigmoid(mul(w_out[...], hidden[...]))


def column_kernel(
    tables, dep_ref, adv_ref, spread_ref, w_field_ref, heat_ref, salt_ref,
    w_in_ref, bias_ref, w_ref, back_coef_ref, back_jump_ref,
    z_ref, base_ref, x_ref, y_ref, take_ref, y_back_ref, x_back_ref, z_back_ref, give_ref,
    mixed_ref, coef_ref, sides, total_ref,
    spec, back, feats, activity, hidden, grads, flat,
    w_in, bias, w, w_out, g_in_ref, g_bias_ref, g_out_ref,
):
    step = pl.program_id(0)
    north, east, levels = tables.north, tables.east, tables.levels
    f32, bf16 = jnp.float32, jnp.bfloat16

    @pl.when(step == 0)
    def _():
        set_weights(w_in_ref, bias_ref, w_ref, w_in, bias, w, w_out, levels)
        g_in_ref[...] = jnp.zeros_like(g_in_ref)
        g_out_ref[...] = jnp.zeros_like(g_out_ref)
        g_bias_ref[...] = jnp.zeros_like(g_bias_ref)

        def use(y, tile):
            back[y] = tile

        finish_solve(
            tables, spec, back_coef_ref, back_jump_ref, base_ref, y_back_ref, x_back_ref,
            z_back_ref, give_ref, use,
        )

    rates = closure(adv_ref, w_in, bias, w_out, feats, activity, hidden)
    for i, ref in enumerate((heat_ref, salt_ref, w_field_ref)):
        flat[i] = ref[0].reshape(levels * SUB, east)
    level = lax.broadcasted_iota(jnp.int32, (levels, east), 0)
    depths = dep_ref[pl.ds(pl.multiple_of(step * SUB, SUB), SUB), :]
    sources = []
    for k in range(SUB):
        lanes = slice(k * east, (k + 1) * east)
        depth = depths[k : k + 1]
        wet = level < depth
        rate = rates[:, lanes]
        flow = jnp.where(level + 1 < depth, TIME_STEP, 0.0) * rate
        slope = -vertical_change(jnp.where(wet, back[step * SUB + k], 0.0))
        mixed = []
        total = jnp.zeros((levels, east), f32)
        for i, share in ((0, THERMAL), (1, -HALINE)):
            value = adv_ref[2 + i, k]
            drop = pltpu.roll(value, levels - 1, 0) - value
            grad = flat[i, pl.ds(k, levels, stride=SUB), :] + share * slope
            grad = jnp.where(wet, grad, 0.0)
            total = total + (grad - pltpu.roll(grad, levels - 1, 0)) * drop
            flux = flow * drop
            value = jnp.where(wet, value + (flux - pltpu.roll(flux, 1, 0)), 0.0)
            mixed.append(value)
            mixed_ref[i, k] = value
        grads[:, lanes] = (total * flow * (1.0 - rate * (1.0 / RATE_MAX))).astype(bf16)
        rise = jnp.where(wet, flat[2, pl.ds(k, levels, stride=SUB), :], 0.0)
        density = THERMAL * mixed[0] - HALINE * mixed[1] - rise * (1.0 / TIME_STEP)
        source = vertical_change(density) - spread_ref[k] * (1.0 / TIME_STEP)
        sources.append(jnp.where(wet, source, 0.0))
    tile = from_left(z_ref[...], jnp.concatenate(sources, 1))
    for k in range(SUB):
        spec[step * SUB + k] = tile[:, k * east : (k + 1) * east]

    over = (((1,), (1,)), ((), ()))
    grad = grads[...]
    g_out_ref[...] += lax.dot_general(hidden[...], grad, over, preferred_element_type=f32)
    pre = mul(w[:, :levels].astype(bf16), grad)
    for k in range(SUB):
        lanes = slice(k * east, (k + 1) * east)
        value = activity[:, lanes]
        value = pre[:, lanes] * (1.0 - value * value)
        g_bias_ref[...] += value
        hidden[:, lanes] = value.astype(bf16)
    g_in_ref[...] += lax.dot_general(feats[...], hidden[...], over, preferred_element_type=f32)

    @pl.when(step == north // SUB - 1)
    def _():
        block_solve(tables, spec, base_ref, x_ref, y_ref, coef_ref)
        block_edges(tables, coef_ref, take_ref, sides)
        inputs, width = g_in_ref.shape
        for k in range(width // east):
            total_ref[k * inputs : (k + 1) * inputs, :] = g_in_ref[:, k * east : (k + 1) * east]
        sums = jnp.sum(g_bias_ref[...], 1, keepdims=True)
        last = jnp.concatenate([g_out_ref[...], jnp.broadcast_to(sums, g_out_ref.shape)], 1)
        at = inputs * width // east
        for k in range(0, width, east):
            total_ref[at + k : at + k + east, :] = last[k : k + east].T
        if total_ref.shape[0] > at + width:
            total_ref[at + width :, :] = jnp.zeros_like(total_ref[at + width :, :])


def column(
    tables, dep, adv, spread, fields, cotangent, in_weight, in_bias, out_weight, coef, jumps
):
    levels, north, east = tables.levels, tables.north, tables.east
    inputs, hidden = in_weight.shape
    f32, bf16 = jnp.float32, jnp.bfloat16
    consts = (
        in_weight, in_bias, out_weight, coef, jumps,
        tables.z_forward, tables.base, tables.x_forward, tables.y_forward, tables.take,
        tables.y_back, tables.x_back, tables.z_back, tables.give,
    )
    mixed = jax.ShapeDtypeStruct((2, north, levels, east), f32)
    coef, edge = solve_shapes(tables)
    rows = inputs * hidden // east + hidden
    assert 2 * levels == east
    rows = -(-rows // tables.count) * tables.count
    total = jax.ShapeDtypeStruct((rows, east), f32)
    lanes = SUB * east
    field = lambda f: pl.BlockSpec((1, levels, SUB, east), lambda k: (f, 0, k, 0))
    return pl.pallas_call(
        functools.partial(column_kernel, tables),
        grid=(north // SUB,),
        in_specs=[
            whole_spec(dep),
            pl.BlockSpec((len(TRACERS), SUB, levels, east), lambda k: (0, k, 0, 0)),
            pl.BlockSpec((SUB, levels, east), lambda k: (k, 0, 0)),
            field(2),
            field(3),
            field(4),
            *(whole_spec(a) for a in consts),
        ],
        out_specs=[
            pl.BlockSpec((2, SUB, levels, east), lambda k: (0, k, 0, 0)),
            whole_spec(coef),
            whole_spec(edge),
            whole_spec(total),
        ],
        out_shape=[mixed, coef, edge, total],
        scratch_shapes=[
            pltpu.VMEM(coef.shape, f32),
            pltpu.VMEM(coef.shape, f32),
            pltpu.VMEM((inputs, lanes), bf16),
            pltpu.VMEM((hidden, lanes), f32),
            pltpu.VMEM((hidden, lanes), bf16),
            pltpu.VMEM((levels, lanes), bf16),
            pltpu.VMEM((3, levels * SUB, east), f32),
            pltpu.VMEM((hidden, inputs), bf16),
            pltpu.VMEM((hidden, east), f32),
            pltpu.VMEM((hidden, east), f32),
            pltpu.VMEM((levels, hidden), bf16),
            pltpu.VMEM((inputs, hidden), f32),
            pltpu.VMEM((hidden, east), f32),
            pltpu.VMEM((hidden, levels), f32),
        ],
        compiler_params=call_params(),
    )(dep, adv, spread, fields, cotangent, cotangent, *consts)


def gather_kernel(adv_ref, mixed_ref, after_ref, new_ref, flat):
    del after_ref
    levels, east = adv_ref.shape[2:]
    for f, (ref, i) in zip(TRACERS, ((adv_ref, 0), (adv_ref, 1), (mixed_ref, 0), (mixed_ref, 1))):
        for k in range(SUB):
            flat[f, pl.ds(k, levels, stride=SUB), :] = ref[i, k]
        new_ref[f] = flat[f].reshape(levels, SUB, east)


def gather_fields(adv, mixed, after):
    _, north, levels, east = adv.shape
    block = pl.BlockSpec((2, SUB, levels, east), lambda k: (0, k, 0, 0))
    return pl.pallas_call(
        gather_kernel,
        grid=(north // SUB,),
        in_specs=[block, block, pl.BlockSpec(memory_space=pl.ANY)],
        out_specs=pl.BlockSpec((FIELDS, levels, SUB, east), lambda k: (0, 0, k, 0)),
        out_shape=jax.ShapeDtypeStruct((FIELDS, levels, north, east), jnp.float32),
        scratch_shapes=[pltpu.VMEM((FIELDS, levels * SUB, east), jnp.float32)],
        compiler_params=call_params(),
    )(adv, mixed, after)


def solve_consts(tables):
    return (tables.base, tables.y_back, tables.x_back, tables.z_back, tables.give)


def pressure_kernel(
    tables, dep_ref, w_ref, new_ref, coef_ref, jump_ref, base_ref, y_ref, x_ref, z_ref, give_ref,
    pressure_ref, out_ref, spec, jumps,
):
    north, east, levels = tables.north, tables.east, tables.levels
    mine = tables.share * PARTS
    each = jump_ref.shape[0] // tables.count
    for part in range(mine):
        jumps[pl.ds(part, tables.count, stride=mine), :] = jump_ref[
            pl.ds(part, tables.count, stride=each), :
        ]
    level = lax.broadcasted_iota(jnp.int32, (levels, east), 0)

    def use(y, tile):
        pressure_ref[pl.ds(y, levels, stride=north), :] = tile
        value = w_ref[0, y] - TIME_STEP * vertical_change(tile)
        value = jnp.where(level < dep_ref[y : y + 1, :], value, 0.0)
        out_ref[0, pl.ds(y, levels, stride=north), :] = value

    finish_solve(
        tables, spec, coef_ref, jumps, base_ref, y_ref, x_ref, z_ref, give_ref, use
    )


def pressure_finish(tables, dep, w, new, coef, jumps):
    levels, north, east = tables.levels, tables.north, tables.east
    consts = solve_consts(tables)
    flat = jax.ShapeDtypeStruct((levels * north, east), jnp.float32)
    pressure, new = pl.pallas_call(
        functools.partial(pressure_kernel, tables),
        grid=(1,),
        in_specs=[
            whole_spec(dep),
            whole_spec(w),
            pl.BlockSpec(memory_space=pl.ANY),
            whole_spec(coef),
            whole_spec(jumps),
            *(whole_spec(a) for a in consts),
        ],
        out_specs=[
            whole_spec(flat),
            pl.BlockSpec((1, levels * north, east), lambda k: (2, 0, 0)),
        ],
        out_shape=[flat, jax.ShapeDtypeStruct((FIELDS, levels * north, east), jnp.float32)],
        input_output_aliases={2: 1},
        scratch_shapes=[
            pltpu.VMEM(coef.shape, jnp.float32),
            pltpu.VMEM((tables.share * tables.count * PARTS, east), jnp.float32),
        ],
        compiler_params=call_params(),
    )(dep, w, new.reshape(FIELDS, levels * north, east), coef, jumps, *consts)
    return pressure.reshape(levels, north, east), new.reshape(FIELDS, levels, north, east)


def sum_kernel(count, skip, pieces_ref, *rest):
    out_ref = rest[-1]
    each = pieces_ref.shape[0] // count
    more = each - skip
    total = pieces_ref[skip:each, :]
    for d in range(1, count):
        total = total + pieces_ref[d * each + skip : (d + 1) * each, :]
    for d in range(count):
        out_ref[d * more : (d + 1) * more, :] = total


def sum_pieces(tables, received, *after):
    skip = tables.share * PARTS
    rows = received.shape[0] - skip * tables.count
    shape = jax.ShapeDtypeStruct((rows, tables.east), jnp.float32)
    return pl.pallas_call(
        functools.partial(sum_kernel, tables.count, skip),
        grid=(1,),
        in_specs=[whole_spec(received), *(pl.BlockSpec(memory_space=pl.ANY) for _ in after)],
        out_specs=whole_spec(shape),
        out_shape=shape,
        compiler_params=call_params(),
    )(received, *after)


def split_kernel(sums_ref, in_ref, bias_ref, out_ref):
    inputs, width = in_ref.shape
    east = sums_ref.shape[1]
    wide = inputs * width // east
    for k in range(width // east):
        lanes = slice(k * east, (k + 1) * east)
        in_ref[:, lanes] = sums_ref[k * inputs : (k + 1) * inputs, :]
        at = wide + k * east
        out_ref[:, lanes] = sums_ref[at : at + out_ref.shape[0], :]
        bias_ref[:, lanes] = sums_ref[at + east // 2 : at + east // 2 + 1, :]


def split_sums(sums, inputs, hidden, outputs):
    shapes = [
        jax.ShapeDtypeStruct(shape, jnp.float32)
        for shape in ((inputs, hidden), (1, hidden), (outputs, hidden))
    ]
    g_in, g_bias, g_out = pl.pallas_call(
        split_kernel,
        grid=(1,),
        in_specs=[whole_spec(sums)],
        out_specs=[whole_spec(a) for a in shapes],
        out_shape=shapes,
        compiler_params=call_params(),
    )(sums)
    return g_in, g_bias.reshape(hidden), g_out.T


def per_device(fields, cotangent, ocean_mask, depth_levels, in_weight, in_bias, out_weight):
    _, levels, north, east = fields.shape
    tables = Tables(levels, north, east, lax.axis_size("rows"), lax.axis_size("cols"))
    inputs, hidden = in_weight.shape
    outputs = out_weight.shape[1]
    in_bias = in_bias.reshape(1, hidden)
    out_weight = out_weight.T
    steps = levels // SUB
    dep, *edges = advance_edges(fields, ocean_mask, depth_levels)
    back_coef = adjoint_local(tables, cotangent, dep)
    back_edges = adjoint_edges(tables, back_coef, edges[0], edges[1])
    half = advect(fields, dep, TRACERS, edges, (0, steps // 2), back_edges)
    back_jumps = interface(tables, exchange(back_edges), half[1], False, 52 << 20)
    adv, spread = advect(fields, dep, TRACERS, edges, (steps // 2, steps), back_jumps, half)
    mixed, coef, sides, grads = column(
        tables, dep, adv, spread, fields, cotangent, in_weight, in_bias, out_weight,
        back_coef, exchange(back_jumps),
    )
    received = exchange(sides)
    new = gather_fields(adv, mixed, coef)
    jumps_out = interface(tables, received, grads, True, VMEM_LIMIT, new)
    w = advect(fields, dep, (2,), edges, (0, steps), jumps_out)[0]
    jumps = exchange(jumps_out)
    sums = exchange(sum_pieces(tables, jumps, w))
    pressure, new_fields = pressure_finish(tables, dep, w, new, coef, jumps)
    return (new_fields, pressure, *split_sums(sums, inputs, hidden, outputs))


def solution(mesh):
    in_specs = (
        P(None, None, "cols", "rows"),
        P(None, None, "cols", "rows"),
        P("cols", "rows"),
        P("cols", "rows"),
        P(),
        P(),
        P(),
    )
    out_specs = (P(None, None, "cols", "rows"), P(None, "cols", "rows"), P(), P(), P())
    return jax.shard_map(
        per_device, mesh=mesh, in_specs=in_specs, out_specs=out_specs, check_vma=False
    )
```

```python
import functools

import jax
import jax.numpy as jnp
import numpy as np
from jax import lax
from jax.experimental import pallas as pl
from jax.experimental.pallas import tpu as pltpu
from jax.sharding import PartitionSpec as P

TIME_STEP = 0.2
RATE_MAX = 2.0
THERMAL = 0.5
HALINE = 0.5
SPECTRAL_SHIFT = 0.001
WENO_EPS = 1e-06
HALO = 3
FIELDS = 5
SUB = 8
PIECES = 4


def pack_kernel(mask_ref, depth_ref, *refs):
    field_refs, refs = refs[:PIECES], refs[PIECES:]
    dep_ref, xfirst_ref, xlast_ref, yfirst_ref, ylast_ref = refs
    field = pl.program_id(0)
    north, east = dep_ref.shape
    some = field_refs[0].shape[1] // north
    levels = PIECES * some
    per = east // north
    blocks = levels // per
    dep = jnp.where(mask_ref[...] == 1, depth_ref[...], 0)
    dep_ref[...] = dep
    tiled = jnp.concatenate([dep] * per, 0)
    level_in_block = lax.broadcasted_iota(jnp.int32, (east, east), 0) // north
    for t in range(blocks):
        piece, at = divmod(t * east, some * north)
        block = field_refs[piece][0, at : at + east, :]
        masked = jnp.where(level_in_block + t * per < tiled, block, 0.0)
        turned = masked.T
        row = field * blocks + t
        for s in range(HALO):
            xfirst_ref[s, pl.ds(row, 1), :] = turned[s : s + 1]
            xlast_ref[s, pl.ds(row, 1), :] = turned[east - HALO + s : east - HALO + s + 1]
    for s, piece in [(s, piece) for s in range(HALO) for piece in range(PIECES)]:
        level = lax.broadcasted_iota(jnp.int32, (some, east), 0) + piece * some
        at = pl.multiple_of((field * HALO + s) * levels + piece * some, SUB)
        low, high = s, north - HALO + s
        first = field_refs[piece][0, pl.ds(low, some, stride=north), :]
        last = field_refs[piece][0, pl.ds(high, some, stride=north), :]
        yfirst_ref[pl.ds(at, some), :] = jnp.where(level < dep[low : low + 1], first, 0.0)
        ylast_ref[pl.ds(at, some), :] = jnp.where(level < dep[high : high + 1], last, 0.0)

    @pl.when(field == 0)
    def _():
        depths = dep.astype(jnp.float32)
        end = FIELDS * HALO * levels
        yfirst_ref[end:, :] = jnp.broadcast_to(depths[:1], (SUB, east))
        ylast_ref[end:, :] = jnp.broadcast_to(depths[north - 1 :], (SUB, east))
        turned = tiled.astype(jnp.float32).T
        for s in range(HALO):
            high = east - HALO + s
            xfirst_ref[s, FIELDS * blocks :, :] = jnp.broadcast_to(turned[s : s + 1], (SUB, east))
            xlast_ref[s, FIELDS * blocks :, :] = jnp.broadcast_to(
                turned[high : high + 1], (SUB, east)
            )


def pack_edges(fields, mask, depth):
    _, levels, north, east = fields.shape
    rows = FIELDS * levels * north // east + SUB
    x_shape = jax.ShapeDtypeStruct((HALO, rows, east), jnp.float32)
    y_shape = jax.ShapeDtypeStruct((FIELDS * HALO * levels + SUB, east), jnp.float32)
    whole = lambda shape: pl.BlockSpec(shape.shape, lambda f: (0,) * len(shape.shape))
    return pl.pallas_call(
        pack_kernel,
        grid=(FIELDS,),
        in_specs=[
            whole(mask),
            whole(depth),
            *(
                pl.BlockSpec((1, levels * north // PIECES, east), lambda f, p=p: (f, p, 0))
                for p in range(PIECES)
            ),
        ],
        out_specs=[whole(mask), whole(x_shape), whole(x_shape), whole(y_shape), whole(y_shape)],
        out_shape=[jax.ShapeDtypeStruct(mask.shape, jnp.int32), x_shape, x_shape, y_shape, y_shape],
        compiler_params=pltpu.CompilerParams(vmem_limit_bytes=61 << 20),
    )(mask, depth, *(fields.reshape(FIELDS, levels * north, east) for _ in range(PIECES)))


def face_flux(slopes, left, right, speed, share):
    dm2, dm1, d0, dp1, dp2 = slopes
    ahead = speed > 0.0
    e1 = jnp.where(ahead, dm2, dp2)
    e2 = jnp.where(ahead, dm1, dp1)
    e4 = jnp.where(ahead, dp1, dm1)
    near = jnp.where(ahead, left, right)
    bend0, bend1, bend2 = e2 - e1, d0 - e2, e4 - d0
    tilt0, tilt1, tilt2 = bend0 + (e2 + e2), e2 + d0, bend2 - (d0 + d0)
    rough0 = bend0 * bend0 * (13.0 / 3.0) + (tilt0 * tilt0 + 4.0 * WENO_EPS)
    rough1 = bend1 * bend1 * (13.0 / 3.0) + (tilt1 * tilt1 + 4.0 * WENO_EPS)
    rough2 = bend2 * bend2 * (13.0 / 3.0) + (tilt2 * tilt2 + 4.0 * WENO_EPS)
    pair0, pair1, pair2 = rough1 * rough2, rough0 * rough2, rough0 * rough1
    g0, g1, g2 = pair0 * pair0, 6.0 * (pair1 * pair1), 3.0 * (pair2 * pair2)
    total = g0 * (tilt0 + (bend0 + e2)) + g1 * (tilt1 + d0) + g2 * (d0 - tilt2)
    return speed * near + share * (total * pltpu.reciprocal(g0 + g1 + g2, approx=True))


def advect_kernel(
    tracers, staged, begin, filled, dep_ref, *refs,
):
    field_refs, refs = refs[: len(staged)], refs[len(staged) :]
    xlo_ref, xhi_ref, ylo_ref, yhi_ref = refs[:4]
    refs = refs[5 + filled :]
    adv_ref = refs[0]
    spread_ref = refs[1] if len(tracers) > 1 else None
    (
        deep, both, lines, slopes, fluxes, cells, wets, su, su6, sv, sv6, sides,
    ) = refs[-12:]
    step = pl.program_id(0) + begin
    north, east = dep_ref.shape
    per = east // north
    blocks = SUB // per
    all_blocks = (xlo_ref.shape[1] - SUB) // FIELDS
    levels = all_blocks * per
    depth_row = FIELDS * all_blocks
    depth_end = FIELDS * HALO * levels
    faces = range(0, east + SUB, SUB)
    first_level = step * SUB

    @pl.when(step == begin)
    def _():
        depths = dep_ref[...].astype(jnp.float32)
        deep[SUB : SUB + east, :] = jnp.concatenate([depths] * per, 0).T
        deep[SUB - 1 : SUB, :] = xlo_ref[HALO - 1, depth_row : depth_row + 1, :]
        deep[SUB + east : SUB + east + 1, :] = xhi_ref[0, depth_row : depth_row + 1, :]
        both[:east, :] = jnp.minimum(deep[SUB - 1 : SUB - 1 + east, :], deep[SUB : SUB + east, :])
        both[east : east + 1, :] = jnp.minimum(
            deep[SUB + east - 1 : SUB + east, :], deep[SUB + east : SUB + east + 1, :]
        )

    level = (lax.broadcasted_iota(jnp.int32, (SUB, east), 0) + first_level).astype(jnp.float32)
    side_level = lax.broadcasted_iota(jnp.int32, (SUB, east), 1) // north + first_level
    depths = dep_ref[...].astype(jnp.float32)
    wets[0] = (level < ylo_ref[depth_end : depth_end + 1, :]).astype(jnp.float32)
    wets[north + 1] = (level < yhi_ref[depth_end : depth_end + 1, :]).astype(jnp.float32)
    for y in range(north):
        wets[y + 1] = (level < depths[y : y + 1]).astype(jnp.float32)

    for slot, f in enumerate(staged):
        field = field_refs[slot]
        for s in range(HALO):
            at = pl.multiple_of((f * HALO + s) * levels + first_level, SUB)
            cells[slot, s] = ylo_ref[pl.ds(at, SUB), :]
            cells[slot, north + HALO + s] = yhi_ref[pl.ds(at, SUB), :]
        for y in range(north):
            cells[slot, y + HALO] = field[0, pl.ds(y, SUB, stride=north), :] * wets[y + 1]
        for b in range(blocks):
            row = f * all_blocks + step * blocks + b
            for s in range(HALO):
                lines[slot, b, SUB - HALO + s : SUB - HALO + s + 1, :] = xlo_ref[
                    s, pl.ds(row, 1), :
                ]
                lines[slot, b, SUB + east + s : SUB + east + s + 1, :] = xhi_ref[
                    s, pl.ds(row, 1), :
                ]
            turned = field[0, b * east : (b + 1) * east, :].T
            height = (side_level + b * per).astype(jnp.float32)
            for r in range(0, east, SUB):
                wet = height < deep[SUB + r : 2 * SUB + r, :]
                lines[slot, b, SUB + r : 2 * SUB + r, :] = jnp.where(
                    wet, turned[r : r + SUB], 0.0
                )

    for b in range(blocks):
        height = (side_level + b * per).astype(jnp.float32)
        for r in faces:
            speed = (0.5 * TIME_STEP) * (
                lines[0, b, SUB + r - 1 : 2 * SUB + r - 1, :] + lines[0, b, SUB + r : 2 * SUB + r, :]
            )
            speed = jnp.where(height < both[r : r + SUB, :], speed, 0.0)
            su[b, r : r + SUB, :] = speed
            su6[b, r : r + SUB, :] = jnp.abs(speed) * (1.0 / 6.0)
        if spread_ref is not None:
            change = 0.5 * (
                lines[0, b, SUB + 1 : SUB + 1 + east, :] - lines[0, b, SUB - 1 : SUB - 1 + east, :]
            )
            sides[b * east : (b + 1) * east, :] = change.T
    if spread_ref is not None:
        for y in range(north):
            spread_ref[y] = sides[pl.ds(y, SUB, stride=north), :] + 0.5 * (
                cells[1, y + HALO + 1] - cells[1, y + HALO - 1]
            )
    for y in range(north + 1):
        speed = (0.5 * TIME_STEP) * (cells[1, y + HALO - 1] + cells[1, y + HALO])
        speed = speed * (wets[y] * wets[y + 1])
        sv[y] = speed
        sv6[y] = jnp.abs(speed) * (1.0 / 6.0)

    first = len(staged) - len(tracers)

    def advance_field(f, carry):
        for b in range(blocks):
            for r in range(0, east + 2 * SUB, SUB):
                ahead = lines[f, b, r + 1 : r + 1 + SUB, :]
                slopes[b, r : r + SUB, :] = ahead - lines[f, b, r : r + SUB, :]
            for r in faces:
                at = SUB + r
                near = [slopes[b, at + k : at + k + SUB, :] for k in (-3, -2, -1, 0, 1)]
                fluxes[b, r : r + SUB, :] = face_flux(
                    near,
                    lines[f, b, at - 1 : at - 1 + SUB, :],
                    lines[f, b, at : at + SUB, :],
                    su[b, r : r + SUB, :],
                    su6[b, r : r + SUB, :],
                )
            change = fluxes[b, 0:east, :] - fluxes[b, 1 : 1 + east, :]
            sides[b * east : (b + 1) * east, :] = change.T
        line = [cells[f, k] for k in range(5)]
        inclines = [line[k + 1] - line[k] for k in range(4)]
        south = None
        for y in range(north + 1):
            line.append(cells[f, y + 2 * HALO - 1])
            inclines.append(line[-1] - line[-2])
            north_face = face_flux(inclines[-5:], line[-4], line[-3], sv[y], sv6[y])
            if y > 0:
                change = sides[pl.ds(y - 1, SUB, stride=north), :] + (south - north_face)
                adv_ref[f - first, y - 1] = wets[y] * (line[-4] + change)
            south = north_face
        return carry

    lax.fori_loop(first, len(staged), advance_field, 0)


def advect(fields, dep, tracers, edges, span, after, filled=()):
    _, levels, north, east = fields.shape
    whole = lambda a: pl.BlockSpec(a.shape, lambda k: (0,) * a.ndim)
    staged = tracers if tracers[0] == 0 else (0, 1, *tracers)
    one = lambda f: pl.BlockSpec((1, SUB * north, east), lambda k: (f, k + span[0], 0))
    f32 = jnp.float32
    blocks = SUB * north // east
    flat = fields.reshape(FIELDS, levels * north, east)
    out_specs = [pl.BlockSpec((len(tracers), north, SUB, east), lambda k: (0, 0, k + span[0], 0))]
    out_shape = [jax.ShapeDtypeStruct((len(tracers), north, levels, east), f32)]
    if tracers[0] == 0:
        out_specs.append(pl.BlockSpec((north, SUB, east), lambda k: (0, k + span[0], 0)))
        out_shape.append(jax.ShapeDtypeStruct((north, levels, east), f32))
    return pl.pallas_call(
        functools.partial(advect_kernel, tracers, staged, span[0], len(filled)),
        grid=(span[1] - span[0],),
        in_specs=[
            whole(dep),
            *(one(f) for f in staged),
            *(whole(a) for a in edges),
            pl.BlockSpec(memory_space=pl.ANY),
            *(pl.BlockSpec(memory_space=pl.ANY) for _ in filled),
        ],
        out_specs=out_specs,
        out_shape=out_shape,
        input_output_aliases={len(staged) + 6 + i: i for i in range(len(filled))},
        scratch_shapes=[
            pltpu.VMEM((east + 2 * SUB, east), f32),
            pltpu.VMEM((east + SUB, east), f32),
            pltpu.VMEM((len(staged), blocks, east + 3 * SUB, east), f32),
            pltpu.VMEM((blocks, east + 3 * SUB, east), f32),
            pltpu.VMEM((blocks, east + SUB, east), f32),
            pltpu.VMEM((len(staged), north + 2 * HALO, SUB, east), f32),
            pltpu.VMEM((north + 2, SUB, east), f32),
            pltpu.VMEM((blocks, east + SUB, east), f32),
            pltpu.VMEM((blocks, east + SUB, east), f32),
            pltpu.VMEM((north + 1, SUB, east), f32),
            pltpu.VMEM((north + 1, SUB, east), f32),
            pltpu.VMEM((SUB * north, east), f32),
        ],
        compiler_params=pltpu.CompilerParams(vmem_limit_bytes=VMEM_LIMIT),
    )(dep, *(flat for _ in staged), *edges, after, *filled)


def shift_both(axis, first, last):
    count = lax.axis_size(axis)
    forward = [(i, i + 1) for i in range(count - 1)]
    backward = [(i + 1, i) for i in range(count - 1)]
    return lax.ppermute(last, axis, forward), lax.ppermute(first, axis, backward)


def advance_edges(fields, mask, depth):
    dep, xfirst, xlast, yfirst, ylast = pack_edges(fields, mask, depth)
    south_north = shift_both("cols", yfirst, ylast)
    return (dep, *shift_both("rows", xfirst, xlast), *south_north)


AXES = ("rows", "cols")
VMEM_LIMIT = 52 << 20
TRACERS = (0, 1, 3, 4)
PARTS = 4


def dct_table(length):
    freq = np.arange(length)[:, None]
    cells = np.arange(length)[None, :]
    scale = np.where(freq == 0, np.sqrt(1.0 / length), np.sqrt(2.0 / length))
    return scale * np.cos(np.pi * (cells + 0.5) * freq / length)


def eigen_table(length):
    return 2.0 - 2.0 * np.cos(np.pi * np.arange(length) / length)


def halves(table):
    high = table.astype(jnp.bfloat16)
    low = (table - high.astype(np.float64)).astype(jnp.bfloat16)
    return high, low


def right_factor(table):
    high, low = halves(table)
    return np.block([[high, low], [high, np.zeros_like(low)]])


def left_factor(table):
    high, low = halves(table)
    return np.concatenate([high, low], 0)


class Tables:
    def __init__(self, levels, north, east, rows, cols):
        self.levels, self.north, self.east, self.rows, self.cols = levels, north, east, rows, cols
        self.count = rows * cols
        self.share = -(-levels // self.count)
        padded = self.share * self.count
        cz, cy, cx = dct_table(levels), dct_table(north), dct_table(east)
        lz, ly, lx = eigen_table(levels), eigen_table(north), eigen_table(east)
        shift = SPECTRAL_SHIFT + lz
        f32 = np.float32
        eye = np.eye(SUB)
        self.ly = [float(v) for v in ly]
        self.south = [float(v) for v in cy[:, 0]]
        self.north_edge = [float(v) for v in cy[:, -1]]
        self.base = (shift[:, None] + lx[None]).astype(f32)
        self.z_forward, self.z_back = left_factor(cz), left_factor(cz.T)
        self.y_forward = left_factor(np.kron(cy, eye))
        self.y_back = left_factor(np.kron(cy.T, eye))
        self.x_forward, self.x_back = right_factor(cx.T), right_factor(cx)
        edges = np.zeros((2 * north, east))
        edges[:north], edges[north:] = cx[:, 0], cx[:, -1]
        self.take = np.concatenate(halves(edges.T), 1)
        edges[:north], edges[north:] = -cx[:, -1], cx[:, 0]
        give = np.concatenate(halves(edges), 0)
        self.give = np.concatenate([give, give], 0)
        assert 4 * north == east
        lanes = max(east, 2 * north)
        assert lanes == east and cols % SUB == 0
        grid = 1.0 / (shift[:, None, None] + ly[None, :, None] + lx[None, None, :])
        alpha = np.einsum("k,myk->my", cx[:, -1] ** 2, grid)
        beta = np.einsum("k,myk->my", cx[:, -1] * cx[:, 0], grid)
        inner = rows - 1
        near = np.eye(inner, k=1) + np.eye(inner, k=-1)
        system = (1.0 + 2.0 * alpha)[..., None, None] * np.eye(inner) - beta[
            ..., None, None
        ] * near
        inverse = np.linalg.inv(system).transpose(0, 2, 3, 1).reshape(levels, inner**2, north)
        cross = np.zeros((padded, inner**2 + 1, east), f32)
        cross[:levels, : inner**2, :north] = inverse
        cross[:, inner**2] = 1.0
        cross[:levels, inner**2] = shift[:, None]
        self.cross = cross
        all_east = eigen_table(rows * east)
        grid = 1.0 / (shift[:, None, None] + ly[None, :, None] + all_east[None, None, :])
        alpha = np.einsum("y,myk->mk", cy[:, -1] ** 2, grid)
        beta = np.einsum("y,myk->mk", cy[:, -1] * cy[:, 0], grid)
        waves = np.cos(np.pi * np.arange(1, cols) / cols)
        along = np.zeros((padded, cols, rows * east), f32)
        along[:levels, : cols - 1] = 1.0 / (
            1.0 + 2.0 * alpha[:, None] - 2.0 * beta[:, None] * waves[None, :, None]
        )
        self.along = along
        order = np.arange(1, cols)
        sines = np.zeros((cols, cols))
        sines[: cols - 1, : cols - 1] = np.sqrt(2.0 / cols) * np.sin(
            np.pi * np.outer(order, order) / cols
        )
        self.sines = np.kron(np.eye(self.share), sines).astype(f32)
        wide = dct_table(rows * east).reshape(rows * east, rows, east)
        turn = np.einsum("gax,kx->gak", wide, cx).reshape(rows * east, rows * east)
        self.wide_forward = np.stack(halves(turn.T))
        self.wide_back = np.stack(halves(turn))
        both = (ly[:, None] + lx[None]).astype(f32)
        self.strip = np.stack(
            [both, np.broadcast_to(cy[:, -1:], both.shape), np.broadcast_to(cy[:, :1], both.shape)]
        ).astype(f32)
        back = np.full((east, east), 1.0)
        gain = np.zeros((east, east))
        back[:, :north] = back[:, north : 2 * north] = both.T
        gain[:, :north], gain[:, north : 2 * north] = cx[:, -1:], cx[:, :1]
        self.column = np.stack([back, gain]).astype(f32)
        lines = np.zeros((SUB, east), f32)
        lines[0], lines[1] = cx[:, -1], cx[:, 0]
        lines[2, :north] = lines[2, north : 2 * north] = cy[:, -1]
        lines[3, :north] = lines[3, north : 2 * north] = cy[:, 0]
        self.lines = lines


def parts(value):
    high = value.astype(jnp.bfloat16)
    return high, (value - high.astype(jnp.float32)).astype(jnp.bfloat16)


def mul(a, b):
    return jnp.dot(a, b, preferred_element_type=jnp.float32)


def from_left(factor, value):
    rows = factor.shape[0] // 2
    high, low = parts(value)
    both = mul(factor, high)
    return both[:rows] + (both[rows:] + mul(factor[:rows], low))


def from_right(value, factor):
    columns = factor.shape[1] // 2
    both = mul(jnp.concatenate(parts(value), 1), factor)
    return both[:, :columns] + both[:, columns:]


def times(value, high, low):
    first, second = parts(value)
    return mul(first, high) + (mul(second, high) + mul(first, low))


def vertical_change(value):
    levels = value.shape[0]
    level = lax.broadcasted_iota(jnp.int32, value.shape, 0)
    above = jnp.where(level == levels - 1, 0.0, pltpu.roll(value, levels - 1, 0))
    below = jnp.where(level == 0, 0.0, pltpu.roll(value, 1, 0))
    return 0.5 * (above - below)


def pair_of(spec, m, rows):
    return jnp.concatenate(
        [spec[:, at : at + SUB, :].reshape(rows, -1) for at in (m, m + SUB)], 1
    )


def block_solve(tables, spec, base_ref, x_ref, y_ref, coef_ref):
    north, east, levels = tables.north, tables.east, tables.levels
    for y in range(0, north, 4):
        tile = spec[y : y + 4].reshape(4 * levels, east)
        spec[y : y + 4] = from_right(tile, x_ref[...]).reshape(4, levels, east)
    for m in range(0, levels, 2 * SUB):
        both = from_left(y_ref[...], pair_of(spec, m, north * SUB))
        for i in range(2):
            at = m + i * SUB
            base = base_ref[at : at + SUB, :]
            tile = both[:, i * east : (i + 1) * east]
            for k in range(north):
                coef_ref[k, at : at + SUB, :] = tile[k * SUB : (k + 1) * SUB] / (
                    base + tables.ly[k]
                )


def block_edges(tables, coef_ref, take_ref, edge_ref):
    north, east, levels = tables.north, tables.east, tables.levels
    zero = jnp.zeros((levels, east), jnp.float32)
    even = odd = total = rest = zero
    lane = lax.broadcasted_iota(jnp.int32, (levels, east), 1)
    place = lane % north
    for k in range(0, north, 4):
        group = coef_ref[k : k + 4]
        high, low = parts(group.reshape(4 * levels, east))
        high, low = mul(high, take_ref[...]), mul(low, take_ref[...])
        for i in range(4):
            value = tables.south[k + i] * group[i]
            if i % 2:
                odd = odd + value
            else:
                even = even + value
            mine = place == k + i
            total = total + jnp.where(mine, high[i * levels : (i + 1) * levels], 0.0)
            rest = rest + jnp.where(mine, low[i * levels : (i + 1) * levels], 0.0)
    total = total + pltpu.roll(total, east // 2, 1) + rest
    sides = (jnp.where(lane < 2 * north, total, 0.0), even + odd, even - odd, zero)
    for part in range(PARTS):
        edge_ref[pl.ds(part, levels, stride=PARTS), :] = sides[part]
    if edge_ref.shape[0] > levels * PARTS:
        edge_ref[levels * PARTS :, :] = jnp.zeros_like(edge_ref[levels * PARTS :, :])


def finish_solve(tables, spec, coef_ref, jump_ref, base_ref, y_ref, x_ref, z_ref, give_ref, use):
    north, east, levels = tables.north, tables.east, tables.levels
    side, ahead, behind = (
        jump_ref[pl.ds(part, levels, stride=PARTS), :] for part in range(PARTS - 1)
    )
    high, low = (half.astype(jnp.float32) for half in parts(side))
    sides = jnp.concatenate([high + pltpu.roll(high, east // 2, 1), low], 1)
    place = lax.broadcasted_iota(jnp.int32, sides.shape, 1) % north
    for k in range(0, north, 4):
        picked = [jnp.where(place == k + i, sides, 0.0).astype(jnp.bfloat16) for i in range(4)]
        change = mul(jnp.concatenate(picked, 0), give_ref[...])
        for i in range(4):
            value = change[i * levels : (i + 1) * levels] + (
                tables.south[k + i] * behind - tables.north_edge[k + i] * ahead
            )
            spec[k + i] = coef_ref[k + i] + value / (base_ref[...] + tables.ly[k + i])
    for m in range(0, levels, 2 * SUB):
        both = from_left(y_ref[...], pair_of(spec, m, north * SUB))
        for i in range(2):
            at = m + i * SUB
            tile = both[:, i * east : (i + 1) * east]
            spec[:, at : at + SUB, :] = tile.reshape(north, SUB, east)
    for y in range(0, north, 4):
        tile = from_right(spec[y : y + 4].reshape(4 * levels, east), x_ref[...])
        tile = jnp.concatenate([tile[k * levels : (k + 1) * levels] for k in range(4)], 1)
        tile = from_left(z_ref[...], tile)
        for k in range(4):
            use(y + k, tile[:, k * east : (k + 1) * east])


def interface_kernel(
    tables, device_ref, edge_ref, cross_ref, along_ref, sines_ref, forward_ref, back_ref,
    strip_ref, column_ref, lines_ref, *rest,
):
    del device_ref
    jump_ref = rest[-1]
    rows, cols, east, north = tables.rows, tables.cols, tables.east, tables.north
    each = edge_ref.shape[0] // tables.count
    mine = tables.share * PARTS
    if each > mine:
        total = edge_ref[mine:each, :]
        for d in range(1, tables.count):
            total = total + edge_ref[d * each + mine : (d + 1) * each, :]
        for d in range(tables.count):
            jump_ref[d * each + mine : (d + 1) * each, :] = total
    share, inner = tables.share, tables.rows - 1
    f32 = jnp.float32
    east_last, east_first = lines_ref[0:1, :], lines_ref[1:2, :]
    north_last, north_first = lines_ref[2:3, :], lines_ref[3:4, :]
    every = lax.Precision.HIGHEST

    def across(m, changes):
        result = []
        for i in range(inner):
            total = jnp.zeros((cols, east), f32)
            for j in range(inner):
                at = i * inner + j
                total = total + cross_ref[m, at : at + 1, :] * changes[j]
            result.append(total)
        return result

    gaps, steps = [], []
    for m in range(share):
        west, south, top = (
            [
                edge_ref[pl.ds(a * cols * each + m * PARTS + part, cols, stride=each), :]
                for a in range(rows)
            ]
            for part in range(PARTS - 1)
        )
        right = [pltpu.roll(tile, east - north, 1) for tile in west]
        gap = [right[i] - west[i + 1] for i in range(inner)]
        gaps.append(gap)
        jumps = jnp.concatenate(across(m, gap), 0)
        shift = cross_ref[m, inner**2 : inner**2 + 1, :]
        inverse = 1.0 / (strip_ref[0] + shift)
        weights = jnp.concatenate([strip_ref[1] * inverse, strip_ref[2] * inverse], 1)
        weights = jnp.concatenate([weights, jnp.zeros((east - north, 2 * east), f32)], 0)
        moved = times(jumps, *parts(weights))
        for a in range(rows):
            for side, at in ((top, 0), (south, east)):
                if a < inner:
                    side[a] = side[a] - east_last * moved[a * cols : (a + 1) * cols, at : at + east]
                if a > 0:
                    side[a] = side[a] + east_first * moved[
                        (a - 1) * cols : a * cols, at : at + east
                    ]
        steps.append(
            jnp.concatenate([top[a] - pltpu.roll(south[a], cols - 1, 0) for a in range(rows)], 1)
        )
    step = jnp.concatenate(steps, 0)
    waves = times(step, forward_ref[0], forward_ref[1])
    waves = jnp.dot(sines_ref[...], waves, precision=every, preferred_element_type=f32)
    waves = waves * jnp.concatenate([along_ref[m] for m in range(share)], 0)
    waves = jnp.dot(sines_ref[...], waves, precision=every, preferred_element_type=f32)
    step = times(waves, back_ref[0], back_ref[1])
    for m in range(share):
        shift = cross_ref[m, inner**2 : inner**2 + 1, :]
        here = step[m * cols : (m + 1) * cols]
        tall = [here[:, a * east : (a + 1) * east] for a in range(rows)]
        weights = column_ref[1] / (column_ref[0] + shift)
        moved = times(jnp.concatenate(tall, 0), *parts(weights))
        sides = []
        for a in range(rows):
            tile = moved[a * cols : (a + 1) * cols]
            sides.append(north_last * tile - north_first * pltpu.roll(tile, 1, 0))
        gap = [
            gaps[m][i] - (sides[i] - pltpu.roll(sides[i + 1], east - north, 1))
            for i in range(inner)
        ]
        jumps = across(m, gap)
        for a in range(rows):
            tile = jnp.zeros((cols, east), f32)
            if a < inner:
                tile = tile + jumps[a]
            if a > 0:
                tile = tile + pltpu.roll(jumps[a - 1], north, 1)
            out = (tile, tall[a], pltpu.roll(tall[a], 1, 0), jnp.zeros_like(tile))
            for part in range(PARTS):
                at = a * cols * each + m * PARTS + part
                jump_ref[pl.ds(at, cols, stride=each), :] = out[part]


def whole_spec(array):
    shape = tuple(array.shape)
    return pl.BlockSpec(shape, lambda *_: (0,) * len(shape))


def call_params(limit=VMEM_LIMIT):
    return pltpu.CompilerParams(vmem_limit_bytes=limit)


def exchange(block):
    return lax.all_to_all(block, AXES, split_axis=0, concat_axis=0, tiled=True)


def interface(tables, received, *after):
    device = lax.axis_index("rows") * lax.axis_size("cols") + lax.axis_index("cols")
    operands = (
        received, tables.cross, tables.along, tables.sines, tables.wide_forward, tables.wide_back,
        tables.strip, tables.column, tables.lines,
    )
    specs = [whole_spec(a) for a in operands]
    for at in (1, 2):
        shape = (tables.share, *operands[at].shape[1:])
        specs[at] = pl.BlockSpec(shape, lambda k, mine: (mine[0], 0, 0))
    return pl.pallas_call(
        functools.partial(interface_kernel, tables),
        grid_spec=pltpu.PrefetchScalarGridSpec(
            num_scalar_prefetch=1,
            grid=(1,),
            in_specs=[*specs, *(pl.BlockSpec(memory_space=pl.ANY) for _ in after)],
            out_specs=whole_spec(received),
        ),
        out_shape=jax.ShapeDtypeStruct(received.shape, jnp.float32),
        compiler_params=call_params(56 << 20),
    )(device.astype(jnp.int32).reshape(1), *operands, *after)


def adjoint_kernel(
    tables, dep_ref, cot_ref, z_ref, base_ref, x_ref, y_ref, coef_ref, spec
):
    north, east, levels = tables.north, tables.east, tables.levels
    level = lax.broadcasted_iota(jnp.int32, (levels, east), 0)
    for y in range(0, north, 4):
        tiles = []
        for k in range(y, y + 4):
            value = cot_ref[0, pl.ds(k, levels, stride=north), :]
            value = jnp.where(level < dep_ref[k : k + 1, :], value, 0.0)
            tiles.append(TIME_STEP * vertical_change(value))
        tile = from_left(z_ref[...], jnp.concatenate(tiles, 1))
        for k in range(4):
            spec[y + k] = tile[:, k * east : (k + 1) * east]
    block_solve(tables, spec, base_ref, x_ref, y_ref, coef_ref)


def solve_shapes(tables):
    coef = jax.ShapeDtypeStruct((tables.north, tables.levels, tables.east), jnp.float32)
    edge = jax.ShapeDtypeStruct((tables.share * tables.count * PARTS, tables.east), jnp.float32)
    return [coef, edge]


def adjoint_local(tables, cotangent, dep):
    levels, north, east = tables.levels, tables.north, tables.east
    consts = (tables.z_forward, tables.base, tables.x_forward, tables.y_forward)
    coef = solve_shapes(tables)[0]
    return pl.pallas_call(
        functools.partial(adjoint_kernel, tables),
        grid=(1,),
        in_specs=[
            whole_spec(dep),
            pl.BlockSpec((1, levels * north, east), lambda k: (2, 0, 0)),
            *(whole_spec(a) for a in consts),
        ],
        out_specs=whole_spec(coef),
        out_shape=coef,
        scratch_shapes=[pltpu.VMEM(coef.shape, jnp.float32)],
        compiler_params=call_params(52 << 20),
    )(dep, cotangent.reshape(FIELDS, levels * north, east), *consts)


def edges_kernel(tables, coef_ref, take_ref, *rest):
    block_edges(tables, coef_ref, take_ref, rest[-1])


def adjoint_edges(tables, coef, *after):
    edge = solve_shapes(tables)[1]
    return pl.pallas_call(
        functools.partial(edges_kernel, tables),
        grid=(1,),
        in_specs=[
            whole_spec(coef),
            whole_spec(tables.take),
            *(pl.BlockSpec(memory_space=pl.ANY) for _ in after),
        ],
        out_specs=whole_spec(edge),
        out_shape=edge,
        compiler_params=call_params(),
    )(coef, tables.take, *after)


def set_weights(w_in_ref, bias_ref, w_ref, w_in, bias, w, w_out, levels):
    inputs, width = w_in_ref.shape
    east = bias.shape[1]
    w_in[...] = w_in_ref[...].astype(jnp.float32).T.astype(jnp.bfloat16)
    bias[...] = jnp.broadcast_to(bias_ref[...], (east, width)).T
    for k in range(0, width, east):
        w[k : k + east, :] = jnp.zeros((east, east), jnp.float32)
        w[k : k + levels - 1, :] = w_ref[:, k : k + east].astype(jnp.float32)
        tile = w[k : k + east, :]
        w_out[:, k : k + east] = tile[:levels].astype(jnp.bfloat16)
        w[k : k + east, :] = tile.T


def closure(adv_ref, w_in, bias, w_out, feats, activity, hidden):
    levels, east = adv_ref.shape[2:]
    for k in range(SUB):
        for f in range(len(TRACERS)):
            feats[f * levels : (f + 1) * levels, k * east : (k + 1) * east] = adv_ref[f, k].astype(
                jnp.bfloat16
            )
    before = mul(w_in[...], feats[...])
    for k in range(SUB):
        lanes = slice(k * east, (k + 1) * east)
        value = jnp.tanh(before[:, lanes] + bias[...])
        if activity is not None:
            activity[:, lanes] = value
        hidden[:, lanes] = value.astype(jnp.bfloat16)
    return RATE_MAX * jax.nn.sigmoid(mul(w_out[...], hidden[...]))


def column_kernel(
    tables, dep_ref, adv_ref, spread_ref, w_field_ref, heat_ref, salt_ref,
    w_in_ref, bias_ref, w_ref, back_coef_ref, back_jump_ref,
    z_ref, base_ref, x_ref, y_ref, take_ref, y_back_ref, x_back_ref, z_back_ref, give_ref,
    mixed_ref, coef_ref, send_ref,
    spec, back, feats, activity, hidden, grads, flat, sides, total_ref,
    w_in, bias, w, w_out, g_in_ref, g_bias_ref, g_out_ref,
):
    step = pl.program_id(0)
    north, east, levels = tables.north, tables.east, tables.levels
    f32, bf16 = jnp.float32, jnp.bfloat16

    @pl.when(step == 0)
    def _():
        set_weights(w_in_ref, bias_ref, w_ref, w_in, bias, w, w_out, levels)
        g_in_ref[...] = jnp.zeros_like(g_in_ref)
        g_out_ref[...] = jnp.zeros_like(g_out_ref)
        g_bias_ref[...] = jnp.zeros_like(g_bias_ref)

        def use(y, tile):
            back[y] = tile

        finish_solve(
            tables, spec, back_coef_ref, back_jump_ref, base_ref, y_back_ref, x_back_ref,
            z_back_ref, give_ref, use,
        )

    rates = closure(adv_ref, w_in, bias, w_out, feats, activity, hidden)
    for i, ref in enumerate((heat_ref, salt_ref, w_field_ref)):
        flat[i] = ref[0].reshape(levels * SUB, east)
    level = lax.broadcasted_iota(jnp.int32, (levels, east), 0)
    depths = dep_ref[pl.ds(pl.multiple_of(step * SUB, SUB), SUB), :]
    sources = []
    for k in range(SUB):
        lanes = slice(k * east, (k + 1) * east)
        depth = depths[k : k + 1]
        wet = level < depth
        rate = rates[:, lanes]
        flow = jnp.where(level + 1 < depth, TIME_STEP, 0.0) * rate
        slope = -vertical_change(jnp.where(wet, back[step * SUB + k], 0.0))
        mixed = []
        total = jnp.zeros((levels, east), f32)
        for i, share in ((0, THERMAL), (1, -HALINE)):
            value = adv_ref[2 + i, k]
            drop = pltpu.roll(value, levels - 1, 0) - value
            grad = flat[i, pl.ds(k, levels, stride=SUB), :] + share * slope
            grad = jnp.where(wet, grad, 0.0)
            total = total + (grad - pltpu.roll(grad, levels - 1, 0)) * drop
            flux = flow * drop
            value = jnp.where(wet, value + (flux - pltpu.roll(flux, 1, 0)), 0.0)
            mixed.append(value)
            mixed_ref[i, k] = value
        grads[:, lanes] = (total * flow * (1.0 - rate * (1.0 / RATE_MAX))).astype(bf16)
        rise = jnp.where(wet, flat[2, pl.ds(k, levels, stride=SUB), :], 0.0)
        density = THERMAL * mixed[0] - HALINE * mixed[1] - rise * (1.0 / TIME_STEP)
        source = vertical_change(density) - spread_ref[k] * (1.0 / TIME_STEP)
        sources.append(jnp.where(wet, source, 0.0))
    tile = from_left(z_ref[...], jnp.concatenate(sources, 1))
    for k in range(SUB):
        spec[step * SUB + k] = tile[:, k * east : (k + 1) * east]

    over = (((1,), (1,)), ((), ()))
    grad = grads[...]
    g_out_ref[...] += lax.dot_general(hidden[...], grad, over, preferred_element_type=f32)
    pre = mul(w[:, :levels].astype(bf16), grad)
    for k in range(SUB):
        lanes = slice(k * east, (k + 1) * east)
        value = activity[:, lanes]
        value = pre[:, lanes] * (1.0 - value * value)
        g_bias_ref[...] += value
        hidden[:, lanes] = value.astype(bf16)
    g_in_ref[...] += lax.dot_general(feats[...], hidden[...], over, preferred_element_type=f32)

    @pl.when(step == north // SUB - 1)
    def _():
        block_solve(tables, spec, base_ref, x_ref, y_ref, coef_ref)
        block_edges(tables, coef_ref, take_ref, sides)
        inputs, width = g_in_ref.shape
        for k in range(width // east):
            total_ref[k * inputs : (k + 1) * inputs, :] = g_in_ref[:, k * east : (k + 1) * east]
        sums = jnp.sum(g_bias_ref[...], 1, keepdims=True)
        last = jnp.concatenate([g_out_ref[...], jnp.broadcast_to(sums, g_out_ref.shape)], 1)
        at = inputs * width // east
        for k in range(0, width, east):
            total_ref[at + k : at + k + east, :] = last[k : k + east].T
        if total_ref.shape[0] > at + width:
            total_ref[at + width :, :] = jnp.zeros_like(total_ref[at + width :, :])
        mine = tables.share * PARTS
        each = send_ref.shape[0] // tables.count
        for part in range(mine):
            send_ref[pl.ds(part, tables.count, stride=each), :] = sides[
                pl.ds(part, tables.count, stride=mine), :
            ]
        more = each - mine
        for d in range(tables.count):
            send_ref[d * each + mine : (d + 1) * each, :] = total_ref[d * more : (d + 1) * more, :]


def column(
    tables, dep, adv, spread, fields, cotangent, in_weight, in_bias, out_weight, coef, jumps
):
    levels, north, east = tables.levels, tables.north, tables.east
    inputs, hidden = in_weight.shape
    f32, bf16 = jnp.float32, jnp.bfloat16
    consts = (
        in_weight, in_bias, out_weight, coef, jumps,
        tables.z_forward, tables.base, tables.x_forward, tables.y_forward, tables.take,
        tables.y_back, tables.x_back, tables.z_back, tables.give,
    )
    mixed = jax.ShapeDtypeStruct((2, north, levels, east), f32)
    coef, edge = solve_shapes(tables)
    rows = inputs * hidden // east + hidden
    assert 2 * levels == east
    rows = -(-rows // tables.count) * tables.count
    send = jax.ShapeDtypeStruct((edge.shape[0] + rows, east), f32)
    lanes = SUB * east
    field = lambda f: pl.BlockSpec((1, levels, SUB, east), lambda k: (f, 0, k, 0))
    return pl.pallas_call(
        functools.partial(column_kernel, tables),
        grid=(north // SUB,),
        in_specs=[
            whole_spec(dep),
            pl.BlockSpec((len(TRACERS), SUB, levels, east), lambda k: (0, k, 0, 0)),
            pl.BlockSpec((SUB, levels, east), lambda k: (k, 0, 0)),
            field(2),
            field(3),
            field(4),
            *(whole_spec(a) for a in consts),
        ],
        out_specs=[
            pl.BlockSpec((2, SUB, levels, east), lambda k: (0, k, 0, 0)),
            whole_spec(coef),
            whole_spec(send),
        ],
        out_shape=[mixed, coef, send],
        scratch_shapes=[
            pltpu.VMEM(coef.shape, f32),
            pltpu.VMEM(coef.shape, f32),
            pltpu.VMEM((inputs, lanes), bf16),
            pltpu.VMEM((hidden, lanes), f32),
            pltpu.VMEM((hidden, lanes), bf16),
            pltpu.VMEM((levels, lanes), bf16),
            pltpu.VMEM((3, levels * SUB, east), f32),
            pltpu.VMEM(edge.shape, f32),
            pltpu.VMEM((rows, east), f32),
            pltpu.VMEM((hidden, inputs), bf16),
            pltpu.VMEM((hidden, east), f32),
            pltpu.VMEM((hidden, east), f32),
            pltpu.VMEM((levels, hidden), bf16),
            pltpu.VMEM((inputs, hidden), f32),
            pltpu.VMEM((hidden, east), f32),
            pltpu.VMEM((hidden, levels), f32),
        ],
        compiler_params=call_params(),
    )(dep, adv, spread, fields, cotangent, cotangent, *consts)


def gather_kernel(adv_ref, mixed_ref, after_ref, new_ref, flat):
    del after_ref
    levels, east = adv_ref.shape[2:]
    for f, (ref, i) in zip(TRACERS, ((adv_ref, 0), (adv_ref, 1), (mixed_ref, 0), (mixed_ref, 1))):
        for k in range(SUB):
            flat[f, pl.ds(k, levels, stride=SUB), :] = ref[i, k]
        new_ref[f] = flat[f].reshape(levels, SUB, east)


def gather_fields(adv, mixed, after):
    _, north, levels, east = adv.shape
    block = pl.BlockSpec((2, SUB, levels, east), lambda k: (0, k, 0, 0))
    return pl.pallas_call(
        gather_kernel,
        grid=(north // SUB,),
        in_specs=[block, block, pl.BlockSpec(memory_space=pl.ANY)],
        out_specs=pl.BlockSpec((FIELDS, levels, SUB, east), lambda k: (0, 0, k, 0)),
        out_shape=jax.ShapeDtypeStruct((FIELDS, levels, north, east), jnp.float32),
        scratch_shapes=[pltpu.VMEM((FIELDS, levels * SUB, east), jnp.float32)],
        compiler_params=call_params(61 << 20),
    )(adv, mixed, after)


def solve_consts(tables):
    return (tables.base, tables.y_back, tables.x_back, tables.z_back, tables.give)


def pressure_kernel(
    tables, dep_ref, w_ref, new_ref, coef_ref, jump_ref, base_ref, y_ref, x_ref, z_ref, give_ref,
    pressure_ref, out_ref, spec, jumps,
):
    north, east, levels = tables.north, tables.east, tables.levels
    mine = tables.share * PARTS
    each = jump_ref.shape[0] // tables.count
    for part in range(mine):
        jumps[pl.ds(part, tables.count, stride=mine), :] = jump_ref[
            pl.ds(part, tables.count, stride=each), :
        ]
    level = lax.broadcasted_iota(jnp.int32, (levels, east), 0)

    def use(y, tile):
        pressure_ref[pl.ds(y, levels, stride=north), :] = tile
        value = w_ref[0, y] - TIME_STEP * vertical_change(tile)
        value = jnp.where(level < dep_ref[y : y + 1, :], value, 0.0)
        out_ref[0, pl.ds(y, levels, stride=north), :] = value

    finish_solve(
        tables, spec, coef_ref, jumps, base_ref, y_ref, x_ref, z_ref, give_ref, use
    )


def pressure_finish(tables, dep, w, new, coef, jumps):
    levels, north, east = tables.levels, tables.north, tables.east
    consts = solve_consts(tables)
    flat = jax.ShapeDtypeStruct((levels * north, east), jnp.float32)
    pressure, new = pl.pallas_call(
        functools.partial(pressure_kernel, tables),
        grid=(1,),
        in_specs=[
            whole_spec(dep),
            whole_spec(w),
            pl.BlockSpec(memory_space=pl.ANY),
            whole_spec(coef),
            whole_spec(jumps),
            *(whole_spec(a) for a in consts),
        ],
        out_specs=[
            whole_spec(flat),
            pl.BlockSpec((1, levels * north, east), lambda k: (2, 0, 0)),
        ],
        out_shape=[flat, jax.ShapeDtypeStruct((FIELDS, levels * north, east), jnp.float32)],
        input_output_aliases={2: 1},
        scratch_shapes=[
            pltpu.VMEM(coef.shape, jnp.float32),
            pltpu.VMEM((tables.share * tables.count * PARTS, east), jnp.float32),
        ],
        compiler_params=call_params(),
    )(dep, w, new.reshape(FIELDS, levels * north, east), coef, jumps, *consts)
    return pressure.reshape(levels, north, east), new.reshape(FIELDS, levels, north, east)


def split_kernel(skip, count, sums_ref, in_ref, bias_ref, out_ref, flat):
    inputs, width = in_ref.shape
    east = sums_ref.shape[1]
    each = sums_ref.shape[0] // count
    more = each - skip
    for d in range(count):
        flat[d * more : (d + 1) * more, :] = sums_ref[d * each + skip : (d + 1) * each, :]
    wide = inputs * width // east
    for k in range(width // east):
        lanes = slice(k * east, (k + 1) * east)
        in_ref[:, lanes] = flat[k * inputs : (k + 1) * inputs, :]
        at = wide + k * east
        out_ref[:, lanes] = flat[at : at + out_ref.shape[0], :]
        bias_ref[:, lanes] = flat[at + east // 2 : at + east // 2 + 1, :]


def split_sums(tables, sums, inputs, hidden, outputs):
    skip = tables.share * PARTS
    rows = sums.shape[0] - skip * tables.count
    shapes = [
        jax.ShapeDtypeStruct(shape, jnp.float32)
        for shape in ((inputs, hidden), (1, hidden), (outputs, hidden))
    ]
    g_in, g_bias, g_out = pl.pallas_call(
        functools.partial(split_kernel, skip, tables.count),
        grid=(1,),
        in_specs=[whole_spec(sums)],
        out_specs=[whole_spec(a) for a in shapes],
        out_shape=shapes,
        scratch_shapes=[pltpu.VMEM((rows, tables.east), jnp.float32)],
        compiler_params=call_params(),
    )(sums)
    return g_in, g_bias.reshape(hidden), g_out.T


def per_device(fields, cotangent, ocean_mask, depth_levels, in_weight, in_bias, out_weight):
    _, levels, north, east = fields.shape
    tables = Tables(levels, north, east, lax.axis_size("rows"), lax.axis_size("cols"))
    inputs, hidden = in_weight.shape
    outputs = out_weight.shape[1]
    in_bias = in_bias.reshape(1, hidden)
    out_weight = out_weight.T
    steps = levels // SUB
    dep, *edges = advance_edges(fields, ocean_mask, depth_levels)
    back_coef = adjoint_local(tables, cotangent, dep)
    back_edges = adjoint_edges(tables, back_coef, edges[0], edges[1])
    half = advect(fields, dep, TRACERS, edges, (0, steps // 2), back_edges)
    back_jumps = interface(tables, exchange(back_edges), half[1])
    adv, spread = advect(fields, dep, TRACERS, edges, (steps // 2, steps), back_jumps, half)
    mixed, coef, send = column(
        tables, dep, adv, spread, fields, cotangent, in_weight, in_bias, out_weight,
        back_coef, exchange(back_jumps),
    )
    received = exchange(send)
    w = advect(fields, dep, (2,), edges, (0, steps), coef)[0]
    new = gather_fields(adv, mixed, coef)
    jumps = exchange(interface(tables, received, w, new))
    pressure, new_fields = pressure_finish(tables, dep, w, new, coef, jumps)
    return (new_fields, pressure, *split_sums(tables, jumps, inputs, hidden, outputs))


def solution(mesh):
    in_specs = (
        P(None, None, "cols", "rows"),
        P(None, None, "cols", "rows"),
        P("cols", "rows"),
        P("cols", "rows"),
        P(),
        P(),
        P(),
    )
    out_specs = (P(None, None, "cols", "rows"), P(None, "cols", "rows"), P(), P(), P())
    return jax.shard_map(
        per_device, mesh=mesh, in_specs=in_specs, out_specs=out_specs, check_vma=False
    )
```

```python
import functools

import jax
import jax.numpy as jnp
import numpy as np
from jax import lax
from jax.experimental import pallas as pl
from jax.experimental.pallas import tpu as pltpu
from jax.sharding import PartitionSpec as P

TIME_STEP = 0.2
RATE_MAX = 2.0
THERMAL = 0.5
HALINE = 0.5
SPECTRAL_SHIFT = 0.001
WENO_EPS = 1e-06
HALO = 3
FIELDS = 5
SUB = 8
PIECES = 4


def spread_rows(rows, b):
    east = rows.shape[1]
    ys = east // SUB
    return jnp.concatenate(
        [jnp.broadcast_to(rows[y : y + 1], (SUB, east)) for y in range(b * ys, (b + 1) * ys)], 0
    )


def pack_kernel(mask_ref, depth_ref, *refs):
    field_refs, refs = refs[:PIECES], refs[PIECES:]
    dep_ref, xfirst_ref, xlast_ref, yfirst_ref, ylast_ref = refs
    field = pl.program_id(0)
    north, east = dep_ref.shape
    some = field_refs[0].shape[1] // north
    levels = PIECES * some
    ys = east // SUB
    halves = north // ys
    blocks = levels // SUB * halves
    dep = jnp.where(mask_ref[...] == 1, depth_ref[...], 0)
    dep_ref[...] = dep
    first_levels = lax.broadcasted_iota(jnp.int32, (SUB, east), 0)
    for t in range(blocks):
        low, start = t // halves * SUB, t % halves * ys
        piece, at = divmod(low, some)
        tiles = []
        for y in range(start, start + ys):
            value = field_refs[piece][0, pl.ds(at * north + y, SUB, stride=north), :]
            tiles.append(jnp.where(first_levels + low < dep[y : y + 1], value, 0.0))
        turned = jnp.concatenate(tiles, 0).T
        row = field * blocks + t
        for s in range(HALO):
            xfirst_ref[s, pl.ds(row, 1), :] = turned[s : s + 1]
            xlast_ref[s, pl.ds(row, 1), :] = turned[east - HALO + s : east - HALO + s + 1]
    for s, piece in [(s, piece) for s in range(HALO) for piece in range(PIECES)]:
        level = lax.broadcasted_iota(jnp.int32, (some, east), 0) + piece * some
        at = pl.multiple_of((field * HALO + s) * levels + piece * some, SUB)
        low, high = s, north - HALO + s
        first = field_refs[piece][0, pl.ds(low, some, stride=north), :]
        last = field_refs[piece][0, pl.ds(high, some, stride=north), :]
        yfirst_ref[pl.ds(at, some), :] = jnp.where(level < dep[low : low + 1], first, 0.0)
        ylast_ref[pl.ds(at, some), :] = jnp.where(level < dep[high : high + 1], last, 0.0)

    @pl.when(field == 0)
    def _():
        depths = dep.astype(jnp.float32)
        end = FIELDS * HALO * levels
        yfirst_ref[end:, :] = jnp.broadcast_to(depths[:1], (SUB, east))
        ylast_ref[end:, :] = jnp.broadcast_to(depths[north - 1 :], (SUB, east))
        for s in range(HALO):
            xfirst_ref[s, FIELDS * blocks :, :] = jnp.zeros((SUB, east), jnp.float32)
            xlast_ref[s, FIELDS * blocks :, :] = jnp.zeros((SUB, east), jnp.float32)
        for b in range(halves):
            turned = spread_rows(depths, b).T
            row = FIELDS * blocks + b
            for s in range(HALO):
                xfirst_ref[s, row : row + 1, :] = turned[s : s + 1]
                xlast_ref[s, row : row + 1, :] = turned[east - HALO + s : east - HALO + s + 1]


def pack_edges(fields, mask, depth):
    _, levels, north, east = fields.shape
    rows = FIELDS * levels * north // east + SUB
    x_shape = jax.ShapeDtypeStruct((HALO, rows, east), jnp.float32)
    y_shape = jax.ShapeDtypeStruct((FIELDS * HALO * levels + SUB, east), jnp.float32)
    whole = lambda shape: pl.BlockSpec(shape.shape, lambda f: (0,) * len(shape.shape))
    return pl.pallas_call(
        pack_kernel,
        grid=(FIELDS,),
        in_specs=[
            whole(mask),
            whole(depth),
            *(
                pl.BlockSpec((1, levels * north // PIECES, east), lambda f, p=p: (f, p, 0))
                for p in range(PIECES)
            ),
        ],
        out_specs=[whole(mask), whole(x_shape), whole(x_shape), whole(y_shape), whole(y_shape)],
        out_shape=[jax.ShapeDtypeStruct(mask.shape, jnp.int32), x_shape, x_shape, y_shape, y_shape],
        compiler_params=pltpu.CompilerParams(vmem_limit_bytes=61 << 20),
    )(mask, depth, *(fields.reshape(FIELDS, levels * north, east) for _ in range(PIECES)))


def face_flux(slopes, left, right, speed, share):
    dm2, dm1, d0, dp1, dp2 = slopes
    ahead = speed > 0.0
    e1 = jnp.where(ahead, dm2, dp2)
    e2 = jnp.where(ahead, dm1, dp1)
    e4 = jnp.where(ahead, dp1, dm1)
    near = jnp.where(ahead, left, right)
    bend0, bend1, bend2 = e2 - e1, d0 - e2, e4 - d0
    tilt0, tilt1, tilt2 = bend0 + (e2 + e2), e2 + d0, bend2 - (d0 + d0)
    rough0 = bend0 * bend0 * (13.0 / 3.0) + (tilt0 * tilt0 + 4.0 * WENO_EPS)
    rough1 = bend1 * bend1 * (13.0 / 3.0) + (tilt1 * tilt1 + 4.0 * WENO_EPS)
    rough2 = bend2 * bend2 * (13.0 / 3.0) + (tilt2 * tilt2 + 4.0 * WENO_EPS)
    pair0, pair1, pair2 = rough1 * rough2, rough0 * rough2, rough0 * rough1
    g0, g1, g2 = pair0 * pair0, 6.0 * (pair1 * pair1), 3.0 * (pair2 * pair2)
    total = g0 * (tilt0 + (bend0 + e2)) + g1 * (tilt1 + d0) + g2 * (d0 - tilt2)
    return speed * near + share * (total * pltpu.reciprocal(g0 + g1 + g2, approx=True))


def advect_kernel(
    tracers, staged, begin, filled, dep_ref, *refs,
):
    field_refs, refs = refs[: len(staged)], refs[len(staged) :]
    xlo_ref, xhi_ref, ylo_ref, yhi_ref = refs[:4]
    refs = refs[5 + filled :]
    adv_ref = refs[0]
    spread_ref = refs[1] if len(tracers) > 1 else None
    (
        deep, both, lines, slopes, fluxes, cells, wets, su, su6, sv, sv6, sides,
    ) = refs[-12:]
    step = pl.program_id(0) + begin
    north, east = dep_ref.shape
    ys = east // SUB
    blocks = north // ys
    all_blocks = (xlo_ref.shape[1] - SUB) // FIELDS
    levels = all_blocks // blocks * SUB
    depth_row = FIELDS * all_blocks
    depth_end = FIELDS * HALO * levels
    faces = range(0, east + SUB, SUB)
    first_level = step * SUB

    @pl.when(step == begin)
    def _():
        depths = dep_ref[...].astype(jnp.float32)
        for b in range(blocks):
            row = depth_row + b
            deep[SUB : SUB + east, :] = spread_rows(depths, b).T
            deep[SUB - 1 : SUB, :] = xlo_ref[HALO - 1, row : row + 1, :]
            deep[SUB + east : SUB + east + 1, :] = xhi_ref[0, row : row + 1, :]
            both[b, :east, :] = jnp.minimum(
                deep[SUB - 1 : SUB - 1 + east, :], deep[SUB : SUB + east, :]
            )
            both[b, east : east + 1, :] = jnp.minimum(
                deep[SUB + east - 1 : SUB + east, :], deep[SUB + east : SUB + east + 1, :]
            )

    level = (lax.broadcasted_iota(jnp.int32, (SUB, east), 0) + first_level).astype(jnp.float32)
    height = lax.broadcasted_iota(jnp.int32, (SUB, east), 1) % SUB + first_level
    height = height.astype(jnp.float32)
    depths = dep_ref[...].astype(jnp.float32)
    wets[0] = (level < ylo_ref[depth_end : depth_end + 1, :]).astype(jnp.float32)
    wets[north + 1] = (level < yhi_ref[depth_end : depth_end + 1, :]).astype(jnp.float32)
    for y in range(north):
        wets[y + 1] = (level < depths[y : y + 1]).astype(jnp.float32)

    for slot, f in enumerate(staged):
        field = field_refs[slot]
        for s in range(HALO):
            at = pl.multiple_of((f * HALO + s) * levels + first_level, SUB)
            cells[slot, s] = ylo_ref[pl.ds(at, SUB), :]
            cells[slot, north + HALO + s] = yhi_ref[pl.ds(at, SUB), :]
        for y in range(north):
            cells[slot, y + HALO] = field[0, pl.ds(y, SUB, stride=north), :] * wets[y + 1]
        for b in range(blocks):
            row = f * all_blocks + step * blocks + b
            for s in range(HALO):
                lines[slot, b, SUB - HALO + s : SUB - HALO + s + 1, :] = xlo_ref[
                    s, pl.ds(row, 1), :
                ]
                lines[slot, b, SUB + east + s : SUB + east + s + 1, :] = xhi_ref[
                    s, pl.ds(row, 1), :
                ]
            tile = cells[slot, HALO + b * ys : HALO + (b + 1) * ys].reshape(east, east)
            lines[slot, b, SUB : SUB + east, :] = tile.T

    for b in range(blocks):
        for r in faces:
            speed = (0.5 * TIME_STEP) * (
                lines[0, b, SUB + r - 1 : 2 * SUB + r - 1, :] + lines[0, b, SUB + r : 2 * SUB + r, :]
            )
            speed = jnp.where(height < both[b, r : r + SUB, :], speed, 0.0)
            su[b, r : r + SUB, :] = speed
            su6[b, r : r + SUB, :] = jnp.abs(speed) * (1.0 / 6.0)
        if spread_ref is not None:
            change = 0.5 * (
                lines[0, b, SUB + 1 : SUB + 1 + east, :] - lines[0, b, SUB - 1 : SUB - 1 + east, :]
            )
            sides[b * east : (b + 1) * east, :] = change.T
    if spread_ref is not None:
        for y in range(north):
            spread_ref[y] = sides[y * SUB : (y + 1) * SUB, :] + 0.5 * (
                cells[1, y + HALO + 1] - cells[1, y + HALO - 1]
            )
    for y in range(north + 1):
        speed = (0.5 * TIME_STEP) * (cells[1, y + HALO - 1] + cells[1, y + HALO])
        speed = speed * (wets[y] * wets[y + 1])
        sv[y] = speed
        sv6[y] = jnp.abs(speed) * (1.0 / 6.0)

    first = len(staged) - len(tracers)

    def advance_field(f, carry):
        for b in range(blocks):
            for r in range(0, east + 2 * SUB, SUB):
                ahead = lines[f, b, r + 1 : r + 1 + SUB, :]
                slopes[b, r : r + SUB, :] = ahead - lines[f, b, r : r + SUB, :]
            for r in faces:
                at = SUB + r
                near = [slopes[b, at + k : at + k + SUB, :] for k in (-3, -2, -1, 0, 1)]
                fluxes[b, r : r + SUB, :] = face_flux(
                    near,
                    lines[f, b, at - 1 : at - 1 + SUB, :],
                    lines[f, b, at : at + SUB, :],
                    su[b, r : r + SUB, :],
                    su6[b, r : r + SUB, :],
                )
            change = fluxes[b, 0:east, :] - fluxes[b, 1 : 1 + east, :]
            sides[b * east : (b + 1) * east, :] = change.T
        line = [cells[f, k] for k in range(5)]
        inclines = [line[k + 1] - line[k] for k in range(4)]
        south = None
        for y in range(north + 1):
            line.append(cells[f, y + 2 * HALO - 1])
            inclines.append(line[-1] - line[-2])
            north_face = face_flux(inclines[-5:], line[-4], line[-3], sv[y], sv6[y])
            if y > 0:
                change = sides[(y - 1) * SUB : y * SUB, :] + (south - north_face)
                adv_ref[f - first, y - 1] = wets[y] * (line[-4] + change)
            south = north_face
        return carry

    lax.fori_loop(first, len(staged), advance_field, 0)


def advect(fields, dep, tracers, edges, span, after, filled=()):
    _, levels, north, east = fields.shape
    whole = lambda a: pl.BlockSpec(a.shape, lambda k: (0,) * a.ndim)
    staged = tracers if tracers[0] == 0 else (0, 1, *tracers)
    one = lambda f: pl.BlockSpec((1, SUB * north, east), lambda k: (f, k + span[0], 0))
    f32 = jnp.float32
    blocks = SUB * north // east
    flat = fields.reshape(FIELDS, levels * north, east)
    out_specs = [pl.BlockSpec((len(tracers), north, SUB, east), lambda k: (0, 0, k + span[0], 0))]
    out_shape = [jax.ShapeDtypeStruct((len(tracers), north, levels, east), f32)]
    if tracers[0] == 0:
        out_specs.append(pl.BlockSpec((north, SUB, east), lambda k: (0, k + span[0], 0)))
        out_shape.append(jax.ShapeDtypeStruct((north, levels, east), f32))
    return pl.pallas_call(
        functools.partial(advect_kernel, tracers, staged, span[0], len(filled)),
        grid=(span[1] - span[0],),
        in_specs=[
            whole(dep),
            *(one(f) for f in staged),
            *(whole(a) for a in edges),
            pl.BlockSpec(memory_space=pl.ANY),
            *(pl.BlockSpec(memory_space=pl.ANY) for _ in filled),
        ],
        out_specs=out_specs,
        out_shape=out_shape,
        input_output_aliases={len(staged) + 6 + i: i for i in range(len(filled))},
        scratch_shapes=[
            pltpu.VMEM((east + 2 * SUB, east), f32),
            pltpu.VMEM((blocks, east + SUB, east), f32),
            pltpu.VMEM((len(staged), blocks, east + 3 * SUB, east), f32),
            pltpu.VMEM((blocks, east + 3 * SUB, east), f32),
            pltpu.VMEM((blocks, east + SUB, east), f32),
            pltpu.VMEM((len(staged), north + 2 * HALO, SUB, east), f32),
            pltpu.VMEM((north + 2, SUB, east), f32),
            pltpu.VMEM((blocks, east + SUB, east), f32),
            pltpu.VMEM((blocks, east + SUB, east), f32),
            pltpu.VMEM((north + 1, SUB, east), f32),
            pltpu.VMEM((north + 1, SUB, east), f32),
            pltpu.VMEM((SUB * north, east), f32),
        ],
        compiler_params=pltpu.CompilerParams(vmem_limit_bytes=VMEM_LIMIT),
    )(dep, *(flat for _ in staged), *edges, after, *filled)


def shift_both(axis, first, last):
    count = lax.axis_size(axis)
    forward = [(i, i + 1) for i in range(count - 1)]
    backward = [(i + 1, i) for i in range(count - 1)]
    return lax.ppermute(last, axis, forward), lax.ppermute(first, axis, backward)


def advance_edges(fields, mask, depth):
    dep, xfirst, xlast, yfirst, ylast = pack_edges(fields, mask, depth)
    south_north = shift_both("cols", yfirst, ylast)
    return (dep, *shift_both("rows", xfirst, xlast), *south_north)


AXES = ("rows", "cols")
VMEM_LIMIT = 52 << 20
TRACERS = (0, 1, 3, 4)
PARTS = 4


def dct_table(length):
    freq = np.arange(length)[:, None]
    cells = np.arange(length)[None, :]
    scale = np.where(freq == 0, np.sqrt(1.0 / length), np.sqrt(2.0 / length))
    return scale * np.cos(np.pi * (cells + 0.5) * freq / length)


def eigen_table(length):
    return 2.0 - 2.0 * np.cos(np.pi * np.arange(length) / length)


def halves(table):
    high = table.astype(jnp.bfloat16)
    low = (table - high.astype(np.float64)).astype(jnp.bfloat16)
    return high, low


def right_factor(table):
    high, low = halves(table)
    return np.block([[high, low], [high, np.zeros_like(low)]])


def left_factor(table):
    high, low = halves(table)
    return np.concatenate([high, low], 0)


class Tables:
    def __init__(self, levels, north, east, rows, cols):
        self.levels, self.north, self.east, self.rows, self.cols = levels, north, east, rows, cols
        self.count = rows * cols
        self.share = -(-levels // self.count)
        padded = self.share * self.count
        cz, cy, cx = dct_table(levels), dct_table(north), dct_table(east)
        lz, ly, lx = eigen_table(levels), eigen_table(north), eigen_table(east)
        shift = SPECTRAL_SHIFT + lz
        f32 = np.float32
        eye = np.eye(SUB)
        self.ly = [float(v) for v in ly]
        self.south = [float(v) for v in cy[:, 0]]
        self.north_edge = [float(v) for v in cy[:, -1]]
        self.base = (shift[:, None] + lx[None]).astype(f32)
        self.z_forward, self.z_back = left_factor(cz), left_factor(cz.T)
        self.y_forward = left_factor(np.kron(cy, eye))
        self.y_back = left_factor(np.kron(cy.T, eye))
        self.x_forward, self.x_back = right_factor(cx.T), right_factor(cx)
        edges = np.zeros((2 * north, east))
        edges[:north], edges[north:] = cx[:, 0], cx[:, -1]
        self.take = np.concatenate(halves(edges.T), 1)
        edges[:north], edges[north:] = -cx[:, -1], cx[:, 0]
        give = np.concatenate(halves(edges), 0)
        self.give = np.concatenate([give, give], 0)
        assert 4 * north == east
        lanes = max(east, 2 * north)
        assert lanes == east and cols % SUB == 0
        grid = 1.0 / (shift[:, None, None] + ly[None, :, None] + lx[None, None, :])
        alpha = np.einsum("k,myk->my", cx[:, -1] ** 2, grid)
        beta = np.einsum("k,myk->my", cx[:, -1] * cx[:, 0], grid)
        inner = rows - 1
        near = np.eye(inner, k=1) + np.eye(inner, k=-1)
        system = (1.0 + 2.0 * alpha)[..., None, None] * np.eye(inner) - beta[
            ..., None, None
        ] * near
        inverse = np.linalg.inv(system).transpose(0, 2, 3, 1).reshape(levels, inner**2, north)
        cross = np.zeros((padded, inner**2 + 1, east), f32)
        cross[:levels, : inner**2, :north] = inverse
        cross[:, inner**2] = 1.0
        cross[:levels, inner**2] = shift[:, None]
        self.cross = cross
        all_east = eigen_table(rows * east)
        grid = 1.0 / (shift[:, None, None] + ly[None, :, None] + all_east[None, None, :])
        alpha = np.einsum("y,myk->mk", cy[:, -1] ** 2, grid)
        beta = np.einsum("y,myk->mk", cy[:, -1] * cy[:, 0], grid)
        waves = np.cos(np.pi * np.arange(1, cols) / cols)
        along = np.zeros((padded, cols, rows * east), f32)
        along[:levels, : cols - 1] = 1.0 / (
            1.0 + 2.0 * alpha[:, None] - 2.0 * beta[:, None] * waves[None, :, None]
        )
        self.along = along
        order = np.arange(1, cols)
        sines = np.zeros((cols, cols))
        sines[: cols - 1, : cols - 1] = np.sqrt(2.0 / cols) * np.sin(
            np.pi * np.outer(order, order) / cols
        )
        self.sines = np.kron(np.eye(self.share), sines).astype(f32)
        wide = dct_table(rows * east).reshape(rows * east, rows, east)
        turn = np.einsum("gax,kx->gak", wide, cx).reshape(rows * east, rows * east)
        self.wide_forward = np.stack(halves(turn.T))
        self.wide_back = np.stack(halves(turn))
        both = (ly[:, None] + lx[None]).astype(f32)
        self.strip = np.stack(
            [both, np.broadcast_to(cy[:, -1:], both.shape), np.broadcast_to(cy[:, :1], both.shape)]
        ).astype(f32)
        back = np.full((east, east), 1.0)
        gain = np.zeros((east, east))
        back[:, :north] = back[:, north : 2 * north] = both.T
        gain[:, :north], gain[:, north : 2 * north] = cx[:, -1:], cx[:, :1]
        self.column = np.stack([back, gain]).astype(f32)
        lines = np.zeros((SUB, east), f32)
        lines[0], lines[1] = cx[:, -1], cx[:, 0]
        lines[2, :north] = lines[2, north : 2 * north] = cy[:, -1]
        lines[3, :north] = lines[3, north : 2 * north] = cy[:, 0]
        self.lines = lines


def parts(value):
    high = value.astype(jnp.bfloat16)
    return high, (value - high.astype(jnp.float32)).astype(jnp.bfloat16)


def mul(a, b):
    return jnp.dot(a, b, preferred_element_type=jnp.float32)


def from_left(factor, value):
    rows = factor.shape[0] // 2
    high, low = parts(value)
    both = mul(factor, high)
    return both[:rows] + (both[rows:] + mul(factor[:rows], low))


def from_right(value, factor):
    columns = factor.shape[1] // 2
    both = mul(jnp.concatenate(parts(value), 1), factor)
    return both[:, :columns] + both[:, columns:]


def times(value, high, low):
    first, second = parts(value)
    return mul(first, high) + (mul(second, high) + mul(first, low))


def vertical_change(value):
    levels = value.shape[0]
    level = lax.broadcasted_iota(jnp.int32, value.shape, 0)
    above = jnp.where(level == levels - 1, 0.0, pltpu.roll(value, levels - 1, 0))
    below = jnp.where(level == 0, 0.0, pltpu.roll(value, 1, 0))
    return 0.5 * (above - below)


def pair_of(spec, m, rows):
    return jnp.concatenate(
        [spec[:, at : at + SUB, :].reshape(rows, -1) for at in (m, m + SUB)], 1
    )


def block_solve(tables, spec, base_ref, x_ref, y_ref, coef_ref):
    north, east, levels = tables.north, tables.east, tables.levels
    for y in range(0, north, 4):
        tile = spec[y : y + 4].reshape(4 * levels, east)
        spec[y : y + 4] = from_right(tile, x_ref[...]).reshape(4, levels, east)
    for m in range(0, levels, 2 * SUB):
        both = from_left(y_ref[...], pair_of(spec, m, north * SUB))
        for i in range(2):
            at = m + i * SUB
            base = base_ref[at : at + SUB, :]
            tile = both[:, i * east : (i + 1) * east]
            for k in range(north):
                coef_ref[k, at : at + SUB, :] = tile[k * SUB : (k + 1) * SUB] / (
                    base + tables.ly[k]
                )


def block_edges(tables, coef_ref, take_ref, edge_ref):
    north, east, levels = tables.north, tables.east, tables.levels
    zero = jnp.zeros((levels, east), jnp.float32)
    even = odd = total = rest = zero
    lane = lax.broadcasted_iota(jnp.int32, (levels, east), 1)
    place = lane % north
    for k in range(0, north, 4):
        group = coef_ref[k : k + 4]
        high, low = parts(group.reshape(4 * levels, east))
        high, low = mul(high, take_ref[...]), mul(low, take_ref[...])
        for i in range(4):
            value = tables.south[k + i] * group[i]
            if i % 2:
                odd = odd + value
            else:
                even = even + value
            mine = place == k + i
            total = total + jnp.where(mine, high[i * levels : (i + 1) * levels], 0.0)
            rest = rest + jnp.where(mine, low[i * levels : (i + 1) * levels], 0.0)
    total = total + pltpu.roll(total, east // 2, 1) + rest
    sides = (jnp.where(lane < 2 * north, total, 0.0), even + odd, even - odd, zero)
    for part in range(PARTS):
        edge_ref[pl.ds(part, levels, stride=PARTS), :] = sides[part]
    if edge_ref.shape[0] > levels * PARTS:
        edge_ref[levels * PARTS :, :] = jnp.zeros_like(edge_ref[levels * PARTS :, :])


def finish_solve(tables, spec, coef_ref, jump_ref, base_ref, y_ref, x_ref, z_ref, give_ref, use):
    north, east, levels = tables.north, tables.east, tables.levels
    side, ahead, behind = (
        jump_ref[pl.ds(part, levels, stride=PARTS), :] for part in range(PARTS - 1)
    )
    high, low = (half.astype(jnp.float32) for half in parts(side))
    sides = jnp.concatenate([high + pltpu.roll(high, east // 2, 1), low], 1)
    place = lax.broadcasted_iota(jnp.int32, sides.shape, 1) % north
    for k in range(0, north, 4):
        picked = [jnp.where(place == k + i, sides, 0.0).astype(jnp.bfloat16) for i in range(4)]
        change = mul(jnp.concatenate(picked, 0), give_ref[...])
        for i in range(4):
            value = change[i * levels : (i + 1) * levels] + (
                tables.south[k + i] * behind - tables.north_edge[k + i] * ahead
            )
            spec[k + i] = coef_ref[k + i] + value / (base_ref[...] + tables.ly[k + i])
    for m in range(0, levels, 2 * SUB):
        both = from_left(y_ref[...], pair_of(spec, m, north * SUB))
        for i in range(2):
            at = m + i * SUB
            tile = both[:, i * east : (i + 1) * east]
            spec[:, at : at + SUB, :] = tile.reshape(north, SUB, east)
    for y in range(0, north, 4):
        tile = from_right(spec[y : y + 4].reshape(4 * levels, east), x_ref[...])
        tile = jnp.concatenate([tile[k * levels : (k + 1) * levels] for k in range(4)], 1)
        tile = from_left(z_ref[...], tile)
        for k in range(4):
            use(y + k, tile[:, k * east : (k + 1) * east])


def interface_kernel(
    tables, device_ref, edge_ref, cross_ref, along_ref, sines_ref, forward_ref, back_ref,
    strip_ref, column_ref, lines_ref, *rest,
):
    del device_ref
    jump_ref = rest[-1]
    rows, cols, east, north = tables.rows, tables.cols, tables.east, tables.north
    each = edge_ref.shape[0] // tables.count
    mine = tables.share * PARTS
    if each > mine:
        total = edge_ref[mine:each, :]
        for d in range(1, tables.count):
            total = total + edge_ref[d * each + mine : (d + 1) * each, :]
        for d in range(tables.count):
            jump_ref[d * each + mine : (d + 1) * each, :] = total
    share, inner = tables.share, tables.rows - 1
    f32 = jnp.float32
    east_last, east_first = lines_ref[0:1, :], lines_ref[1:2, :]
    north_last, north_first = lines_ref[2:3, :], lines_ref[3:4, :]
    every = lax.Precision.HIGHEST

    def across(m, changes):
        result = []
        for i in range(inner):
            total = jnp.zeros((cols, east), f32)
            for j in range(inner):
                at = i * inner + j
                total = total + cross_ref[m, at : at + 1, :] * changes[j]
            result.append(total)
        return result

    gaps, steps = [], []
    for m in range(share):
        west, south, top = (
            [
                edge_ref[pl.ds(a * cols * each + m * PARTS + part, cols, stride=each), :]
                for a in range(rows)
            ]
            for part in range(PARTS - 1)
        )
        right = [pltpu.roll(tile, east - north, 1) for tile in west]
        gap = [right[i] - west[i + 1] for i in range(inner)]
        gaps.append(gap)
        jumps = jnp.concatenate(across(m, gap), 0)
        shift = cross_ref[m, inner**2 : inner**2 + 1, :]
        inverse = 1.0 / (strip_ref[0] + shift)
        weights = jnp.concatenate([strip_ref[1] * inverse, strip_ref[2] * inverse], 1)
        weights = jnp.concatenate([weights, jnp.zeros((east - north, 2 * east), f32)], 0)
        moved = times(jumps, *parts(weights))
        for a in range(rows):
            for side, at in ((top, 0), (south, east)):
                if a < inner:
                    side[a] = side[a] - east_last * moved[a * cols : (a + 1) * cols, at : at + east]
                if a > 0:
                    side[a] = side[a] + east_first * moved[
                        (a - 1) * cols : a * cols, at : at + east
                    ]
        steps.append(
            jnp.concatenate([top[a] - pltpu.roll(south[a], cols - 1, 0) for a in range(rows)], 1)
        )
    step = jnp.concatenate(steps, 0)
    waves = times(step, forward_ref[0], forward_ref[1])
    waves = jnp.dot(sines_ref[...], waves, precision=every, preferred_element_type=f32)
    waves = waves * jnp.concatenate([along_ref[m] for m in range(share)], 0)
    waves = jnp.dot(sines_ref[...], waves, precision=every, preferred_element_type=f32)
    step = times(waves, back_ref[0], back_ref[1])
    for m in range(share):
        shift = cross_ref[m, inner**2 : inner**2 + 1, :]
        here = step[m * cols : (m + 1) * cols]
        tall = [here[:, a * east : (a + 1) * east] for a in range(rows)]
        weights = column_ref[1] / (column_ref[0] + shift)
        moved = times(jnp.concatenate(tall, 0), *parts(weights))
        sides = []
        for a in range(rows):
            tile = moved[a * cols : (a + 1) * cols]
            sides.append(north_last * tile - north_first * pltpu.roll(tile, 1, 0))
        gap = [
            gaps[m][i] - (sides[i] - pltpu.roll(sides[i + 1], east - north, 1))
            for i in range(inner)
        ]
        jumps = across(m, gap)
        for a in range(rows):
            tile = jnp.zeros((cols, east), f32)
            if a < inner:
                tile = tile + jumps[a]
            if a > 0:
                tile = tile + pltpu.roll(jumps[a - 1], north, 1)
            out = (tile, tall[a], pltpu.roll(tall[a], 1, 0), jnp.zeros_like(tile))
            for part in range(PARTS):
                at = a * cols * each + m * PARTS + part
                jump_ref[pl.ds(at, cols, stride=each), :] = out[part]


def whole_spec(array):
    shape = tuple(array.shape)
    return pl.BlockSpec(shape, lambda *_: (0,) * len(shape))


def call_params(limit=VMEM_LIMIT):
    return pltpu.CompilerParams(vmem_limit_bytes=limit)


def exchange(block):
    return lax.all_to_all(block, AXES, split_axis=0, concat_axis=0, tiled=True)


def interface(tables, received, limit, *after):
    device = lax.axis_index("rows") * lax.axis_size("cols") + lax.axis_index("cols")
    operands = (
        received, tables.cross, tables.along, tables.sines, tables.wide_forward, tables.wide_back,
        tables.strip, tables.column, tables.lines,
    )
    specs = [whole_spec(a) for a in operands]
    for at in (1, 2):
        shape = (tables.share, *operands[at].shape[1:])
        specs[at] = pl.BlockSpec(shape, lambda k, mine: (mine[0], 0, 0))
    return pl.pallas_call(
        functools.partial(interface_kernel, tables),
        grid_spec=pltpu.PrefetchScalarGridSpec(
            num_scalar_prefetch=1,
            grid=(1,),
            in_specs=[*specs, *(pl.BlockSpec(memory_space=pl.ANY) for _ in after)],
            out_specs=whole_spec(received),
        ),
        out_shape=jax.ShapeDtypeStruct(received.shape, jnp.float32),
        compiler_params=call_params(limit),
    )(device.astype(jnp.int32).reshape(1), *operands, *after)


def adjoint_kernel(
    tables, dep_ref, cot_ref, z_ref, base_ref, x_ref, y_ref, coef_ref, spec
):
    north, east, levels = tables.north, tables.east, tables.levels
    level = lax.broadcasted_iota(jnp.int32, (levels, east), 0)
    for y in range(0, north, 4):
        tiles = []
        for k in range(y, y + 4):
            value = cot_ref[0, pl.ds(k, levels, stride=north), :]
            value = jnp.where(level < dep_ref[k : k + 1, :], value, 0.0)
            tiles.append(TIME_STEP * vertical_change(value))
        tile = from_left(z_ref[...], jnp.concatenate(tiles, 1))
        for k in range(4):
            spec[y + k] = tile[:, k * east : (k + 1) * east]
    block_solve(tables, spec, base_ref, x_ref, y_ref, coef_ref)


def solve_shapes(tables):
    coef = jax.ShapeDtypeStruct((tables.north, tables.levels, tables.east), jnp.float32)
    edge = jax.ShapeDtypeStruct((tables.share * tables.count * PARTS, tables.east), jnp.float32)
    return [coef, edge]


def adjoint_local(tables, cotangent, dep):
    levels, north, east = tables.levels, tables.north, tables.east
    consts = (tables.z_forward, tables.base, tables.x_forward, tables.y_forward)
    coef = solve_shapes(tables)[0]
    return pl.pallas_call(
        functools.partial(adjoint_kernel, tables),
        grid=(1,),
        in_specs=[
            whole_spec(dep),
            pl.BlockSpec((1, levels * north, east), lambda k: (2, 0, 0)),
            *(whole_spec(a) for a in consts),
        ],
        out_specs=whole_spec(coef),
        out_shape=coef,
        scratch_shapes=[pltpu.VMEM(coef.shape, jnp.float32)],
        compiler_params=call_params(52 << 20),
    )(dep, cotangent.reshape(FIELDS, levels * north, east), *consts)


def edges_kernel(tables, coef_ref, take_ref, *rest):
    block_edges(tables, coef_ref, take_ref, rest[-1])


def adjoint_edges(tables, coef, *after):
    edge = solve_shapes(tables)[1]
    return pl.pallas_call(
        functools.partial(edges_kernel, tables),
        grid=(1,),
        in_specs=[
            whole_spec(coef),
            whole_spec(tables.take),
            *(pl.BlockSpec(memory_space=pl.ANY) for _ in after),
        ],
        out_specs=whole_spec(edge),
        out_shape=edge,
        compiler_params=call_params(),
    )(coef, tables.take, *after)


def set_weights(w_in_ref, bias_ref, w_ref, w_in, bias, w, w_out, levels):
    inputs, width = w_in_ref.shape
    east = bias.shape[1]
    w_in[...] = w_in_ref[...].astype(jnp.float32).T.astype(jnp.bfloat16)
    bias[...] = jnp.broadcast_to(bias_ref[...], (east, width)).T
    for k in range(0, width, east):
        w[k : k + east, :] = jnp.zeros((east, east), jnp.float32)
        w[k : k + levels - 1, :] = w_ref[:, k : k + east].astype(jnp.float32)
        tile = w[k : k + east, :]
        w_out[:, k : k + east] = tile[:levels].astype(jnp.bfloat16)
        w[k : k + east, :] = tile.T


def closure(adv_ref, w_in, bias, w_out, feats, activity, hidden):
    levels, east = adv_ref.shape[2:]
    for k in range(SUB):
        for f in range(len(TRACERS)):
            feats[f * levels : (f + 1) * levels, k * east : (k + 1) * east] = adv_ref[f, k].astype(
                jnp.bfloat16
            )
    before = mul(w_in[...], feats[...])
    for k in range(SUB):
        lanes = slice(k * east, (k + 1) * east)
        value = jnp.tanh(before[:, lanes] + bias[...])
        if activity is not None:
            activity[:, lanes] = value
        hidden[:, lanes] = value.astype(jnp.bfloat16)
    return RATE_MAX * jax.nn.sigmoid(mul(w_out[...], hidden[...]))


def column_kernel(
    tables, dep_ref, adv_ref, spread_ref, w_field_ref, heat_ref, salt_ref,
    w_in_ref, bias_ref, w_ref, back_coef_ref, back_jump_ref,
    z_ref, base_ref, x_ref, y_ref, take_ref, y_back_ref, x_back_ref, z_back_ref, give_ref,
    mixed_ref, coef_ref, send_ref,
    spec, back, feats, activity, hidden, grads, flat, sides, total_ref,
    w_in, bias, w, w_out, g_in_ref, g_bias_ref, g_out_ref,
):
    step = pl.program_id(0)
    north, east, levels = tables.north, tables.east, tables.levels
    f32, bf16 = jnp.float32, jnp.bfloat16

    @pl.when(step == 0)
    def _():
        set_weights(w_in_ref, bias_ref, w_ref, w_in, bias, w, w_out, levels)
        g_in_ref[...] = jnp.zeros_like(g_in_ref)
        g_out_ref[...] = jnp.zeros_like(g_out_ref)
        g_bias_ref[...] = jnp.zeros_like(g_bias_ref)

        def use(y, tile):
            back[y] = tile

        finish_solve(
            tables, spec, back_coef_ref, back_jump_ref, base_ref, y_back_ref, x_back_ref,
            z_back_ref, give_ref, use,
        )

    rates = closure(adv_ref, w_in, bias, w_out, feats, activity, hidden)
    for i, ref in enumerate((heat_ref, salt_ref, w_field_ref)):
        flat[i] = ref[0].reshape(levels * SUB, east)
    level = lax.broadcasted_iota(jnp.int32, (levels, east), 0)
    depths = dep_ref[pl.ds(pl.multiple_of(step * SUB, SUB), SUB), :]
    sources = []
    for k in range(SUB):
        lanes = slice(k * east, (k + 1) * east)
        depth = depths[k : k + 1]
        wet = level < depth
        rate = rates[:, lanes]
        flow = jnp.where(level + 1 < depth, TIME_STEP, 0.0) * rate
        slope = -vertical_change(jnp.where(wet, back[step * SUB + k], 0.0))
        mixed = []
        total = jnp.zeros((levels, east), f32)
        for i, share in ((0, THERMAL), (1, -HALINE)):
            value = adv_ref[2 + i, k]
            drop = pltpu.roll(value, levels - 1, 0) - value
            grad = flat[i, pl.ds(k, levels, stride=SUB), :] + share * slope
            grad = jnp.where(wet, grad, 0.0)
            total = total + (grad - pltpu.roll(grad, levels - 1, 0)) * drop
            flux = flow * drop
            value = jnp.where(wet, value + (flux - pltpu.roll(flux, 1, 0)), 0.0)
            mixed.append(value)
            mixed_ref[i, k] = value
        grads[:, lanes] = (total * flow * (1.0 - rate * (1.0 / RATE_MAX))).astype(bf16)
        rise = jnp.where(wet, flat[2, pl.ds(k, levels, stride=SUB), :], 0.0)
        density = THERMAL * mixed[0] - HALINE * mixed[1] - rise * (1.0 / TIME_STEP)
        source = vertical_change(density) - spread_ref[k] * (1.0 / TIME_STEP)
        sources.append(jnp.where(wet, source, 0.0))
    tile = from_left(z_ref[...], jnp.concatenate(sources, 1))
    for k in range(SUB):
        spec[step * SUB + k] = tile[:, k * east : (k + 1) * east]

    over = (((1,), (1,)), ((), ()))
    grad = grads[...]
    g_out_ref[...] += lax.dot_general(hidden[...], grad, over, preferred_element_type=f32)
    pre = mul(w[:, :levels].astype(bf16), grad)
    for k in range(SUB):
        lanes = slice(k * east, (k + 1) * east)
        value = activity[:, lanes]
        value = pre[:, lanes] * (1.0 - value * value)
        g_bias_ref[...] += value
        hidden[:, lanes] = value.astype(bf16)
    g_in_ref[...] += lax.dot_general(feats[...], hidden[...], over, preferred_element_type=f32)

    @pl.when(step == north // SUB - 1)
    def _():
        block_solve(tables, spec, base_ref, x_ref, y_ref, coef_ref)
        block_edges(tables, coef_ref, take_ref, sides)
        inputs, width = g_in_ref.shape
        for k in range(width // east):
            total_ref[k * inputs : (k + 1) * inputs, :] = g_in_ref[:, k * east : (k + 1) * east]
        sums = jnp.sum(g_bias_ref[...], 1, keepdims=True)
        last = jnp.concatenate([g_out_ref[...], jnp.broadcast_to(sums, g_out_ref.shape)], 1)
        at = inputs * width // east
        for k in range(0, width, east):
            total_ref[at + k : at + k + east, :] = last[k : k + east].T
        if total_ref.shape[0] > at + width:
            total_ref[at + width :, :] = jnp.zeros_like(total_ref[at + width :, :])
        mine = tables.share * PARTS
        each = send_ref.shape[0] // tables.count
        for part in range(mine):
            send_ref[pl.ds(part, tables.count, stride=each), :] = sides[
                pl.ds(part, tables.count, stride=mine), :
            ]
        more = each - mine
        for d in range(tables.count):
            send_ref[d * each + mine : (d + 1) * each, :] = total_ref[d * more : (d + 1) * more, :]


def column(
    tables, dep, adv, spread, fields, cotangent, in_weight, in_bias, out_weight, coef, jumps
):
    levels, north, east = tables.levels, tables.north, tables.east
    inputs, hidden = in_weight.shape
    f32, bf16 = jnp.float32, jnp.bfloat16
    consts = (
        in_weight, in_bias, out_weight, coef, jumps,
        tables.z_forward, tables.base, tables.x_forward, tables.y_forward, tables.take,
        tables.y_back, tables.x_back, tables.z_back, tables.give,
    )
    mixed = jax.ShapeDtypeStruct((2, north, levels, east), f32)
    coef, edge = solve_shapes(tables)
    rows = inputs * hidden // east + hidden
    assert 2 * levels == east
    rows = -(-rows // tables.count) * tables.count
    send = jax.ShapeDtypeStruct((edge.shape[0] + rows, east), f32)
    lanes = SUB * east
    field = lambda f: pl.BlockSpec((1, levels, SUB, east), lambda k: (f, 0, k, 0))
    return pl.pallas_call(
        functools.partial(column_kernel, tables),
        grid=(north // SUB,),
        in_specs=[
            whole_spec(dep),
            pl.BlockSpec((len(TRACERS), SUB, levels, east), lambda k: (0, k, 0, 0)),
            pl.BlockSpec((SUB, levels, east), lambda k: (k, 0, 0)),
            field(2),
            field(3),
            field(4),
            *(whole_spec(a) for a in consts),
        ],
        out_specs=[
            pl.BlockSpec((2, SUB, levels, east), lambda k: (0, k, 0, 0)),
            whole_spec(coef),
            whole_spec(send),
        ],
        out_shape=[mixed, coef, send],
        scratch_shapes=[
            pltpu.VMEM(coef.shape, f32),
            pltpu.VMEM(coef.shape, f32),
            pltpu.VMEM((inputs, lanes), bf16),
            pltpu.VMEM((hidden, lanes), f32),
            pltpu.VMEM((hidden, lanes), bf16),
            pltpu.VMEM((levels, lanes), bf16),
            pltpu.VMEM((3, levels * SUB, east), f32),
            pltpu.VMEM(edge.shape, f32),
            pltpu.VMEM((rows, east), f32),
            pltpu.VMEM((hidden, inputs), bf16),
            pltpu.VMEM((hidden, east), f32),
            pltpu.VMEM((hidden, east), f32),
            pltpu.VMEM((levels, hidden), bf16),
            pltpu.VMEM((inputs, hidden), f32),
            pltpu.VMEM((hidden, east), f32),
            pltpu.VMEM((hidden, levels), f32),
        ],
        compiler_params=call_params(),
    )(dep, adv, spread, fields, cotangent, cotangent, *consts)


def gather_kernel(adv_ref, mixed_ref, after_ref, new_ref, flat):
    del after_ref
    levels, east = adv_ref.shape[2:]
    for f, (ref, i) in zip(TRACERS, ((adv_ref, 0), (adv_ref, 1), (mixed_ref, 0), (mixed_ref, 1))):
        for k in range(SUB):
            flat[f, pl.ds(k, levels, stride=SUB), :] = ref[i, k]
        new_ref[f] = flat[f].reshape(levels, SUB, east)


def gather_fields(adv, mixed, after):
    _, north, levels, east = adv.shape
    block = pl.BlockSpec((2, SUB, levels, east), lambda k: (0, k, 0, 0))
    return pl.pallas_call(
        gather_kernel,
        grid=(north // SUB,),
        in_specs=[block, block, pl.BlockSpec(memory_space=pl.ANY)],
        out_specs=pl.BlockSpec((FIELDS, levels, SUB, east), lambda k: (0, 0, k, 0)),
        out_shape=jax.ShapeDtypeStruct((FIELDS, levels, north, east), jnp.float32),
        scratch_shapes=[pltpu.VMEM((FIELDS, levels * SUB, east), jnp.float32)],
        compiler_params=call_params(61 << 20),
    )(adv, mixed, after)


def solve_consts(tables):
    return (tables.base, tables.y_back, tables.x_back, tables.z_back, tables.give)


def pressure_kernel(
    tables, dep_ref, w_ref, new_ref, coef_ref, jump_ref, base_ref, y_ref, x_ref, z_ref, give_ref,
    pressure_ref, out_ref, spec, jumps,
):
    north, east, levels = tables.north, tables.east, tables.levels
    mine = tables.share * PARTS
    each = jump_ref.shape[0] // tables.count
    for part in range(mine):
        jumps[pl.ds(part, tables.count, stride=mine), :] = jump_ref[
            pl.ds(part, tables.count, stride=each), :
        ]
    level = lax.broadcasted_iota(jnp.int32, (levels, east), 0)

    def use(y, tile):
        pressure_ref[pl.ds(y, levels, stride=north), :] = tile
        value = w_ref[0, y] - TIME_STEP * vertical_change(tile)
        value = jnp.where(level < dep_ref[y : y + 1, :], value, 0.0)
        out_ref[0, pl.ds(y, levels, stride=north), :] = value

    finish_solve(
        tables, spec, coef_ref, jumps, base_ref, y_ref, x_ref, z_ref, give_ref, use
    )


def pressure_finish(tables, dep, w, new, coef, jumps):
    levels, north, east = tables.levels, tables.north, tables.east
    consts = solve_consts(tables)
    flat = jax.ShapeDtypeStruct((levels * north, east), jnp.float32)
    pressure, new = pl.pallas_call(
        functools.partial(pressure_kernel, tables),
        grid=(1,),
        in_specs=[
            whole_spec(dep),
            whole_spec(w),
            pl.BlockSpec(memory_space=pl.ANY),
            whole_spec(coef),
            whole_spec(jumps),
            *(whole_spec(a) for a in consts),
        ],
        out_specs=[
            whole_spec(flat),
            pl.BlockSpec((1, levels * north, east), lambda k: (2, 0, 0)),
        ],
        out_shape=[flat, jax.ShapeDtypeStruct((FIELDS, levels * north, east), jnp.float32)],
        input_output_aliases={2: 1},
        scratch_shapes=[
            pltpu.VMEM(coef.shape, jnp.float32),
            pltpu.VMEM((tables.share * tables.count * PARTS, east), jnp.float32),
        ],
        compiler_params=call_params(44 << 20),
    )(dep, w, new.reshape(FIELDS, levels * north, east), coef, jumps, *consts)
    return pressure.reshape(levels, north, east), new.reshape(FIELDS, levels, north, east)


def split_kernel(skip, count, sums_ref, in_ref, bias_ref, out_ref, flat):
    inputs, width = in_ref.shape
    east = sums_ref.shape[1]
    each = sums_ref.shape[0] // count
    more = each - skip
    for d in range(count):
        flat[d * more : (d + 1) * more, :] = sums_ref[d * each + skip : (d + 1) * each, :]
    wide = inputs * width // east
    for k in range(width // east):
        lanes = slice(k * east, (k + 1) * east)
        in_ref[:, lanes] = flat[k * inputs : (k + 1) * inputs, :]
        at = wide + k * east
        out_ref[:, lanes] = flat[at : at + out_ref.shape[0], :]
        bias_ref[:, lanes] = flat[at + east // 2 : at + east // 2 + 1, :]


def split_sums(tables, sums, inputs, hidden, outputs):
    skip = tables.share * PARTS
    rows = sums.shape[0] - skip * tables.count
    shapes = [
        jax.ShapeDtypeStruct(shape, jnp.float32)
        for shape in ((inputs, hidden), (1, hidden), (outputs, hidden))
    ]
    g_in, g_bias, g_out = pl.pallas_call(
        functools.partial(split_kernel, skip, tables.count),
        grid=(1,),
        in_specs=[whole_spec(sums)],
        out_specs=[whole_spec(a) for a in shapes],
        out_shape=shapes,
        scratch_shapes=[pltpu.VMEM((rows, tables.east), jnp.float32)],
        compiler_params=call_params(),
    )(sums)
    return g_in, g_bias.reshape(hidden), g_out.T


def per_device(fields, cotangent, ocean_mask, depth_levels, in_weight, in_bias, out_weight):
    _, levels, north, east = fields.shape
    tables = Tables(levels, north, east, lax.axis_size("rows"), lax.axis_size("cols"))
    inputs, hidden = in_weight.shape
    outputs = out_weight.shape[1]
    in_bias = in_bias.reshape(1, hidden)
    out_weight = out_weight.T
    steps = levels // SUB
    dep, *edges = advance_edges(fields, ocean_mask, depth_levels)
    back_coef = adjoint_local(tables, cotangent, dep)
    back_edges = adjoint_edges(tables, back_coef, edges[0], edges[1])
    half = advect(fields, dep, TRACERS, edges, (0, steps // 2), back_edges)
    back_jumps = interface(tables, exchange(back_edges), 56 << 20, half[1])
    adv, spread = advect(fields, dep, TRACERS, edges, (steps // 2, steps), back_jumps, half)
    mixed, coef, send = column(
        tables, dep, adv, spread, fields, cotangent, in_weight, in_bias, out_weight,
        back_coef, exchange(back_jumps),
    )
    received = exchange(send)
    w = advect(fields, dep, (2,), edges, (0, steps), coef)[0]
    new = gather_fields(adv, mixed, coef)
    jumps = exchange(interface(tables, received, VMEM_LIMIT, w, new))
    pressure, new_fields = pressure_finish(tables, dep, w, new, coef, jumps)
    return (new_fields, pressure, *split_sums(tables, jumps, inputs, hidden, outputs))


def solution(mesh):
    in_specs = (
        P(None, None, "cols", "rows"),
        P(None, None, "cols", "rows"),
        P("cols", "rows"),
        P("cols", "rows"),
        P(),
        P(),
        P(),
    )
    out_specs = (P(None, None, "cols", "rows"), P(None, "cols", "rows"), P(), P(), P())
    return jax.shard_map(
        per_device, mesh=mesh, in_specs=in_specs, out_specs=out_specs, check_vma=False
    )
```

```python
import functools

import jax
import jax.numpy as jnp
import numpy as np
from jax import lax
from jax.experimental import pallas as pl
from jax.experimental.pallas import tpu as pltpu
from jax.sharding import PartitionSpec as P

TIME_STEP = 0.2
RATE_MAX = 2.0
THERMAL = 0.5
HALINE = 0.5
SPECTRAL_SHIFT = 0.001
WENO_EPS = 1e-06
HALO = 3
FIELDS = 5
SUB = 8
PIECES = 4


def spread_rows(rows, b):
    east = rows.shape[1]
    ys = east // SUB
    return jnp.concatenate(
        [jnp.broadcast_to(rows[y : y + 1], (SUB, east)) for y in range(b * ys, (b + 1) * ys)], 0
    )


def pack_kernel(mask_ref, depth_ref, *refs):
    field_refs, refs = refs[:PIECES], refs[PIECES:]
    dep_ref, xfirst_ref, xlast_ref, yfirst_ref, ylast_ref = refs
    field = pl.program_id(0)
    north, east = dep_ref.shape
    some = field_refs[0].shape[1] // north
    levels = PIECES * some
    ys = east // SUB
    halves = north // ys
    blocks = levels // SUB * halves
    dep = jnp.where(mask_ref[...] == 1, depth_ref[...], 0)
    dep_ref[...] = dep
    first_levels = lax.broadcasted_iota(jnp.int32, (SUB, east), 0)
    for t in range(blocks):
        low, start = t // halves * SUB, t % halves * ys
        piece, at = divmod(low, some)
        tiles = []
        for y in range(start, start + ys):
            value = field_refs[piece][0, pl.ds(at * north + y, SUB, stride=north), :]
            tiles.append(jnp.where(first_levels + low < dep[y : y + 1], value, 0.0))
        turned = jnp.concatenate(tiles, 0).T
        row = field * blocks + t
        for s in range(HALO):
            xfirst_ref[s, pl.ds(row, 1), :] = turned[s : s + 1]
            xlast_ref[s, pl.ds(row, 1), :] = turned[east - HALO + s : east - HALO + s + 1]
    for s, piece in [(s, piece) for s in range(HALO) for piece in range(PIECES)]:
        level = lax.broadcasted_iota(jnp.int32, (some, east), 0) + piece * some
        at = pl.multiple_of((field * HALO + s) * levels + piece * some, SUB)
        low, high = s, north - HALO + s
        first = field_refs[piece][0, pl.ds(low, some, stride=north), :]
        last = field_refs[piece][0, pl.ds(high, some, stride=north), :]
        yfirst_ref[pl.ds(at, some), :] = jnp.where(level < dep[low : low + 1], first, 0.0)
        ylast_ref[pl.ds(at, some), :] = jnp.where(level < dep[high : high + 1], last, 0.0)

    @pl.when(field == 0)
    def _():
        depths = dep.astype(jnp.float32)
        end = FIELDS * HALO * levels
        yfirst_ref[end:, :] = jnp.broadcast_to(depths[:1], (SUB, east))
        ylast_ref[end:, :] = jnp.broadcast_to(depths[north - 1 :], (SUB, east))
        for s in range(HALO):
            xfirst_ref[s, FIELDS * blocks :, :] = jnp.zeros((SUB, east), jnp.float32)
            xlast_ref[s, FIELDS * blocks :, :] = jnp.zeros((SUB, east), jnp.float32)
        for b in range(halves):
            turned = spread_rows(depths, b).T
            row = FIELDS * blocks + b
            for s in range(HALO):
                xfirst_ref[s, row : row + 1, :] = turned[s : s + 1]
                xlast_ref[s, row : row + 1, :] = turned[east - HALO + s : east - HALO + s + 1]


def pack_edges(fields, mask, depth):
    _, levels, north, east = fields.shape
    rows = FIELDS * levels * north // east + SUB
    x_shape = jax.ShapeDtypeStruct((HALO, rows, east), jnp.float32)
    y_shape = jax.ShapeDtypeStruct((FIELDS * HALO * levels + SUB, east), jnp.float32)
    whole = lambda shape: pl.BlockSpec(shape.shape, lambda f: (0,) * len(shape.shape))
    return pl.pallas_call(
        pack_kernel,
        grid=(FIELDS,),
        in_specs=[
            whole(mask),
            whole(depth),
            *(
                pl.BlockSpec((1, levels * north // PIECES, east), lambda f, p=p: (f, p, 0))
                for p in range(PIECES)
            ),
        ],
        out_specs=[whole(mask), whole(x_shape), whole(x_shape), whole(y_shape), whole(y_shape)],
        out_shape=[jax.ShapeDtypeStruct(mask.shape, jnp.int32), x_shape, x_shape, y_shape, y_shape],
        compiler_params=pltpu.CompilerParams(vmem_limit_bytes=61 << 20),
    )(mask, depth, *(fields.reshape(FIELDS, levels * north, east) for _ in range(PIECES)))


def face_flux(slopes, left, right, speed, share):
    dm2, dm1, d0, dp1, dp2 = slopes
    ahead = speed > 0.0
    e1 = jnp.where(ahead, dm2, dp2)
    e2 = jnp.where(ahead, dm1, dp1)
    e4 = jnp.where(ahead, dp1, dm1)
    near = jnp.where(ahead, left, right)
    bend0, bend1, bend2 = e2 - e1, d0 - e2, e4 - d0
    tilt0, tilt1, tilt2 = bend0 + (e2 + e2), e2 + d0, bend2 - (d0 + d0)
    rough0 = bend0 * bend0 * (13.0 / 3.0) + (tilt0 * tilt0 + 4.0 * WENO_EPS)
    rough1 = bend1 * bend1 * (13.0 / 3.0) + (tilt1 * tilt1 + 4.0 * WENO_EPS)
    rough2 = bend2 * bend2 * (13.0 / 3.0) + (tilt2 * tilt2 + 4.0 * WENO_EPS)
    pair0, pair1, pair2 = rough1 * rough2, rough0 * rough2, rough0 * rough1
    g0, g1, g2 = pair0 * pair0, 6.0 * (pair1 * pair1), 3.0 * (pair2 * pair2)
    total = g0 * (tilt0 + (bend0 + e2)) + g1 * (tilt1 + d0) + g2 * (d0 - tilt2)
    return speed * near + share * (total * pltpu.reciprocal(g0 + g1 + g2, approx=True))


def advect_kernel(
    tracers, staged, begin, filled, dep_ref, *refs,
):
    field_refs, refs = refs[: len(staged)], refs[len(staged) :]
    xlo_ref, xhi_ref, ylo_ref, yhi_ref = refs[:4]
    refs = refs[5 + filled :]
    adv_ref = refs[0]
    spread_ref = refs[1] if len(tracers) > 1 else None
    (
        deep, both, lines, slopes, fluxes, cells, wets, su, su6, sv, sv6, sides,
    ) = refs[-12:]
    step = pl.program_id(0) + begin
    north, east = dep_ref.shape
    ys = east // SUB
    blocks = north // ys
    all_blocks = (xlo_ref.shape[1] - SUB) // FIELDS
    levels = all_blocks // blocks * SUB
    depth_row = FIELDS * all_blocks
    depth_end = FIELDS * HALO * levels
    faces = range(0, east + SUB, SUB)
    first_level = step * SUB

    @pl.when(step == begin)
    def _():
        depths = dep_ref[...].astype(jnp.float32)
        for b in range(blocks):
            row = depth_row + b
            deep[SUB : SUB + east, :] = spread_rows(depths, b).T
            deep[SUB - 1 : SUB, :] = xlo_ref[HALO - 1, row : row + 1, :]
            deep[SUB + east : SUB + east + 1, :] = xhi_ref[0, row : row + 1, :]
            both[b, :east, :] = jnp.minimum(
                deep[SUB - 1 : SUB - 1 + east, :], deep[SUB : SUB + east, :]
            )
            both[b, east : east + 1, :] = jnp.minimum(
                deep[SUB + east - 1 : SUB + east, :], deep[SUB + east : SUB + east + 1, :]
            )

    level = (lax.broadcasted_iota(jnp.int32, (SUB, east), 0) + first_level).astype(jnp.float32)
    height = lax.broadcasted_iota(jnp.int32, (SUB, east), 1) % SUB + first_level
    height = height.astype(jnp.float32)
    depths = dep_ref[...].astype(jnp.float32)
    wets[0] = (level < ylo_ref[depth_end : depth_end + 1, :]).astype(jnp.float32)
    wets[north + 1] = (level < yhi_ref[depth_end : depth_end + 1, :]).astype(jnp.float32)
    for y in range(north):
        wets[y + 1] = (level < depths[y : y + 1]).astype(jnp.float32)

    for slot, f in enumerate(staged):
        field = field_refs[slot]
        for s in range(HALO):
            at = pl.multiple_of((f * HALO + s) * levels + first_level, SUB)
            cells[slot, s] = ylo_ref[pl.ds(at, SUB), :]
            cells[slot, north + HALO + s] = yhi_ref[pl.ds(at, SUB), :]
        for y in range(north):
            cells[slot, y + HALO] = field[0, pl.ds(y, SUB, stride=north), :] * wets[y + 1]
        for b in range(blocks):
            row = f * all_blocks + step * blocks + b
            for s in range(HALO):
                lines[slot, b, SUB - HALO + s : SUB - HALO + s + 1, :] = xlo_ref[
                    s, pl.ds(row, 1), :
                ]
                lines[slot, b, SUB + east + s : SUB + east + s + 1, :] = xhi_ref[
                    s, pl.ds(row, 1), :
                ]
            tile = cells[slot, HALO + b * ys : HALO + (b + 1) * ys].reshape(east, east)
            lines[slot, b, SUB : SUB + east, :] = tile.T

    for b in range(blocks):
        for r in faces:
            speed = (0.5 * TIME_STEP) * (
                lines[0, b, SUB + r - 1 : 2 * SUB + r - 1, :] + lines[0, b, SUB + r : 2 * SUB + r, :]
            )
            speed = jnp.where(height < both[b, r : r + SUB, :], speed, 0.0)
            su[b, r : r + SUB, :] = speed
            su6[b, r : r + SUB, :] = jnp.abs(speed) * (1.0 / 6.0)
        if spread_ref is not None:
            change = 0.5 * (
                lines[0, b, SUB + 1 : SUB + 1 + east, :] - lines[0, b, SUB - 1 : SUB - 1 + east, :]
            )
            sides[b * east : (b + 1) * east, :] = change.T
    if spread_ref is not None:
        for y in range(north):
            spread_ref[y] = sides[y * SUB : (y + 1) * SUB, :] + 0.5 * (
                cells[1, y + HALO + 1] - cells[1, y + HALO - 1]
            )
    for y in range(north + 1):
        speed = (0.5 * TIME_STEP) * (cells[1, y + HALO - 1] + cells[1, y + HALO])
        speed = speed * (wets[y] * wets[y + 1])
        sv[y] = speed
        sv6[y] = jnp.abs(speed) * (1.0 / 6.0)

    first = len(staged) - len(tracers)

    def advance_field(f):
        for b in range(blocks):
            for r in range(0, east + 2 * SUB, SUB):
                ahead = lines[f, b, r + 1 : r + 1 + SUB, :]
                slopes[b, r : r + SUB, :] = ahead - lines[f, b, r : r + SUB, :]
            for r in faces:
                at = SUB + r
                near = [slopes[b, at + k : at + k + SUB, :] for k in (-3, -2, -1, 0, 1)]
                fluxes[b, r : r + SUB, :] = face_flux(
                    near,
                    lines[f, b, at - 1 : at - 1 + SUB, :],
                    lines[f, b, at : at + SUB, :],
                    su[b, r : r + SUB, :],
                    su6[b, r : r + SUB, :],
                )
            change = fluxes[b, 0:east, :] - fluxes[b, 1 : 1 + east, :]
            sides[b * east : (b + 1) * east, :] = change.T
        line = [cells[f, k] for k in range(5)]
        inclines = [line[k + 1] - line[k] for k in range(4)]
        south = None
        for y in range(north + 1):
            line.append(cells[f, y + 2 * HALO - 1])
            inclines.append(line[-1] - line[-2])
            north_face = face_flux(inclines[-5:], line[-4], line[-3], sv[y], sv6[y])
            if y > 0:
                change = sides[(y - 1) * SUB : y * SUB, :] + (south - north_face)
                adv_ref[f - first, y - 1] = wets[y] * (line[-4] + change)
            south = north_face

    for f in range(first, len(staged)):
        advance_field(f)


def advect(fields, dep, tracers, edges, span, after, filled=()):
    _, levels, north, east = fields.shape
    whole = lambda a: pl.BlockSpec(a.shape, lambda k: (0,) * a.ndim)
    staged = tracers if tracers[0] == 0 else (0, 1, *tracers)
    one = lambda f: pl.BlockSpec((1, SUB * north, east), lambda k: (f, k + span[0], 0))
    f32 = jnp.float32
    blocks = SUB * north // east
    flat = fields.reshape(FIELDS, levels * north, east)
    out_specs = [pl.BlockSpec((len(tracers), north, SUB, east), lambda k: (0, 0, k + span[0], 0))]
    out_shape = [jax.ShapeDtypeStruct((len(tracers), north, levels, east), f32)]
    if tracers[0] == 0:
        out_specs.append(pl.BlockSpec((north, SUB, east), lambda k: (0, k + span[0], 0)))
        out_shape.append(jax.ShapeDtypeStruct((north, levels, east), f32))
    return pl.pallas_call(
        functools.partial(advect_kernel, tracers, staged, span[0], len(filled)),
        grid=(span[1] - span[0],),
        in_specs=[
            whole(dep),
            *(one(f) for f in staged),
            *(whole(a) for a in edges),
            pl.BlockSpec(memory_space=pl.ANY),
            *(pl.BlockSpec(memory_space=pl.ANY) for _ in filled),
        ],
        out_specs=out_specs,
        out_shape=out_shape,
        input_output_aliases={len(staged) + 6 + i: i for i in range(len(filled))},
        scratch_shapes=[
            pltpu.VMEM((east + 2 * SUB, east), f32),
            pltpu.VMEM((blocks, east + SUB, east), f32),
            pltpu.VMEM((len(staged), blocks, east + 3 * SUB, east), f32),
            pltpu.VMEM((blocks, east + 3 * SUB, east), f32),
            pltpu.VMEM((blocks, east + SUB, east), f32),
            pltpu.VMEM((len(staged), north + 2 * HALO, SUB, east), f32),
            pltpu.VMEM((north + 2, SUB, east), f32),
            pltpu.VMEM((blocks, east + SUB, east), f32),
            pltpu.VMEM((blocks, east + SUB, east), f32),
            pltpu.VMEM((north + 1, SUB, east), f32),
            pltpu.VMEM((north + 1, SUB, east), f32),
            pltpu.VMEM((SUB * north, east), f32),
        ],
        compiler_params=pltpu.CompilerParams(vmem_limit_bytes=VMEM_LIMIT),
    )(dep, *(flat for _ in staged), *edges, after, *filled)


def shift_both(axis, first, last):
    count = lax.axis_size(axis)
    forward = [(i, i + 1) for i in range(count - 1)]
    backward = [(i + 1, i) for i in range(count - 1)]
    return lax.ppermute(last, axis, forward), lax.ppermute(first, axis, backward)


def advance_edges(fields, mask, depth):
    dep, xfirst, xlast, yfirst, ylast = pack_edges(fields, mask, depth)
    south_north = shift_both("cols", yfirst, ylast)
    return (dep, *shift_both("rows", xfirst, xlast), *south_north)


AXES = ("rows", "cols")
VMEM_LIMIT = 52 << 20
TRACERS = (0, 1, 3, 4)
PARTS = 4


def dct_table(length):
    freq = np.arange(length)[:, None]
    cells = np.arange(length)[None, :]
    scale = np.where(freq == 0, np.sqrt(1.0 / length), np.sqrt(2.0 / length))
    return scale * np.cos(np.pi * (cells + 0.5) * freq / length)


def eigen_table(length):
    return 2.0 - 2.0 * np.cos(np.pi * np.arange(length) / length)


def halves(table):
    high = table.astype(jnp.bfloat16)
    low = (table - high.astype(np.float64)).astype(jnp.bfloat16)
    return high, low


def right_factor(table):
    high, low = halves(table)
    return np.block([[high, low], [high, np.zeros_like(low)]])


def left_factor(table):
    high, low = halves(table)
    return np.concatenate([high, low], 0)


class Tables:
    def __init__(self, levels, north, east, rows, cols):
        self.levels, self.north, self.east, self.rows, self.cols = levels, north, east, rows, cols
        self.count = rows * cols
        self.share = -(-levels // self.count)
        padded = self.share * self.count
        cz, cy, cx = dct_table(levels), dct_table(north), dct_table(east)
        lz, ly, lx = eigen_table(levels), eigen_table(north), eigen_table(east)
        shift = SPECTRAL_SHIFT + lz
        f32 = np.float32
        eye = np.eye(SUB)
        self.ly = [float(v) for v in ly]
        self.south = [float(v) for v in cy[:, 0]]
        self.north_edge = [float(v) for v in cy[:, -1]]
        self.base = (shift[:, None] + lx[None]).astype(f32)
        self.z_forward, self.z_back = left_factor(cz), left_factor(cz.T)
        self.y_forward = left_factor(np.kron(cy, eye))
        self.y_back = left_factor(np.kron(cy.T, eye))
        self.x_forward, self.x_back = right_factor(cx.T), right_factor(cx)
        edges = np.zeros((2 * north, east))
        edges[:north], edges[north:] = cx[:, 0], cx[:, -1]
        self.take = np.concatenate(halves(edges.T), 1)
        edges[:north], edges[north:] = -cx[:, -1], cx[:, 0]
        give = np.concatenate(halves(edges), 0)
        self.give = np.concatenate([give, give], 0)
        assert 4 * north == east
        lanes = max(east, 2 * north)
        assert lanes == east and cols % SUB == 0
        grid = 1.0 / (shift[:, None, None] + ly[None, :, None] + lx[None, None, :])
        alpha = np.einsum("k,myk->my", cx[:, -1] ** 2, grid)
        beta = np.einsum("k,myk->my", cx[:, -1] * cx[:, 0], grid)
        inner = rows - 1
        near = np.eye(inner, k=1) + np.eye(inner, k=-1)
        system = (1.0 + 2.0 * alpha)[..., None, None] * np.eye(inner) - beta[
            ..., None, None
        ] * near
        inverse = np.linalg.inv(system).transpose(0, 2, 3, 1).reshape(levels, inner**2, north)
        cross = np.zeros((padded, inner**2 + 1, east), f32)
        cross[:levels, : inner**2, :north] = inverse
        cross[:, inner**2] = 1.0
        cross[:levels, inner**2] = shift[:, None]
        self.cross = cross
        all_east = eigen_table(rows * east)
        grid = 1.0 / (shift[:, None, None] + ly[None, :, None] + all_east[None, None, :])
        alpha = np.einsum("y,myk->mk", cy[:, -1] ** 2, grid)
        beta = np.einsum("y,myk->mk", cy[:, -1] * cy[:, 0], grid)
        waves = np.cos(np.pi * np.arange(1, cols) / cols)
        along = np.zeros((padded, cols, rows * east), f32)
        along[:levels, : cols - 1] = 1.0 / (
            1.0 + 2.0 * alpha[:, None] - 2.0 * beta[:, None] * waves[None, :, None]
        )
        self.along = along
        order = np.arange(1, cols)
        sines = np.zeros((cols, cols))
        sines[: cols - 1, : cols - 1] = np.sqrt(2.0 / cols) * np.sin(
            np.pi * np.outer(order, order) / cols
        )
        self.sines = np.kron(np.eye(self.share), sines).astype(f32)
        wide = dct_table(rows * east).reshape(rows * east, rows, east)
        turn = np.einsum("gax,kx->gak", wide, cx).reshape(rows * east, rows * east)
        self.wide_forward = np.stack(halves(turn.T))
        self.wide_back = np.stack(halves(turn))
        both = (ly[:, None] + lx[None]).astype(f32)
        self.strip = np.stack(
            [both, np.broadcast_to(cy[:, -1:], both.shape), np.broadcast_to(cy[:, :1], both.shape)]
        ).astype(f32)
        back = np.full((east, east), 1.0)
        gain = np.zeros((east, east))
        back[:, :north] = back[:, north : 2 * north] = both.T
        gain[:, :north], gain[:, north : 2 * north] = cx[:, -1:], cx[:, :1]
        self.column = np.stack([back, gain]).astype(f32)
        lines = np.zeros((SUB, east), f32)
        lines[0], lines[1] = cx[:, -1], cx[:, 0]
        lines[2, :north] = lines[2, north : 2 * north] = cy[:, -1]
        lines[3, :north] = lines[3, north : 2 * north] = cy[:, 0]
        self.lines = lines


def parts(value):
    high = value.astype(jnp.bfloat16)
    return high, (value - high.astype(jnp.float32)).astype(jnp.bfloat16)


def mul(a, b):
    return jnp.dot(a, b, preferred_element_type=jnp.float32)


def from_left(factor, value):
    rows = factor.shape[0] // 2
    high, low = parts(value)
    both = mul(factor, high)
    return both[:rows] + (both[rows:] + mul(factor[:rows], low))


def from_right(value, factor):
    columns = factor.shape[1] // 2
    both = mul(jnp.concatenate(parts(value), 1), factor)
    return both[:, :columns] + both[:, columns:]


def times(value, high, low):
    first, second = parts(value)
    return mul(first, high) + (mul(second, high) + mul(first, low))


def vertical_change(value):
    levels = value.shape[0]
    level = lax.broadcasted_iota(jnp.int32, value.shape, 0)
    above = jnp.where(level == levels - 1, 0.0, pltpu.roll(value, levels - 1, 0))
    below = jnp.where(level == 0, 0.0, pltpu.roll(value, 1, 0))
    return 0.5 * (above - below)


def pair_of(spec, m, rows):
    return jnp.concatenate(
        [spec[:, at : at + SUB, :].reshape(rows, -1) for at in (m, m + SUB)], 1
    )


def block_solve(tables, spec, base_ref, x_ref, y_ref, coef_ref):
    north, east, levels = tables.north, tables.east, tables.levels
    for y in range(0, north, 4):
        tile = spec[y : y + 4].reshape(4 * levels, east)
        spec[y : y + 4] = from_right(tile, x_ref[...]).reshape(4, levels, east)
    for m in range(0, levels, 2 * SUB):
        both = from_left(y_ref[...], pair_of(spec, m, north * SUB))
        for i in range(2):
            at = m + i * SUB
            base = base_ref[at : at + SUB, :]
            tile = both[:, i * east : (i + 1) * east]
            for k in range(north):
                coef_ref[k, at : at + SUB, :] = tile[k * SUB : (k + 1) * SUB] / (
                    base + tables.ly[k]
                )


def block_edges(tables, coef_ref, take_ref, edge_ref):
    north, east, levels = tables.north, tables.east, tables.levels
    zero = jnp.zeros((levels, east), jnp.float32)
    even = odd = total = rest = zero
    lane = lax.broadcasted_iota(jnp.int32, (levels, east), 1)
    place = lane % north
    for k in range(0, north, 4):
        group = coef_ref[k : k + 4]
        high, low = parts(group.reshape(4 * levels, east))
        high, low = mul(high, take_ref[...]), mul(low, take_ref[...])
        for i in range(4):
            value = tables.south[k + i] * group[i]
            if i % 2:
                odd = odd + value
            else:
                even = even + value
            mine = place == k + i
            total = total + jnp.where(mine, high[i * levels : (i + 1) * levels], 0.0)
            rest = rest + jnp.where(mine, low[i * levels : (i + 1) * levels], 0.0)
    total = total + pltpu.roll(total, east // 2, 1) + rest
    sides = (jnp.where(lane < 2 * north, total, 0.0), even + odd, even - odd, zero)
    for part in range(PARTS):
        edge_ref[pl.ds(part, levels, stride=PARTS), :] = sides[part]
    if edge_ref.shape[0] > levels * PARTS:
        edge_ref[levels * PARTS :, :] = jnp.zeros_like(edge_ref[levels * PARTS :, :])


def finish_solve(tables, spec, coef_ref, jump_ref, base_ref, y_ref, x_ref, z_ref, give_ref, use):
    north, east, levels = tables.north, tables.east, tables.levels
    side, ahead, behind = (
        jump_ref[pl.ds(part, levels, stride=PARTS), :] for part in range(PARTS - 1)
    )
    high, low = (half.astype(jnp.float32) for half in parts(side))
    sides = jnp.concatenate([high + pltpu.roll(high, east // 2, 1), low], 1)
    place = lax.broadcasted_iota(jnp.int32, sides.shape, 1) % north
    for k in range(0, north, 4):
        picked = [jnp.where(place == k + i, sides, 0.0).astype(jnp.bfloat16) for i in range(4)]
        change = mul(jnp.concatenate(picked, 0), give_ref[...])
        for i in range(4):
            value = change[i * levels : (i + 1) * levels] + (
                tables.south[k + i] * behind - tables.north_edge[k + i] * ahead
            )
            spec[k + i] = coef_ref[k + i] + value / (base_ref[...] + tables.ly[k + i])
    for m in range(0, levels, 2 * SUB):
        both = from_left(y_ref[...], pair_of(spec, m, north * SUB))
        for i in range(2):
            at = m + i * SUB
            tile = both[:, i * east : (i + 1) * east]
            spec[:, at : at + SUB, :] = tile.reshape(north, SUB, east)
    for y in range(0, north, 4):
        tile = from_right(spec[y : y + 4].reshape(4 * levels, east), x_ref[...])
        tile = jnp.concatenate([tile[k * levels : (k + 1) * levels] for k in range(4)], 1)
        tile = from_left(z_ref[...], tile)
        for k in range(4):
            use(y + k, tile[:, k * east : (k + 1) * east])


def interface_kernel(
    tables, device_ref, edge_ref, cross_ref, along_ref, sines_ref, forward_ref, back_ref,
    strip_ref, column_ref, lines_ref, *rest,
):
    del device_ref
    jump_ref = rest[-1]
    rows, cols, east, north = tables.rows, tables.cols, tables.east, tables.north
    each = edge_ref.shape[0] // tables.count
    mine = tables.share * PARTS
    if each > mine:
        total = edge_ref[mine:each, :]
        for d in range(1, tables.count):
            total = total + edge_ref[d * each + mine : (d + 1) * each, :]
        for d in range(tables.count):
            jump_ref[d * each + mine : (d + 1) * each, :] = total
    share, inner = tables.share, tables.rows - 1
    f32 = jnp.float32
    east_last, east_first = lines_ref[0:1, :], lines_ref[1:2, :]
    north_last, north_first = lines_ref[2:3, :], lines_ref[3:4, :]
    every = lax.Precision.HIGHEST

    def across(m, changes):
        result = []
        for i in range(inner):
            total = jnp.zeros((cols, east), f32)
            for j in range(inner):
                at = i * inner + j
                total = total + cross_ref[m, at : at + 1, :] * changes[j]
            result.append(total)
        return result

    gaps, steps = [], []
    for m in range(share):
        west, south, top = (
            [
                edge_ref[pl.ds(a * cols * each + m * PARTS + part, cols, stride=each), :]
                for a in range(rows)
            ]
            for part in range(PARTS - 1)
        )
        right = [pltpu.roll(tile, east - north, 1) for tile in west]
        gap = [right[i] - west[i + 1] for i in range(inner)]
        gaps.append(gap)
        jumps = jnp.concatenate(across(m, gap), 0)
        shift = cross_ref[m, inner**2 : inner**2 + 1, :]
        inverse = 1.0 / (strip_ref[0] + shift)
        weights = jnp.concatenate([strip_ref[1] * inverse, strip_ref[2] * inverse], 1)
        weights = jnp.concatenate([weights, jnp.zeros((east - north, 2 * east), f32)], 0)
        moved = times(jumps, *parts(weights))
        for a in range(rows):
            for side, at in ((top, 0), (south, east)):
                if a < inner:
                    side[a] = side[a] - east_last * moved[a * cols : (a + 1) * cols, at : at + east]
                if a > 0:
                    side[a] = side[a] + east_first * moved[
                        (a - 1) * cols : a * cols, at : at + east
                    ]
        steps.append(
            jnp.concatenate([top[a] - pltpu.roll(south[a], cols - 1, 0) for a in range(rows)], 1)
        )
    step = jnp.concatenate(steps, 0)
    waves = times(step, forward_ref[0], forward_ref[1])
    waves = jnp.dot(sines_ref[...], waves, precision=every, preferred_element_type=f32)
    waves = waves * jnp.concatenate([along_ref[m] for m in range(share)], 0)
    waves = jnp.dot(sines_ref[...], waves, precision=every, preferred_element_type=f32)
    step = times(waves, back_ref[0], back_ref[1])
    for m in range(share):
        shift = cross_ref[m, inner**2 : inner**2 + 1, :]
        here = step[m * cols : (m + 1) * cols]
        tall = [here[:, a * east : (a + 1) * east] for a in range(rows)]
        weights = column_ref[1] / (column_ref[0] + shift)
        moved = times(jnp.concatenate(tall, 0), *parts(weights))
        sides = []
        for a in range(rows):
            tile = moved[a * cols : (a + 1) * cols]
            sides.append(north_last * tile - north_first * pltpu.roll(tile, 1, 0))
        gap = [
            gaps[m][i] - (sides[i] - pltpu.roll(sides[i + 1], east - north, 1))
            for i in range(inner)
        ]
        jumps = across(m, gap)
        for a in range(rows):
            tile = jnp.zeros((cols, east), f32)
            if a < inner:
                tile = tile + jumps[a]
            if a > 0:
                tile = tile + pltpu.roll(jumps[a - 1], north, 1)
            out = (tile, tall[a], pltpu.roll(tall[a], 1, 0), jnp.zeros_like(tile))
            for part in range(PARTS):
                at = a * cols * each + m * PARTS + part
                jump_ref[pl.ds(at, cols, stride=each), :] = out[part]


def whole_spec(array):
    shape = tuple(array.shape)
    return pl.BlockSpec(shape, lambda *_: (0,) * len(shape))


def call_params(limit=VMEM_LIMIT):
    return pltpu.CompilerParams(vmem_limit_bytes=limit)


def exchange(block):
    return lax.all_to_all(block, AXES, split_axis=0, concat_axis=0, tiled=True)


def interface(tables, received, limit, *after):
    device = lax.axis_index("rows") * lax.axis_size("cols") + lax.axis_index("cols")
    operands = (
        received, tables.cross, tables.along, tables.sines, tables.wide_forward, tables.wide_back,
        tables.strip, tables.column, tables.lines,
    )
    specs = [whole_spec(a) for a in operands]
    for at in (1, 2):
        shape = (tables.share, *operands[at].shape[1:])
        specs[at] = pl.BlockSpec(shape, lambda k, mine: (mine[0], 0, 0))
    return pl.pallas_call(
        functools.partial(interface_kernel, tables),
        grid_spec=pltpu.PrefetchScalarGridSpec(
            num_scalar_prefetch=1,
            grid=(1,),
            in_specs=[*specs, *(pl.BlockSpec(memory_space=pl.ANY) for _ in after)],
            out_specs=whole_spec(received),
        ),
        out_shape=jax.ShapeDtypeStruct(received.shape, jnp.float32),
        compiler_params=call_params(limit),
    )(device.astype(jnp.int32).reshape(1), *operands, *after)


def adjoint_kernel(
    tables, dep_ref, cot_ref, z_ref, base_ref, x_ref, y_ref, coef_ref, spec
):
    north, east, levels = tables.north, tables.east, tables.levels
    level = lax.broadcasted_iota(jnp.int32, (levels, east), 0)
    for y in range(0, north, 4):
        tiles = []
        for k in range(y, y + 4):
            value = cot_ref[0, pl.ds(k, levels, stride=north), :]
            value = jnp.where(level < dep_ref[k : k + 1, :], value, 0.0)
            tiles.append(TIME_STEP * vertical_change(value))
        tile = from_left(z_ref[...], jnp.concatenate(tiles, 1))
        for k in range(4):
            spec[y + k] = tile[:, k * east : (k + 1) * east]
    block_solve(tables, spec, base_ref, x_ref, y_ref, coef_ref)


def solve_shapes(tables):
    coef = jax.ShapeDtypeStruct((tables.north, tables.levels, tables.east), jnp.float32)
    edge = jax.ShapeDtypeStruct((tables.share * tables.count * PARTS, tables.east), jnp.float32)
    return [coef, edge]


def adjoint_local(tables, cotangent, dep):
    levels, north, east = tables.levels, tables.north, tables.east
    consts = (tables.z_forward, tables.base, tables.x_forward, tables.y_forward)
    coef = solve_shapes(tables)[0]
    return pl.pallas_call(
        functools.partial(adjoint_kernel, tables),
        grid=(1,),
        in_specs=[
            whole_spec(dep),
            pl.BlockSpec((1, levels * north, east), lambda k: (2, 0, 0)),
            *(whole_spec(a) for a in consts),
        ],
        out_specs=whole_spec(coef),
        out_shape=coef,
        scratch_shapes=[pltpu.VMEM(coef.shape, jnp.float32)],
        compiler_params=call_params(52 << 20),
    )(dep, cotangent.reshape(FIELDS, levels * north, east), *consts)


def edges_kernel(tables, coef_ref, take_ref, *rest):
    block_edges(tables, coef_ref, take_ref, rest[-1])


def adjoint_edges(tables, coef, *after):
    edge = solve_shapes(tables)[1]
    return pl.pallas_call(
        functools.partial(edges_kernel, tables),
        grid=(1,),
        in_specs=[
            whole_spec(coef),
            whole_spec(tables.take),
            *(pl.BlockSpec(memory_space=pl.ANY) for _ in after),
        ],
        out_specs=whole_spec(edge),
        out_shape=edge,
        compiler_params=call_params(),
    )(coef, tables.take, *after)


def set_weights(w_in_ref, bias_ref, w_ref, w_in, bias, w, w_out, levels):
    inputs, width = w_in_ref.shape
    east = bias.shape[1]
    w_in[...] = w_in_ref[...].astype(jnp.float32).T.astype(jnp.bfloat16)
    bias[...] = jnp.broadcast_to(bias_ref[...], (east, width)).T
    for k in range(0, width, east):
        w[k : k + east, :] = jnp.zeros((east, east), jnp.float32)
        w[k : k + levels - 1, :] = w_ref[:, k : k + east].astype(jnp.float32)
        tile = w[k : k + east, :]
        w_out[:, k : k + east] = tile[:levels].astype(jnp.bfloat16)
        w[k : k + east, :] = tile.T


def closure(adv_ref, w_in, bias, w_out, feats, activity, hidden):
    levels, east = adv_ref.shape[2:]
    for k in range(SUB):
        for f in range(len(TRACERS)):
            feats[f * levels : (f + 1) * levels, k * east : (k + 1) * east] = adv_ref[f, k].astype(
                jnp.bfloat16
            )
    before = mul(w_in[...], feats[...])
    for k in range(SUB):
        lanes = slice(k * east, (k + 1) * east)
        value = jnp.tanh(before[:, lanes] + bias[...])
        if activity is not None:
            activity[:, lanes] = value
        hidden[:, lanes] = value.astype(jnp.bfloat16)
    return RATE_MAX * jax.nn.sigmoid(mul(w_out[...], hidden[...]))


def column_kernel(
    tables, dep_ref, adv_ref, spread_ref, w_field_ref, heat_ref, salt_ref,
    w_in_ref, bias_ref, w_ref, back_coef_ref, back_jump_ref,
    z_ref, base_ref, x_ref, y_ref, take_ref, y_back_ref, x_back_ref, z_back_ref, give_ref,
    mixed_ref, coef_ref, send_ref,
    spec, back, feats, activity, hidden, grads, flat, sides, total_ref,
    w_in, bias, w, w_out, g_in_ref, g_bias_ref, g_out_ref,
):
    step = pl.program_id(0)
    north, east, levels = tables.north, tables.east, tables.levels
    f32, bf16 = jnp.float32, jnp.bfloat16

    @pl.when(step == 0)
    def _():
        set_weights(w_in_ref, bias_ref, w_ref, w_in, bias, w, w_out, levels)
        g_in_ref[...] = jnp.zeros_like(g_in_ref)
        g_out_ref[...] = jnp.zeros_like(g_out_ref)
        g_bias_ref[...] = jnp.zeros_like(g_bias_ref)

        def use(y, tile):
            back[y] = tile

        finish_solve(
            tables, spec, back_coef_ref, back_jump_ref, base_ref, y_back_ref, x_back_ref,
            z_back_ref, give_ref, use,
        )

    rates = closure(adv_ref, w_in, bias, w_out, feats, activity, hidden)
    for i, ref in enumerate((heat_ref, salt_ref, w_field_ref)):
        flat[i] = ref[0].reshape(levels * SUB, east)
    level = lax.broadcasted_iota(jnp.int32, (levels, east), 0)
    depths = dep_ref[pl.ds(pl.multiple_of(step * SUB, SUB), SUB), :]
    sources = []
    for k in range(SUB):
        lanes = slice(k * east, (k + 1) * east)
        depth = depths[k : k + 1]
        wet = level < depth
        rate = rates[:, lanes]
        flow = jnp.where(level + 1 < depth, TIME_STEP, 0.0) * rate
        slope = -vertical_change(jnp.where(wet, back[step * SUB + k], 0.0))
        mixed = []
        total = jnp.zeros((levels, east), f32)
        for i, share in ((0, THERMAL), (1, -HALINE)):
            value = adv_ref[2 + i, k]
            drop = pltpu.roll(value, levels - 1, 0) - value
            grad = flat[i, pl.ds(k, levels, stride=SUB), :] + share * slope
            grad = jnp.where(wet, grad, 0.0)
            total = total + (grad - pltpu.roll(grad, levels - 1, 0)) * drop
            flux = flow * drop
            value = jnp.where(wet, value + (flux - pltpu.roll(flux, 1, 0)), 0.0)
            mixed.append(value)
            mixed_ref[i, k] = value
        grads[:, lanes] = (total * flow * (1.0 - rate * (1.0 / RATE_MAX))).astype(bf16)
        rise = jnp.where(wet, flat[2, pl.ds(k, levels, stride=SUB), :], 0.0)
        density = THERMAL * mixed[0] - HALINE * mixed[1] - rise * (1.0 / TIME_STEP)
        source = vertical_change(density) - spread_ref[k] * (1.0 / TIME_STEP)
        sources.append(jnp.where(wet, source, 0.0))
    tile = from_left(z_ref[...], jnp.concatenate(sources, 1))
    for k in range(SUB):
        spec[step * SUB + k] = tile[:, k * east : (k + 1) * east]

    over = (((1,), (1,)), ((), ()))
    grad = grads[...]
    g_out_ref[...] += lax.dot_general(hidden[...], grad, over, preferred_element_type=f32)
    pre = mul(w[:, :levels].astype(bf16), grad)
    for k in range(SUB):
        lanes = slice(k * east, (k + 1) * east)
        value = activity[:, lanes]
        value = pre[:, lanes] * (1.0 - value * value)
        g_bias_ref[...] += value
        hidden[:, lanes] = value.astype(bf16)
    g_in_ref[...] += lax.dot_general(feats[...], hidden[...], over, preferred_element_type=f32)

    @pl.when(step == north // SUB - 1)
    def _():
        block_solve(tables, spec, base_ref, x_ref, y_ref, coef_ref)
        block_edges(tables, coef_ref, take_ref, sides)
        inputs, width = g_in_ref.shape
        for k in range(width // east):
            total_ref[k * inputs : (k + 1) * inputs, :] = g_in_ref[:, k * east : (k + 1) * east]
        sums = jnp.sum(g_bias_ref[...], 1, keepdims=True)
        last = jnp.concatenate([g_out_ref[...], jnp.broadcast_to(sums, g_out_ref.shape)], 1)
        at = inputs * width // east
        for k in range(0, width, east):
            total_ref[at + k : at + k + east, :] = last[k : k + east].T
        if total_ref.shape[0] > at + width:
            total_ref[at + width :, :] = jnp.zeros_like(total_ref[at + width :, :])
        mine = tables.share * PARTS
        each = send_ref.shape[0] // tables.count
        for part in range(mine):
            send_ref[pl.ds(part, tables.count, stride=each), :] = sides[
                pl.ds(part, tables.count, stride=mine), :
            ]
        more = each - mine
        for d in range(tables.count):
            send_ref[d * each + mine : (d + 1) * each, :] = total_ref[d * more : (d + 1) * more, :]


def column(
    tables, dep, adv, spread, fields, cotangent, in_weight, in_bias, out_weight, coef, jumps
):
    levels, north, east = tables.levels, tables.north, tables.east
    inputs, hidden = in_weight.shape
    f32, bf16 = jnp.float32, jnp.bfloat16
    consts = (
        in_weight, in_bias, out_weight, coef, jumps,
        tables.z_forward, tables.base, tables.x_forward, tables.y_forward, tables.take,
        tables.y_back, tables.x_back, tables.z_back, tables.give,
    )
    mixed = jax.ShapeDtypeStruct((2, north, levels, east), f32)
    coef, edge = solve_shapes(tables)
    rows = inputs * hidden // east + hidden
    assert 2 * levels == east
    rows = -(-rows // tables.count) * tables.count
    send = jax.ShapeDtypeStruct((edge.shape[0] + rows, east), f32)
    lanes = SUB * east
    field = lambda f: pl.BlockSpec((1, levels, SUB, east), lambda k: (f, 0, k, 0))
    return pl.pallas_call(
        functools.partial(column_kernel, tables),
        grid=(north // SUB,),
        in_specs=[
            whole_spec(dep),
            pl.BlockSpec((len(TRACERS), SUB, levels, east), lambda k: (0, k, 0, 0)),
            pl.BlockSpec((SUB, levels, east), lambda k: (k, 0, 0)),
            field(2),
            field(3),
            field(4),
            *(whole_spec(a) for a in consts),
        ],
        out_specs=[
            pl.BlockSpec((2, SUB, levels, east), lambda k: (0, k, 0, 0)),
            whole_spec(coef),
            whole_spec(send),
        ],
        out_shape=[mixed, coef, send],
        scratch_shapes=[
            pltpu.VMEM(coef.shape, f32),
            pltpu.VMEM(coef.shape, f32),
            pltpu.VMEM((inputs, lanes), bf16),
            pltpu.VMEM((hidden, lanes), f32),
            pltpu.VMEM((hidden, lanes), bf16),
            pltpu.VMEM((levels, lanes), bf16),
            pltpu.VMEM((3, levels * SUB, east), f32),
            pltpu.VMEM(edge.shape, f32),
            pltpu.VMEM((rows, east), f32),
            pltpu.VMEM((hidden, inputs), bf16),
            pltpu.VMEM((hidden, east), f32),
            pltpu.VMEM((hidden, east), f32),
            pltpu.VMEM((levels, hidden), bf16),
            pltpu.VMEM((inputs, hidden), f32),
            pltpu.VMEM((hidden, east), f32),
            pltpu.VMEM((hidden, levels), f32),
        ],
        compiler_params=call_params(),
    )(dep, adv, spread, fields, cotangent, cotangent, *consts)


def gather_kernel(adv_ref, mixed_ref, after_ref, new_ref, flat):
    del after_ref
    levels, east = adv_ref.shape[2:]
    for f, (ref, i) in zip(TRACERS, ((adv_ref, 0), (adv_ref, 1), (mixed_ref, 0), (mixed_ref, 1))):
        for k in range(SUB):
            flat[f, pl.ds(k, levels, stride=SUB), :] = ref[i, k]
        new_ref[f] = flat[f].reshape(levels, SUB, east)


def gather_fields(adv, mixed, after):
    _, north, levels, east = adv.shape
    block = pl.BlockSpec((2, SUB, levels, east), lambda k: (0, k, 0, 0))
    return pl.pallas_call(
        gather_kernel,
        grid=(north // SUB,),
        in_specs=[block, block, pl.BlockSpec(memory_space=pl.ANY)],
        out_specs=pl.BlockSpec((FIELDS, levels, SUB, east), lambda k: (0, 0, k, 0)),
        out_shape=jax.ShapeDtypeStruct((FIELDS, levels, north, east), jnp.float32),
        scratch_shapes=[pltpu.VMEM((FIELDS, levels * SUB, east), jnp.float32)],
        compiler_params=call_params(61 << 20),
    )(adv, mixed, after)


def solve_consts(tables):
    return (tables.base, tables.y_back, tables.x_back, tables.z_back, tables.give)


def pressure_kernel(
    tables, dep_ref, w_ref, new_ref, coef_ref, jump_ref, base_ref, y_ref, x_ref, z_ref, give_ref,
    pressure_ref, out_ref, spec, jumps,
):
    north, east, levels = tables.north, tables.east, tables.levels
    mine = tables.share * PARTS
    each = jump_ref.shape[0] // tables.count
    for part in range(mine):
        jumps[pl.ds(part, tables.count, stride=mine), :] = jump_ref[
            pl.ds(part, tables.count, stride=each), :
        ]
    level = lax.broadcasted_iota(jnp.int32, (levels, east), 0)

    def use(y, tile):
        pressure_ref[pl.ds(y, levels, stride=north), :] = tile
        value = w_ref[0, y] - TIME_STEP * vertical_change(tile)
        value = jnp.where(level < dep_ref[y : y + 1, :], value, 0.0)
        out_ref[0, pl.ds(y, levels, stride=north), :] = value

    finish_solve(
        tables, spec, coef_ref, jumps, base_ref, y_ref, x_ref, z_ref, give_ref, use
    )


def pressure_finish(tables, dep, w, new, coef, jumps):
    levels, north, east = tables.levels, tables.north, tables.east
    consts = solve_consts(tables)
    flat = jax.ShapeDtypeStruct((levels * north, east), jnp.float32)
    pressure, new = pl.pallas_call(
        functools.partial(pressure_kernel, tables),
        grid=(1,),
        in_specs=[
            whole_spec(dep),
            whole_spec(w),
            pl.BlockSpec(memory_space=pl.ANY),
            whole_spec(coef),
            whole_spec(jumps),
            *(whole_spec(a) for a in consts),
        ],
        out_specs=[
            whole_spec(flat),
            pl.BlockSpec((1, levels * north, east), lambda k: (2, 0, 0)),
        ],
        out_shape=[flat, jax.ShapeDtypeStruct((FIELDS, levels * north, east), jnp.float32)],
        input_output_aliases={2: 1},
        scratch_shapes=[
            pltpu.VMEM(coef.shape, jnp.float32),
            pltpu.VMEM((tables.share * tables.count * PARTS, east), jnp.float32),
        ],
        compiler_params=call_params(44 << 20),
    )(dep, w, new.reshape(FIELDS, levels * north, east), coef, jumps, *consts)
    return pressure.reshape(levels, north, east), new.reshape(FIELDS, levels, north, east)


def split_kernel(skip, count, sums_ref, in_ref, bias_ref, out_ref, flat):
    inputs, width = in_ref.shape
    east = sums_ref.shape[1]
    each = sums_ref.shape[0] // count
    more = each - skip
    for d in range(count):
        flat[d * more : (d + 1) * more, :] = sums_ref[d * each + skip : (d + 1) * each, :]
    wide = inputs * width // east
    for k in range(width // east):
        lanes = slice(k * east, (k + 1) * east)
        in_ref[:, lanes] = flat[k * inputs : (k + 1) * inputs, :]
        at = wide + k * east
        out_ref[:, lanes] = flat[at : at + out_ref.shape[0], :]
        bias_ref[:, lanes] = flat[at + east // 2 : at + east // 2 + 1, :]


def split_sums(tables, sums, inputs, hidden, outputs):
    skip = tables.share * PARTS
    rows = sums.shape[0] - skip * tables.count
    shapes = [
        jax.ShapeDtypeStruct(shape, jnp.float32)
        for shape in ((inputs, hidden), (1, hidden), (outputs, hidden))
    ]
    g_in, g_bias, g_out = pl.pallas_call(
        functools.partial(split_kernel, skip, tables.count),
        grid=(1,),
        in_specs=[whole_spec(sums)],
        out_specs=[whole_spec(a) for a in shapes],
        out_shape=shapes,
        scratch_shapes=[pltpu.VMEM((rows, tables.east), jnp.float32)],
        compiler_params=call_params(),
    )(sums)
    return g_in, g_bias.reshape(hidden), g_out.T


def per_device(fields, cotangent, ocean_mask, depth_levels, in_weight, in_bias, out_weight):
    _, levels, north, east = fields.shape
    tables = Tables(levels, north, east, lax.axis_size("rows"), lax.axis_size("cols"))
    inputs, hidden = in_weight.shape
    outputs = out_weight.shape[1]
    in_bias = in_bias.reshape(1, hidden)
    out_weight = out_weight.T
    steps = levels // SUB
    dep, *edges = advance_edges(fields, ocean_mask, depth_levels)
    back_coef = adjoint_local(tables, cotangent, dep)
    back_edges = adjoint_edges(tables, back_coef, edges[0], edges[1])
    half = advect(fields, dep, TRACERS, edges, (0, steps // 2), back_edges)
    back_jumps = interface(tables, exchange(back_edges), 56 << 20, half[1])
    adv, spread = advect(fields, dep, TRACERS, edges, (steps // 2, steps), back_jumps, half)
    mixed, coef, send = column(
        tables, dep, adv, spread, fields, cotangent, in_weight, in_bias, out_weight,
        back_coef, exchange(back_jumps),
    )
    received = exchange(send)
    w = advect(fields, dep, (2,), edges, (0, steps), coef)[0]
    new = gather_fields(adv, mixed, coef)
    jumps = exchange(interface(tables, received, VMEM_LIMIT, w, new))
    pressure, new_fields = pressure_finish(tables, dep, w, new, coef, jumps)
    return (new_fields, pressure, *split_sums(tables, jumps, inputs, hidden, outputs))


def solution(mesh):
    in_specs = (
        P(None, None, "cols", "rows"),
        P(None, None, "cols", "rows"),
        P("cols", "rows"),
        P("cols", "rows"),
        P(),
        P(),
        P(),
    )
    out_specs = (P(None, None, "cols", "rows"), P(None, "cols", "rows"), P(), P(), P())
    return jax.shard_map(
        per_device, mesh=mesh, in_specs=in_specs, out_specs=out_specs, check_vma=False
    )
```

```python
import functools

import jax
import jax.numpy as jnp
import numpy as np
from jax import lax
from jax.experimental import pallas as pl
from jax.experimental.pallas import tpu as pltpu
from jax.sharding import PartitionSpec as P

TIME_STEP = 0.2
RATE_MAX = 2.0
THERMAL = 0.5
HALINE = 0.5
SPECTRAL_SHIFT = 0.001
WENO_EPS = 1e-06
HALO = 3
FIELDS = 5
SUB = 8
PIECES = 4


def spread_rows(rows, b):
    east = rows.shape[1]
    ys = east // SUB
    return jnp.concatenate(
        [jnp.broadcast_to(rows[y : y + 1], (SUB, east)) for y in range(b * ys, (b + 1) * ys)], 0
    )


def pack_kernel(mask_ref, depth_ref, *refs):
    field_refs, refs = refs[:PIECES], refs[PIECES:]
    dep_ref, xfirst_ref, xlast_ref, yfirst_ref, ylast_ref = refs
    field = pl.program_id(0)
    north, east = dep_ref.shape
    some = field_refs[0].shape[1] // north
    levels = PIECES * some
    ys = east // SUB
    halves = north // ys
    blocks = levels // SUB * halves
    dep = jnp.where(mask_ref[...] == 1, depth_ref[...], 0)
    dep_ref[...] = dep
    first_levels = lax.broadcasted_iota(jnp.int32, (SUB, east), 0)
    for t in range(blocks):
        low, start = t // halves * SUB, t % halves * ys
        piece, at = divmod(low, some)
        tiles = []
        for y in range(start, start + ys):
            value = field_refs[piece][0, pl.ds(at * north + y, SUB, stride=north), :]
            tiles.append(jnp.where(first_levels + low < dep[y : y + 1], value, 0.0))
        turned = jnp.concatenate(tiles, 0).T
        row = field * blocks + t
        for s in range(HALO):
            xfirst_ref[s, pl.ds(row, 1), :] = turned[s : s + 1]
            xlast_ref[s, pl.ds(row, 1), :] = turned[east - HALO + s : east - HALO + s + 1]
    for s, piece in [(s, piece) for s in range(HALO) for piece in range(PIECES)]:
        level = lax.broadcasted_iota(jnp.int32, (some, east), 0) + piece * some
        at = pl.multiple_of((field * HALO + s) * levels + piece * some, SUB)
        low, high = s, north - HALO + s
        first = field_refs[piece][0, pl.ds(low, some, stride=north), :]
        last = field_refs[piece][0, pl.ds(high, some, stride=north), :]
        yfirst_ref[pl.ds(at, some), :] = jnp.where(level < dep[low : low + 1], first, 0.0)
        ylast_ref[pl.ds(at, some), :] = jnp.where(level < dep[high : high + 1], last, 0.0)

    @pl.when(field == 0)
    def _():
        depths = dep.astype(jnp.float32)
        end = FIELDS * HALO * levels
        yfirst_ref[end:, :] = jnp.broadcast_to(depths[:1], (SUB, east))
        ylast_ref[end:, :] = jnp.broadcast_to(depths[north - 1 :], (SUB, east))
        for s in range(HALO):
            xfirst_ref[s, FIELDS * blocks :, :] = jnp.zeros((SUB, east), jnp.float32)
            xlast_ref[s, FIELDS * blocks :, :] = jnp.zeros((SUB, east), jnp.float32)
        for b in range(halves):
            turned = spread_rows(depths, b).T
            row = FIELDS * blocks + b
            for s in range(HALO):
                xfirst_ref[s, row : row + 1, :] = turned[s : s + 1]
                xlast_ref[s, row : row + 1, :] = turned[east - HALO + s : east - HALO + s + 1]


def pack_edges(fields, mask, depth):
    _, levels, north, east = fields.shape
    rows = FIELDS * levels * north // east + SUB
    x_shape = jax.ShapeDtypeStruct((HALO, rows, east), jnp.float32)
    y_shape = jax.ShapeDtypeStruct((FIELDS * HALO * levels + SUB, east), jnp.float32)
    whole = lambda shape: pl.BlockSpec(shape.shape, lambda f: (0,) * len(shape.shape))
    return pl.pallas_call(
        pack_kernel,
        grid=(FIELDS,),
        in_specs=[
            whole(mask),
            whole(depth),
            *(
                pl.BlockSpec((1, levels * north // PIECES, east), lambda f, p=p: (f, p, 0))
                for p in range(PIECES)
            ),
        ],
        out_specs=[whole(mask), whole(x_shape), whole(x_shape), whole(y_shape), whole(y_shape)],
        out_shape=[jax.ShapeDtypeStruct(mask.shape, jnp.int32), x_shape, x_shape, y_shape, y_shape],
        compiler_params=pltpu.CompilerParams(vmem_limit_bytes=61 << 20),
    )(mask, depth, *(fields.reshape(FIELDS, levels * north, east) for _ in range(PIECES)))


def face_flux(slopes, left, right, speed, share):
    dm2, dm1, d0, dp1, dp2 = slopes
    ahead = speed > 0.0
    e1 = jnp.where(ahead, dm2, dp2)
    e2 = jnp.where(ahead, dm1, dp1)
    e4 = jnp.where(ahead, dp1, dm1)
    near = jnp.where(ahead, left, right)
    bend0, bend1, bend2 = e2 - e1, d0 - e2, e4 - d0
    tilt0, tilt1, tilt2 = bend0 + (e2 + e2), e2 + d0, bend2 - (d0 + d0)
    rough0 = bend0 * bend0 * (13.0 / 3.0) + (tilt0 * tilt0 + 4.0 * WENO_EPS)
    rough1 = bend1 * bend1 * (13.0 / 3.0) + (tilt1 * tilt1 + 4.0 * WENO_EPS)
    rough2 = bend2 * bend2 * (13.0 / 3.0) + (tilt2 * tilt2 + 4.0 * WENO_EPS)
    pair0, pair1, pair2 = rough1 * rough2, rough0 * rough2, rough0 * rough1
    g0, g1, g2 = pair0 * pair0, 6.0 * (pair1 * pair1), 3.0 * (pair2 * pair2)
    total = g0 * (tilt0 + (bend0 + e2)) + g1 * (tilt1 + d0) + g2 * (d0 - tilt2)
    return speed * near + share * (total * pltpu.reciprocal(g0 + g1 + g2, approx=True))


def advect_kernel(
    tracers, staged, begin, filled, dep_ref, *refs,
):
    field_refs, refs = refs[: len(staged)], refs[len(staged) :]
    xlo_ref, xhi_ref, ylo_ref, yhi_ref = refs[:4]
    refs = refs[5 + filled :]
    adv_ref = refs[0]
    spread_ref = refs[1] if len(tracers) > 1 else None
    (
        deep, both, lines, slopes, fluxes, cells, wets, su, su6, sv, sv6, sides,
    ) = refs[-12:]
    step = pl.program_id(0) + begin
    north, east = dep_ref.shape
    ys = east // SUB
    blocks = north // ys
    all_blocks = (xlo_ref.shape[1] - SUB) // FIELDS
    levels = all_blocks // blocks * SUB
    depth_row = FIELDS * all_blocks
    depth_end = FIELDS * HALO * levels
    faces = range(0, east + SUB, SUB)
    first_level = step * SUB

    @pl.when(step == begin)
    def _():
        depths = dep_ref[...].astype(jnp.float32)
        for b in range(blocks):
            row = depth_row + b
            deep[SUB : SUB + east, :] = spread_rows(depths, b).T
            deep[SUB - 1 : SUB, :] = xlo_ref[HALO - 1, row : row + 1, :]
            deep[SUB + east : SUB + east + 1, :] = xhi_ref[0, row : row + 1, :]
            both[b, :east, :] = jnp.minimum(
                deep[SUB - 1 : SUB - 1 + east, :], deep[SUB : SUB + east, :]
            )
            both[b, east : east + 1, :] = jnp.minimum(
                deep[SUB + east - 1 : SUB + east, :], deep[SUB + east : SUB + east + 1, :]
            )

    level = (lax.broadcasted_iota(jnp.int32, (SUB, east), 0) + first_level).astype(jnp.float32)
    height = lax.broadcasted_iota(jnp.int32, (SUB, east), 1) % SUB + first_level
    height = height.astype(jnp.float32)
    depths = dep_ref[...].astype(jnp.float32)
    wets[0] = (level < ylo_ref[depth_end : depth_end + 1, :]).astype(jnp.float32)
    wets[north + 1] = (level < yhi_ref[depth_end : depth_end + 1, :]).astype(jnp.float32)
    for y in range(north):
        wets[y + 1] = (level < depths[y : y + 1]).astype(jnp.float32)

    for slot, f in enumerate(staged):
        field = field_refs[slot]
        for s in range(HALO):
            at = pl.multiple_of((f * HALO + s) * levels + first_level, SUB)
            cells[slot, s] = ylo_ref[pl.ds(at, SUB), :]
            cells[slot, north + HALO + s] = yhi_ref[pl.ds(at, SUB), :]
        for y in range(north):
            cells[slot, y + HALO] = field[0, pl.ds(y, SUB, stride=north), :] * wets[y + 1]
        for b in range(blocks):
            row = f * all_blocks + step * blocks + b
            for s in range(HALO):
                lines[slot, b, SUB - HALO + s : SUB - HALO + s + 1, :] = xlo_ref[
                    s, pl.ds(row, 1), :
                ]
                lines[slot, b, SUB + east + s : SUB + east + s + 1, :] = xhi_ref[
                    s, pl.ds(row, 1), :
                ]
            tile = cells[slot, HALO + b * ys : HALO + (b + 1) * ys].reshape(east, east)
            lines[slot, b, SUB : SUB + east, :] = tile.T

    for b in range(blocks):
        for r in faces:
            speed = (0.5 * TIME_STEP) * (
                lines[0, b, SUB + r - 1 : 2 * SUB + r - 1, :] + lines[0, b, SUB + r : 2 * SUB + r, :]
            )
            speed = jnp.where(height < both[b, r : r + SUB, :], speed, 0.0)
            su[b, r : r + SUB, :] = speed
            su6[b, r : r + SUB, :] = jnp.abs(speed) * (1.0 / 6.0)
        if spread_ref is not None:
            change = 0.5 * (
                lines[0, b, SUB + 1 : SUB + 1 + east, :] - lines[0, b, SUB - 1 : SUB - 1 + east, :]
            )
            sides[b * east : (b + 1) * east, :] = change.T
    if spread_ref is not None:
        for y in range(north):
            spread_ref[y] = sides[y * SUB : (y + 1) * SUB, :] + 0.5 * (
                cells[1, y + HALO + 1] - cells[1, y + HALO - 1]
            )
    for y in range(north + 1):
        speed = (0.5 * TIME_STEP) * (cells[1, y + HALO - 1] + cells[1, y + HALO])
        speed = speed * (wets[y] * wets[y + 1])
        sv[y] = speed
        sv6[y] = jnp.abs(speed) * (1.0 / 6.0)

    first = len(staged) - len(tracers)

    def advance_field(f):
        for b in range(blocks):
            for r in range(0, east + 2 * SUB, SUB):
                ahead = lines[f, b, r + 1 : r + 1 + SUB, :]
                slopes[b, r : r + SUB, :] = ahead - lines[f, b, r : r + SUB, :]
            for r in faces:
                at = SUB + r
                near = [slopes[b, at + k : at + k + SUB, :] for k in (-3, -2, -1, 0, 1)]
                fluxes[b, r : r + SUB, :] = face_flux(
                    near,
                    lines[f, b, at - 1 : at - 1 + SUB, :],
                    lines[f, b, at : at + SUB, :],
                    su[b, r : r + SUB, :],
                    su6[b, r : r + SUB, :],
                )
            change = fluxes[b, 0:east, :] - fluxes[b, 1 : 1 + east, :]
            sides[b * east : (b + 1) * east, :] = change.T
        line = [cells[f, k] for k in range(5)]
        inclines = [line[k + 1] - line[k] for k in range(4)]
        south = None
        for y in range(north + 1):
            line.append(cells[f, y + 2 * HALO - 1])
            inclines.append(line[-1] - line[-2])
            north_face = face_flux(inclines[-5:], line[-4], line[-3], sv[y], sv6[y])
            if y > 0:
                change = sides[(y - 1) * SUB : y * SUB, :] + (south - north_face)
                adv_ref[f - first, y - 1] = wets[y] * (line[-4] + change)
            south = north_face

    for f in range(first, len(staged)):
        advance_field(f)


def advect(fields, dep, tracers, edges, span, after, filled=()):
    _, levels, north, east = fields.shape
    whole = lambda a: pl.BlockSpec(a.shape, lambda k: (0,) * a.ndim)
    staged = tracers if tracers[0] == 0 else (0, 1, *tracers)
    one = lambda f: pl.BlockSpec((1, SUB * north, east), lambda k: (f, k + span[0], 0))
    f32 = jnp.float32
    blocks = SUB * north // east
    flat = fields.reshape(FIELDS, levels * north, east)
    out_specs = [pl.BlockSpec((len(tracers), north, SUB, east), lambda k: (0, 0, k + span[0], 0))]
    out_shape = [jax.ShapeDtypeStruct((len(tracers), north, levels, east), f32)]
    if tracers[0] == 0:
        out_specs.append(pl.BlockSpec((north, SUB, east), lambda k: (0, k + span[0], 0)))
        out_shape.append(jax.ShapeDtypeStruct((north, levels, east), f32))
    return pl.pallas_call(
        functools.partial(advect_kernel, tracers, staged, span[0], len(filled)),
        grid=(span[1] - span[0],),
        in_specs=[
            whole(dep),
            *(one(f) for f in staged),
            *(whole(a) for a in edges),
            pl.BlockSpec(memory_space=pl.ANY),
            *(pl.BlockSpec(memory_space=pl.ANY) for _ in filled),
        ],
        out_specs=out_specs,
        out_shape=out_shape,
        input_output_aliases={len(staged) + 6 + i: i for i in range(len(filled))},
        scratch_shapes=[
            pltpu.VMEM((east + 2 * SUB, east), f32),
            pltpu.VMEM((blocks, east + SUB, east), f32),
            pltpu.VMEM((len(staged), blocks, east + 3 * SUB, east), f32),
            pltpu.VMEM((blocks, east + 3 * SUB, east), f32),
            pltpu.VMEM((blocks, east + SUB, east), f32),
            pltpu.VMEM((len(staged), north + 2 * HALO, SUB, east), f32),
            pltpu.VMEM((north + 2, SUB, east), f32),
            pltpu.VMEM((blocks, east + SUB, east), f32),
            pltpu.VMEM((blocks, east + SUB, east), f32),
            pltpu.VMEM((north + 1, SUB, east), f32),
            pltpu.VMEM((north + 1, SUB, east), f32),
            pltpu.VMEM((SUB * north, east), f32),
        ],
        compiler_params=pltpu.CompilerParams(vmem_limit_bytes=VMEM_LIMIT),
    )(dep, *(flat for _ in staged), *edges, after, *filled)


def shift_both(axis, first, last):
    count = lax.axis_size(axis)
    forward = [(i, i + 1) for i in range(count - 1)]
    backward = [(i + 1, i) for i in range(count - 1)]
    return lax.ppermute(last, axis, forward), lax.ppermute(first, axis, backward)


def advance_edges(fields, mask, depth):
    dep, xfirst, xlast, yfirst, ylast = pack_edges(fields, mask, depth)
    south_north = shift_both("cols", yfirst, ylast)
    return (dep, *shift_both("rows", xfirst, xlast), *south_north)


AXES = ("rows", "cols")
VMEM_LIMIT = 52 << 20
TRACERS = (0, 1, 3, 4)
PARTS = 4


def dct_table(length):
    freq = np.arange(length)[:, None]
    cells = np.arange(length)[None, :]
    scale = np.where(freq == 0, np.sqrt(1.0 / length), np.sqrt(2.0 / length))
    return scale * np.cos(np.pi * (cells + 0.5) * freq / length)


def eigen_table(length):
    return 2.0 - 2.0 * np.cos(np.pi * np.arange(length) / length)


def halves(table):
    high = table.astype(jnp.bfloat16)
    low = (table - high.astype(np.float64)).astype(jnp.bfloat16)
    return high, low


def right_factor(table):
    high, low = halves(table)
    return np.block([[high, low], [high, np.zeros_like(low)]])


def left_factor(table):
    high, low = halves(table)
    return np.concatenate([high, low], 0)


class Tables:
    def __init__(self, levels, north, east, rows, cols):
        self.levels, self.north, self.east, self.rows, self.cols = levels, north, east, rows, cols
        self.count = rows * cols
        self.share = -(-levels // self.count)
        padded = self.share * self.count
        cz, cy, cx = dct_table(levels), dct_table(north), dct_table(east)
        lz, ly, lx = eigen_table(levels), eigen_table(north), eigen_table(east)
        shift = SPECTRAL_SHIFT + lz
        f32 = np.float32
        eye = np.eye(SUB)
        self.ly = [float(v) for v in ly]
        self.south = [float(v) for v in cy[:, 0]]
        self.north_edge = [float(v) for v in cy[:, -1]]
        self.base = (shift[:, None] + lx[None]).astype(f32)
        self.z_forward, self.z_back = left_factor(cz), left_factor(cz.T)
        self.y_forward = left_factor(np.kron(cy, eye))
        self.y_back = left_factor(np.kron(cy.T, eye))
        self.x_forward, self.x_back = right_factor(cx.T), right_factor(cx)
        edges = np.zeros((2 * north, east))
        edges[:north], edges[north:] = cx[:, 0], cx[:, -1]
        self.take = np.concatenate(halves(edges.T), 1)
        edges[:north], edges[north:] = -cx[:, -1], cx[:, 0]
        give = np.concatenate(halves(edges), 0)
        self.give = np.concatenate([give, give], 0)
        assert 4 * north == east
        lanes = max(east, 2 * north)
        assert lanes == east and cols % SUB == 0
        grid = 1.0 / (shift[:, None, None] + ly[None, :, None] + lx[None, None, :])
        alpha = np.einsum("k,myk->my", cx[:, -1] ** 2, grid)
        beta = np.einsum("k,myk->my", cx[:, -1] * cx[:, 0], grid)
        inner = rows - 1
        near = np.eye(inner, k=1) + np.eye(inner, k=-1)
        system = (1.0 + 2.0 * alpha)[..., None, None] * np.eye(inner) - beta[
            ..., None, None
        ] * near
        inverse = np.linalg.inv(system).transpose(0, 2, 3, 1).reshape(levels, inner**2, north)
        cross = np.zeros((padded, inner**2 + 1, east), f32)
        cross[:levels, : inner**2, :north] = inverse
        cross[:, inner**2] = 1.0
        cross[:levels, inner**2] = shift[:, None]
        self.cross = cross
        all_east = eigen_table(rows * east)
        grid = 1.0 / (shift[:, None, None] + ly[None, :, None] + all_east[None, None, :])
        alpha = np.einsum("y,myk->mk", cy[:, -1] ** 2, grid)
        beta = np.einsum("y,myk->mk", cy[:, -1] * cy[:, 0], grid)
        waves = np.cos(np.pi * np.arange(1, cols) / cols)
        along = np.zeros((padded, cols, rows * east), f32)
        along[:levels, : cols - 1] = 1.0 / (
            1.0 + 2.0 * alpha[:, None] - 2.0 * beta[:, None] * waves[None, :, None]
        )
        self.along = along
        order = np.arange(1, cols)
        sines = np.zeros((cols, cols))
        sines[: cols - 1, : cols - 1] = np.sqrt(2.0 / cols) * np.sin(
            np.pi * np.outer(order, order) / cols
        )
        self.sines = np.kron(np.eye(self.share), sines).astype(f32)
        wide = dct_table(rows * east).reshape(rows * east, rows, east)
        turn = np.einsum("gax,kx->gak", wide, cx).reshape(rows * east, rows * east)
        self.wide_forward = np.stack(halves(turn.T))
        self.wide_back = np.stack(halves(turn))
        both = (ly[:, None] + lx[None]).astype(f32)
        self.strip = np.stack(
            [both, np.broadcast_to(cy[:, -1:], both.shape), np.broadcast_to(cy[:, :1], both.shape)]
        ).astype(f32)
        back = np.full((east, east), 1.0)
        gain = np.zeros((east, east))
        back[:, :north] = back[:, north : 2 * north] = both.T
        gain[:, :north], gain[:, north : 2 * north] = cx[:, -1:], cx[:, :1]
        self.column = np.stack([back, gain]).astype(f32)
        lines = np.zeros((SUB, east), f32)
        lines[0], lines[1] = cx[:, -1], cx[:, 0]
        lines[2, :north] = lines[2, north : 2 * north] = cy[:, -1]
        lines[3, :north] = lines[3, north : 2 * north] = cy[:, 0]
        self.lines = lines


def parts(value):
    high = value.astype(jnp.bfloat16)
    return high, (value - high.astype(jnp.float32)).astype(jnp.bfloat16)


def mul(a, b):
    return jnp.dot(a, b, preferred_element_type=jnp.float32)


def from_left(factor, value):
    rows = factor.shape[0] // 2
    high, low = parts(value)
    both = mul(factor, high)
    return both[:rows] + (both[rows:] + mul(factor[:rows], low))


def from_right(value, factor):
    columns = factor.shape[1] // 2
    both = mul(jnp.concatenate(parts(value), 1), factor)
    return both[:, :columns] + both[:, columns:]


def times(value, high, low):
    first, second = parts(value)
    return mul(first, high) + (mul(second, high) + mul(first, low))


def vertical_change(value):
    levels = value.shape[0]
    level = lax.broadcasted_iota(jnp.int32, value.shape, 0)
    above = jnp.where(level == levels - 1, 0.0, pltpu.roll(value, levels - 1, 0))
    below = jnp.where(level == 0, 0.0, pltpu.roll(value, 1, 0))
    return 0.5 * (above - below)


def pair_of(spec, m, rows):
    return jnp.concatenate(
        [spec[:, at : at + SUB, :].reshape(rows, -1) for at in (m, m + SUB)], 1
    )


def block_solve(tables, spec, base_ref, x_ref, y_ref, coef_ref):
    north, east, levels = tables.north, tables.east, tables.levels
    for y in range(0, north, 4):
        tile = spec[y : y + 4].reshape(4 * levels, east)
        spec[y : y + 4] = from_right(tile, x_ref[...]).reshape(4, levels, east)
    for m in range(0, levels, 2 * SUB):
        both = from_left(y_ref[...], pair_of(spec, m, north * SUB))
        for i in range(2):
            at = m + i * SUB
            base = base_ref[at : at + SUB, :]
            tile = both[:, i * east : (i + 1) * east]
            for k in range(north):
                coef_ref[k, at : at + SUB, :] = tile[k * SUB : (k + 1) * SUB] / (
                    base + tables.ly[k]
                )


def block_edges(tables, coef_ref, take_ref, edge_ref):
    north, east, levels = tables.north, tables.east, tables.levels
    zero = jnp.zeros((levels, east), jnp.float32)
    even = odd = total = rest = zero
    lane = lax.broadcasted_iota(jnp.int32, (levels, east), 1)
    place = lane % north
    for k in range(0, north, 4):
        group = coef_ref[k : k + 4]
        high, low = parts(group.reshape(4 * levels, east))
        high, low = mul(high, take_ref[...]), mul(low, take_ref[...])
        for i in range(4):
            value = tables.south[k + i] * group[i]
            if i % 2:
                odd = odd + value
            else:
                even = even + value
            mine = place == k + i
            total = total + jnp.where(mine, high[i * levels : (i + 1) * levels], 0.0)
            rest = rest + jnp.where(mine, low[i * levels : (i + 1) * levels], 0.0)
    total = total + pltpu.roll(total, east // 2, 1) + rest
    sides = (jnp.where(lane < 2 * north, total, 0.0), even + odd, even - odd, zero)
    for part in range(PARTS):
        edge_ref[pl.ds(part, levels, stride=PARTS), :] = sides[part]
    if edge_ref.shape[0] > levels * PARTS:
        edge_ref[levels * PARTS :, :] = jnp.zeros_like(edge_ref[levels * PARTS :, :])


def finish_solve(tables, spec, coef_ref, jump_ref, base_ref, y_ref, x_ref, z_ref, give_ref, use):
    north, east, levels = tables.north, tables.east, tables.levels
    side, ahead, behind = (
        jump_ref[pl.ds(part, levels, stride=PARTS), :] for part in range(PARTS - 1)
    )
    high, low = (half.astype(jnp.float32) for half in parts(side))
    sides = jnp.concatenate([high + pltpu.roll(high, east // 2, 1), low], 1)
    place = lax.broadcasted_iota(jnp.int32, sides.shape, 1) % north
    for k in range(0, north, 4):
        picked = [jnp.where(place == k + i, sides, 0.0).astype(jnp.bfloat16) for i in range(4)]
        change = mul(jnp.concatenate(picked, 0), give_ref[...])
        for i in range(4):
            value = change[i * levels : (i + 1) * levels] + (
                tables.south[k + i] * behind - tables.north_edge[k + i] * ahead
            )
            spec[k + i] = coef_ref[k + i] + value / (base_ref[...] + tables.ly[k + i])
    for m in range(0, levels, 2 * SUB):
        both = from_left(y_ref[...], pair_of(spec, m, north * SUB))
        for i in range(2):
            at = m + i * SUB
            tile = both[:, i * east : (i + 1) * east]
            spec[:, at : at + SUB, :] = tile.reshape(north, SUB, east)
    for y in range(0, north, 4):
        tile = from_right(spec[y : y + 4].reshape(4 * levels, east), x_ref[...])
        tile = jnp.concatenate([tile[k * levels : (k + 1) * levels] for k in range(4)], 1)
        tile = from_left(z_ref[...], tile)
        for k in range(4):
            use(y + k, tile[:, k * east : (k + 1) * east])


def interface_kernel(
    tables, device_ref, edge_ref, cross_ref, along_ref, sines_ref, forward_ref, back_ref,
    strip_ref, column_ref, lines_ref, *rest,
):
    del device_ref
    jump_ref = rest[-1]
    rows, cols, east, north = tables.rows, tables.cols, tables.east, tables.north
    each = edge_ref.shape[0] // tables.count
    mine = tables.share * PARTS
    if each > mine:
        total = edge_ref[mine:each, :]
        for d in range(1, tables.count):
            total = total + edge_ref[d * each + mine : (d + 1) * each, :]
        for d in range(tables.count):
            jump_ref[d * each + mine : (d + 1) * each, :] = total
    share, inner = tables.share, tables.rows - 1
    f32 = jnp.float32
    east_last, east_first = lines_ref[0:1, :], lines_ref[1:2, :]
    north_last, north_first = lines_ref[2:3, :], lines_ref[3:4, :]
    every = lax.Precision.HIGHEST

    def across(m, changes):
        result = []
        for i in range(inner):
            total = jnp.zeros((cols, east), f32)
            for j in range(inner):
                at = i * inner + j
                total = total + cross_ref[m, at : at + 1, :] * changes[j]
            result.append(total)
        return result

    gaps, steps = [], []
    for m in range(share):
        west, south, top = (
            [
                edge_ref[pl.ds(a * cols * each + m * PARTS + part, cols, stride=each), :]
                for a in range(rows)
            ]
            for part in range(PARTS - 1)
        )
        right = [pltpu.roll(tile, east - north, 1) for tile in west]
        gap = [right[i] - west[i + 1] for i in range(inner)]
        gaps.append(gap)
        jumps = jnp.concatenate(across(m, gap), 0)
        shift = cross_ref[m, inner**2 : inner**2 + 1, :]
        inverse = 1.0 / (strip_ref[0] + shift)
        weights = jnp.concatenate([strip_ref[1] * inverse, strip_ref[2] * inverse], 1)
        weights = jnp.concatenate([weights, jnp.zeros((east - north, 2 * east), f32)], 0)
        moved = times(jumps, *parts(weights))
        for a in range(rows):
            for side, at in ((top, 0), (south, east)):
                if a < inner:
                    side[a] = side[a] - east_last * moved[a * cols : (a + 1) * cols, at : at + east]
                if a > 0:
                    side[a] = side[a] + east_first * moved[
                        (a - 1) * cols : a * cols, at : at + east
                    ]
        steps.append(
            jnp.concatenate([top[a] - pltpu.roll(south[a], cols - 1, 0) for a in range(rows)], 1)
        )
    step = jnp.concatenate(steps, 0)
    waves = times(step, forward_ref[0], forward_ref[1])
    waves = jnp.dot(sines_ref[...], waves, precision=every, preferred_element_type=f32)
    waves = waves * jnp.concatenate([along_ref[m] for m in range(share)], 0)
    waves = jnp.dot(sines_ref[...], waves, precision=every, preferred_element_type=f32)
    step = times(waves, back_ref[0], back_ref[1])
    for m in range(share):
        shift = cross_ref[m, inner**2 : inner**2 + 1, :]
        here = step[m * cols : (m + 1) * cols]
        tall = [here[:, a * east : (a + 1) * east] for a in range(rows)]
        weights = column_ref[1] / (column_ref[0] + shift)
        moved = times(jnp.concatenate(tall, 0), *parts(weights))
        sides = []
        for a in range(rows):
            tile = moved[a * cols : (a + 1) * cols]
            sides.append(north_last * tile - north_first * pltpu.roll(tile, 1, 0))
        gap = [
            gaps[m][i] - (sides[i] - pltpu.roll(sides[i + 1], east - north, 1))
            for i in range(inner)
        ]
        jumps = across(m, gap)
        for a in range(rows):
            tile = jnp.zeros((cols, east), f32)
            if a < inner:
                tile = tile + jumps[a]
            if a > 0:
                tile = tile + pltpu.roll(jumps[a - 1], north, 1)
            out = (tile, tall[a], pltpu.roll(tall[a], 1, 0), jnp.zeros_like(tile))
            for part in range(PARTS):
                at = a * cols * each + m * PARTS + part
                jump_ref[pl.ds(at, cols, stride=each), :] = out[part]


def whole_spec(array):
    shape = tuple(array.shape)
    return pl.BlockSpec(shape, lambda *_: (0,) * len(shape))


def call_params(limit=VMEM_LIMIT):
    return pltpu.CompilerParams(vmem_limit_bytes=limit)


def exchange(block):
    return lax.all_to_all(block, AXES, split_axis=0, concat_axis=0, tiled=True)


def interface(tables, received, limit, *after):
    device = lax.axis_index("rows") * lax.axis_size("cols") + lax.axis_index("cols")
    operands = (
        received, tables.cross, tables.along, tables.sines, tables.wide_forward, tables.wide_back,
        tables.strip, tables.column, tables.lines,
    )
    specs = [whole_spec(a) for a in operands]
    for at in (1, 2):
        shape = (tables.share, *operands[at].shape[1:])
        specs[at] = pl.BlockSpec(shape, lambda k, mine: (mine[0], 0, 0))
    return pl.pallas_call(
        functools.partial(interface_kernel, tables),
        grid_spec=pltpu.PrefetchScalarGridSpec(
            num_scalar_prefetch=1,
            grid=(1,),
            in_specs=[*specs, *(pl.BlockSpec(memory_space=pl.ANY) for _ in after)],
            out_specs=whole_spec(received),
        ),
        out_shape=jax.ShapeDtypeStruct(received.shape, jnp.float32),
        compiler_params=call_params(limit),
    )(device.astype(jnp.int32).reshape(1), *operands, *after)


def adjoint_kernel(
    tables, dep_ref, cot_ref, z_ref, base_ref, x_ref, y_ref, coef_ref, spec
):
    north, east, levels = tables.north, tables.east, tables.levels
    level = lax.broadcasted_iota(jnp.int32, (levels, east), 0)
    for y in range(0, north, 4):
        tiles = []
        for k in range(y, y + 4):
            value = cot_ref[0, pl.ds(k, levels, stride=north), :]
            value = jnp.where(level < dep_ref[k : k + 1, :], value, 0.0)
            tiles.append(TIME_STEP * vertical_change(value))
        tile = from_left(z_ref[...], jnp.concatenate(tiles, 1))
        for k in range(4):
            spec[y + k] = tile[:, k * east : (k + 1) * east]
    block_solve(tables, spec, base_ref, x_ref, y_ref, coef_ref)


def solve_shapes(tables):
    coef = jax.ShapeDtypeStruct((tables.north, tables.levels, tables.east), jnp.float32)
    edge = jax.ShapeDtypeStruct((tables.share * tables.count * PARTS, tables.east), jnp.float32)
    return [coef, edge]


def adjoint_local(tables, cotangent, dep):
    levels, north, east = tables.levels, tables.north, tables.east
    consts = (tables.z_forward, tables.base, tables.x_forward, tables.y_forward)
    coef = solve_shapes(tables)[0]
    return pl.pallas_call(
        functools.partial(adjoint_kernel, tables),
        grid=(1,),
        in_specs=[
            whole_spec(dep),
            pl.BlockSpec((1, levels * north, east), lambda k: (2, 0, 0)),
            *(whole_spec(a) for a in consts),
        ],
        out_specs=whole_spec(coef),
        out_shape=coef,
        scratch_shapes=[pltpu.VMEM(coef.shape, jnp.float32)],
        compiler_params=call_params(52 << 20),
    )(dep, cotangent.reshape(FIELDS, levels * north, east), *consts)


def edges_kernel(tables, coef_ref, take_ref, *rest):
    block_edges(tables, coef_ref, take_ref, rest[-1])


def adjoint_edges(tables, coef, *after):
    edge = solve_shapes(tables)[1]
    return pl.pallas_call(
        functools.partial(edges_kernel, tables),
        grid=(1,),
        in_specs=[
            whole_spec(coef),
            whole_spec(tables.take),
            *(pl.BlockSpec(memory_space=pl.ANY) for _ in after),
        ],
        out_specs=whole_spec(edge),
        out_shape=edge,
        compiler_params=call_params(),
    )(coef, tables.take, *after)


def set_weights(w_in_ref, bias_ref, w_ref, w_in, bias, w, w_out, levels):
    inputs, width = w_in_ref.shape
    east = bias.shape[1]
    w_in[...] = w_in_ref[...].astype(jnp.float32).T.astype(jnp.bfloat16)
    bias[...] = jnp.broadcast_to(bias_ref[...], (east, width)).T
    for k in range(0, width, east):
        w[k : k + east, :] = jnp.zeros((east, east), jnp.float32)
        w[k : k + levels - 1, :] = w_ref[:, k : k + east].astype(jnp.float32)
        tile = w[k : k + east, :]
        w_out[:, k : k + east] = tile[:levels].astype(jnp.bfloat16)
        w[k : k + east, :] = tile.T


def closure(adv_ref, w_in, bias, w_out, feats, activity, hidden):
    levels, east = adv_ref.shape[2:]
    for k in range(SUB):
        for f in range(len(TRACERS)):
            feats[f * levels : (f + 1) * levels, k * east : (k + 1) * east] = adv_ref[f, k].astype(
                jnp.bfloat16
            )
    before = mul(w_in[...], feats[...])
    for k in range(SUB):
        lanes = slice(k * east, (k + 1) * east)
        value = jnp.tanh(before[:, lanes] + bias[...])
        if activity is not None:
            activity[:, lanes] = value
        hidden[:, lanes] = value.astype(jnp.bfloat16)
    return RATE_MAX * jax.nn.sigmoid(mul(w_out[...], hidden[...]))


def column_kernel(
    tables, dep_ref, adv_ref, spread_ref, w_field_ref, heat_ref, salt_ref,
    w_in_ref, bias_ref, w_ref, back_coef_ref, back_jump_ref,
    z_ref, base_ref, x_ref, y_ref, take_ref, y_back_ref, x_back_ref, z_back_ref, give_ref,
    mixed_ref, coef_ref, send_ref,
    spec, back, feats, activity, hidden, grads, flat, sides, total_ref,
    w_in, bias, w, w_out, g_in_ref, g_bias_ref, g_out_ref,
):
    step = pl.program_id(0)
    north, east, levels = tables.north, tables.east, tables.levels
    f32, bf16 = jnp.float32, jnp.bfloat16

    @pl.when(step == 0)
    def _():
        set_weights(w_in_ref, bias_ref, w_ref, w_in, bias, w, w_out, levels)
        g_in_ref[...] = jnp.zeros_like(g_in_ref)
        g_out_ref[...] = jnp.zeros_like(g_out_ref)
        g_bias_ref[...] = jnp.zeros_like(g_bias_ref)

        def use(y, tile):
            back[y] = tile

        finish_solve(
            tables, spec, back_coef_ref, back_jump_ref, base_ref, y_back_ref, x_back_ref,
            z_back_ref, give_ref, use,
        )

    rates = closure(adv_ref, w_in, bias, w_out, feats, activity, hidden)
    for i, ref in enumerate((heat_ref, salt_ref, w_field_ref)):
        flat[i] = ref[0].reshape(levels * SUB, east)
    level = lax.broadcasted_iota(jnp.int32, (levels, east), 0)
    depths = dep_ref[pl.ds(pl.multiple_of(step * SUB, SUB), SUB), :]
    sources = []
    for k in range(SUB):
        lanes = slice(k * east, (k + 1) * east)
        depth = depths[k : k + 1]
        wet = level < depth
        rate = rates[:, lanes]
        flow = jnp.where(level + 1 < depth, TIME_STEP, 0.0) * rate
        slope = -vertical_change(jnp.where(wet, back[step * SUB + k], 0.0))
        mixed = []
        total = jnp.zeros((levels, east), f32)
        for i, share in ((0, THERMAL), (1, -HALINE)):
            value = adv_ref[2 + i, k]
            drop = pltpu.roll(value, levels - 1, 0) - value
            grad = flat[i, pl.ds(k, levels, stride=SUB), :] + share * slope
            grad = jnp.where(wet, grad, 0.0)
            total = total + (grad - pltpu.roll(grad, levels - 1, 0)) * drop
            flux = flow * drop
            value = jnp.where(wet, value + (flux - pltpu.roll(flux, 1, 0)), 0.0)
            mixed.append(value)
            mixed_ref[i, k] = value
        grads[:, lanes] = (total * flow * (1.0 - rate * (1.0 / RATE_MAX))).astype(bf16)
        rise = jnp.where(wet, flat[2, pl.ds(k, levels, stride=SUB), :], 0.0)
        density = THERMAL * mixed[0] - HALINE * mixed[1] - rise * (1.0 / TIME_STEP)
        source = vertical_change(density) - spread_ref[k] * (1.0 / TIME_STEP)
        sources.append(jnp.where(wet, source, 0.0))
    tile = from_left(z_ref[...], jnp.concatenate(sources, 1))
    for k in range(SUB):
        spec[step * SUB + k] = tile[:, k * east : (k + 1) * east]

    over = (((1,), (1,)), ((), ()))
    grad = grads[...]
    g_out_ref[...] += lax.dot_general(hidden[...], grad, over, preferred_element_type=f32)
    pre = mul(w[:, :levels].astype(bf16), grad)
    for k in range(SUB):
        lanes = slice(k * east, (k + 1) * east)
        value = activity[:, lanes]
        value = pre[:, lanes] * (1.0 - value * value)
        g_bias_ref[...] += value
        hidden[:, lanes] = value.astype(bf16)
    g_in_ref[...] += lax.dot_general(feats[...], hidden[...], over, preferred_element_type=f32)

    @pl.when(step == north // SUB - 1)
    def _():
        block_solve(tables, spec, base_ref, x_ref, y_ref, coef_ref)
        block_edges(tables, coef_ref, take_ref, sides)
        inputs, width = g_in_ref.shape
        for k in range(width // east):
            total_ref[k * inputs : (k + 1) * inputs, :] = g_in_ref[:, k * east : (k + 1) * east]
        sums = jnp.sum(g_bias_ref[...], 1, keepdims=True)
        last = jnp.concatenate([g_out_ref[...], jnp.broadcast_to(sums, g_out_ref.shape)], 1)
        at = inputs * width // east
        for k in range(0, width, east):
            total_ref[at + k : at + k + east, :] = last[k : k + east].T
        if total_ref.shape[0] > at + width:
            total_ref[at + width :, :] = jnp.zeros_like(total_ref[at + width :, :])
        mine = tables.share * PARTS
        each = send_ref.shape[0] // tables.count
        for part in range(mine):
            send_ref[pl.ds(part, tables.count, stride=each), :] = sides[
                pl.ds(part, tables.count, stride=mine), :
            ]
        more = each - mine
        for d in range(tables.count):
            send_ref[d * each + mine : (d + 1) * each, :] = total_ref[d * more : (d + 1) * more, :]


def column(
    tables, dep, adv, spread, fields, cotangent, in_weight, in_bias, out_weight, coef, jumps
):
    levels, north, east = tables.levels, tables.north, tables.east
    inputs, hidden = in_weight.shape
    f32, bf16 = jnp.float32, jnp.bfloat16
    consts = (
        in_weight, in_bias, out_weight, coef, jumps,
        tables.z_forward, tables.base, tables.x_forward, tables.y_forward, tables.take,
        tables.y_back, tables.x_back, tables.z_back, tables.give,
    )
    mixed = jax.ShapeDtypeStruct((2, north, levels, east), f32)
    coef, edge = solve_shapes(tables)
    rows = inputs * hidden // east + hidden
    assert 2 * levels == east
    rows = -(-rows // tables.count) * tables.count
    send = jax.ShapeDtypeStruct((edge.shape[0] + rows, east), f32)
    lanes = SUB * east
    field = lambda f: pl.BlockSpec((1, levels, SUB, east), lambda k: (f, 0, k, 0))
    return pl.pallas_call(
        functools.partial(column_kernel, tables),
        grid=(north // SUB,),
        in_specs=[
            whole_spec(dep),
            pl.BlockSpec((len(TRACERS), SUB, levels, east), lambda k: (0, k, 0, 0)),
            pl.BlockSpec((SUB, levels, east), lambda k: (k, 0, 0)),
            field(2),
            field(3),
            field(4),
            *(whole_spec(a) for a in consts),
        ],
        out_specs=[
            pl.BlockSpec((2, SUB, levels, east), lambda k: (0, k, 0, 0)),
            whole_spec(coef),
            whole_spec(send),
        ],
        out_shape=[mixed, coef, send],
        scratch_shapes=[
            pltpu.VMEM(coef.shape, f32),
            pltpu.VMEM(coef.shape, f32),
            pltpu.VMEM((inputs, lanes), bf16),
            pltpu.VMEM((hidden, lanes), f32),
            pltpu.VMEM((hidden, lanes), bf16),
            pltpu.VMEM((levels, lanes), bf16),
            pltpu.VMEM((3, levels * SUB, east), f32),
            pltpu.VMEM(edge.shape, f32),
            pltpu.VMEM((rows, east), f32),
            pltpu.VMEM((hidden, inputs), bf16),
            pltpu.VMEM((hidden, east), f32),
            pltpu.VMEM((hidden, east), f32),
            pltpu.VMEM((levels, hidden), bf16),
            pltpu.VMEM((inputs, hidden), f32),
            pltpu.VMEM((hidden, east), f32),
            pltpu.VMEM((hidden, levels), f32),
        ],
        compiler_params=call_params(),
    )(dep, adv, spread, fields, cotangent, cotangent, *consts)


def gather_kernel(adv_ref, mixed_ref, after_ref, new_ref, flat):
    del after_ref
    levels, east = adv_ref.shape[2:]
    for f, (ref, i) in zip(TRACERS, ((adv_ref, 0), (adv_ref, 1), (mixed_ref, 0), (mixed_ref, 1))):
        for k in range(SUB):
            flat[f, pl.ds(k, levels, stride=SUB), :] = ref[i, k]
        new_ref[f] = flat[f].reshape(levels, SUB, east)


def gather_fields(adv, mixed, after):
    _, north, levels, east = adv.shape
    block = pl.BlockSpec((2, SUB, levels, east), lambda k: (0, k, 0, 0))
    return pl.pallas_call(
        gather_kernel,
        grid=(north // SUB,),
        in_specs=[block, block, pl.BlockSpec(memory_space=pl.ANY)],
        out_specs=pl.BlockSpec((FIELDS, levels, SUB, east), lambda k: (0, 0, k, 0)),
        out_shape=jax.ShapeDtypeStruct((FIELDS, levels, north, east), jnp.float32),
        scratch_shapes=[pltpu.VMEM((FIELDS, levels * SUB, east), jnp.float32)],
        compiler_params=call_params(61 << 20),
    )(adv, mixed, after)


def solve_consts(tables):
    return (tables.base, tables.y_back, tables.x_back, tables.z_back, tables.give)


def pressure_kernel(
    tables, dep_ref, w_ref, new_ref, coef_ref, jump_ref, base_ref, y_ref, x_ref, z_ref, give_ref,
    pressure_ref, out_ref, g_in_ref, g_bias_ref, g_out_ref, spec, jumps, flat,
):
    north, east, levels = tables.north, tables.east, tables.levels
    mine = tables.share * PARTS
    split_kernel(mine, tables.count, jump_ref, g_in_ref, g_bias_ref, g_out_ref, flat)
    each = jump_ref.shape[0] // tables.count
    for part in range(mine):
        jumps[pl.ds(part, tables.count, stride=mine), :] = jump_ref[
            pl.ds(part, tables.count, stride=each), :
        ]
    level = lax.broadcasted_iota(jnp.int32, (levels, east), 0)

    def use(y, tile):
        pressure_ref[pl.ds(y, levels, stride=north), :] = tile
        value = w_ref[0, y] - TIME_STEP * vertical_change(tile)
        value = jnp.where(level < dep_ref[y : y + 1, :], value, 0.0)
        out_ref[0, pl.ds(y, levels, stride=north), :] = value

    finish_solve(
        tables, spec, coef_ref, jumps, base_ref, y_ref, x_ref, z_ref, give_ref, use
    )


def pressure_finish(tables, dep, w, new, coef, jumps, inputs, hidden, outputs):
    levels, north, east = tables.levels, tables.north, tables.east
    consts = solve_consts(tables)
    flat = jax.ShapeDtypeStruct((levels * north, east), jnp.float32)
    rows = jumps.shape[0] - tables.share * tables.count * PARTS
    sums = [
        jax.ShapeDtypeStruct(shape, jnp.float32)
        for shape in ((inputs, hidden), (1, hidden), (outputs, hidden))
    ]
    pressure, new, g_in, g_bias, g_out = pl.pallas_call(
        functools.partial(pressure_kernel, tables),
        grid=(1,),
        in_specs=[
            whole_spec(dep),
            whole_spec(w),
            pl.BlockSpec(memory_space=pl.ANY),
            whole_spec(coef),
            whole_spec(jumps),
            *(whole_spec(a) for a in consts),
        ],
        out_specs=[
            whole_spec(flat),
            pl.BlockSpec((1, levels * north, east), lambda k: (2, 0, 0)),
            *(whole_spec(a) for a in sums),
        ],
        out_shape=[
            flat, jax.ShapeDtypeStruct((FIELDS, levels * north, east), jnp.float32), *sums
        ],
        input_output_aliases={2: 1},
        scratch_shapes=[
            pltpu.VMEM(coef.shape, jnp.float32),
            pltpu.VMEM((tables.share * tables.count * PARTS, east), jnp.float32),
            pltpu.VMEM((rows, east), jnp.float32),
        ],
        compiler_params=call_params(44 << 20),
    )(dep, w, new.reshape(FIELDS, levels * north, east), coef, jumps, *consts)
    pressure = pressure.reshape(levels, north, east)
    new = new.reshape(FIELDS, levels, north, east)
    return new, pressure, g_in, g_bias.reshape(hidden), g_out.T


def split_kernel(skip, count, sums_ref, in_ref, bias_ref, out_ref, flat):
    inputs, width = in_ref.shape
    east = sums_ref.shape[1]
    each = sums_ref.shape[0] // count
    more = each - skip
    for d in range(count):
        flat[d * more : (d + 1) * more, :] = sums_ref[d * each + skip : (d + 1) * each, :]
    wide = inputs * width // east
    for k in range(width // east):
        lanes = slice(k * east, (k + 1) * east)
        in_ref[:, lanes] = flat[k * inputs : (k + 1) * inputs, :]
        at = wide + k * east
        out_ref[:, lanes] = flat[at : at + out_ref.shape[0], :]
        bias_ref[:, lanes] = flat[at + east // 2 : at + east // 2 + 1, :]


def per_device(fields, cotangent, ocean_mask, depth_levels, in_weight, in_bias, out_weight):
    _, levels, north, east = fields.shape
    tables = Tables(levels, north, east, lax.axis_size("rows"), lax.axis_size("cols"))
    inputs, hidden = in_weight.shape
    outputs = out_weight.shape[1]
    in_bias = in_bias.reshape(1, hidden)
    out_weight = out_weight.T
    steps = levels // SUB
    dep, *edges = advance_edges(fields, ocean_mask, depth_levels)
    back_coef = adjoint_local(tables, cotangent, dep)
    back_edges = adjoint_edges(tables, back_coef, edges[0], edges[1])
    half = advect(fields, dep, TRACERS, edges, (0, steps // 2), back_edges)
    back_jumps = interface(tables, exchange(back_edges), 56 << 20, half[1])
    adv, spread = advect(fields, dep, TRACERS, edges, (steps // 2, steps), back_jumps, half)
    mixed, coef, send = column(
        tables, dep, adv, spread, fields, cotangent, in_weight, in_bias, out_weight,
        back_coef, exchange(back_jumps),
    )
    received = exchange(send)
    w = advect(fields, dep, (2,), edges, (0, steps), coef)[0]
    new = gather_fields(adv, mixed, coef)
    jumps = exchange(interface(tables, received, VMEM_LIMIT, w, new))
    return pressure_finish(tables, dep, w, new, coef, jumps, inputs, hidden, outputs)


def solution(mesh):
    in_specs = (
        P(None, None, "cols", "rows"),
        P(None, None, "cols", "rows"),
        P("cols", "rows"),
        P("cols", "rows"),
        P(),
        P(),
        P(),
    )
    out_specs = (P(None, None, "cols", "rows"), P(None, "cols", "rows"), P(), P(), P())
    return jax.shard_map(
        per_device, mesh=mesh, in_specs=in_specs, out_specs=out_specs, check_vma=False
    )
```
